32 devices in a mesh: ty: 4 (over y, core), tx: 8 (over z, x).
Axes of the slice: x: 2, y: 2, z: 4, core: 2. Of those that a mesh axis runs over, the one named last changes fastest.
Arguments:
- incident: float32 [2, 1280, 3072], P(None, 'ty', 'tx'), may hold values from -6 to 6
- phases: float32 [2, 1280, 3072], P(None, 'ty', 'tx'), may hold values from -3.140625 to 3.140625
- cotangent: float32 [2, 1280, 3072], P(None, 'ty', 'tx'), may hold values from -6 to 6
- propagator: float32 [2, 33], replicated, may hold values from -0.6 to 0.6
Outputs:
- phase_grad: float32 [2, 1280, 3072], P(None, 'ty', 'tx')
- probe_grad: float32 [2, 1280, 3072], P(None, 'ty', 'tx')
The draws below stay inside these ranges and needn't reach their ends.
All inputs are finite; a program needn't handle non-finite values.
Results may differ from the reference program's by a relative error of at most 0.00015.
Values sent between devices are 32-bit elements; how exact they have to be, the bound alone decides.
A program may use at most 64 MiB of HBM per device.

```python
import jax
import jax.numpy as jnp
from jax import lax

HY = 320
HX = 384
TAPS = 33
SLICES = 2
RIM = 16
NY = 1280
NX = 3072
N_TY = 4
N_TX = 8


def levels(own_key, extent, cuts, least, largest):
    level = 1.0
    for axis_at, blocks in cuts:
        heights = jax.random.uniform(jax.random.fold_in(jax.random.fold_in(own_key, 6), axis_at), (blocks,), jnp.float32, least / len(cuts), largest / len(cuts))
        level = level * jnp.repeat(jnp.exp(heights), extent[axis_at] // blocks).reshape((-1,) + (1,) * (len(extent) - 1 - axis_at))
    return level


def scatter_about(key, dims, width, bound, split=(), kind=jnp.bfloat16):
    result = jax.random.normal(key, dims, jnp.float32) * width
    if len(split) > 0:
        result = levels(key, dims, split, -0.22, 0.18) * result
    return jnp.clip(result, min=-bound, max=bound).astype(kind)


def setup_inputs(seed: int = 0) -> dict:
    key_of = jax.random.split(jax.random.key(seed), 5)
    return {
        "incident": scatter_about(key_of[0], (2, NY, NX), 1.0, 6.0, ((1, 4), (2, 8)), jnp.float32),
        "phases": jnp.clip(jax.random.uniform(key_of[1], (SLICES, NY, NX), jnp.float32, -3.140625, 3.140625), -3.140625, 3.140625),
        "cotangent": scatter_about(key_of[2], (2, NY, NX), 1.0, 6.0, ((1, 4), (2, 8)), jnp.float32),
        "propagator": scatter_about(key_of[3], (2, TAPS), 0.12, 0.6, (), jnp.float32),
    }


def spectrum(propagator, length):
    taps = lax.complex(propagator[0], propagator[1])
    places = (RIM - jnp.arange(TAPS, dtype=jnp.int32)) % length
    kernel = jnp.zeros((length,), taps.dtype).at[places].add(taps)
    return jnp.fft.fft(kernel)


def pass_rows(field, spec_rows):
    blocks = field.reshape(NY, N_TX, HX).transpose(1, 0, 2)

    def one_block(block):
        return jnp.fft.ifft(jnp.fft.fft(block, axis=0) * spec_rows[:, None], axis=0)

    return lax.map(one_block, blocks).transpose(1, 0, 2).reshape(NY, NX)


def pass_columns(field, spec_columns):
    blocks = field.reshape(N_TY, HY, NX)

    def one_block(block):
        return jnp.fft.ifft(jnp.fft.fft(block, axis=1) * spec_columns[None, :], axis=1)

    return lax.map(one_block, blocks).reshape(NY, NX)


def propagate(field, spec_rows, spec_columns):
    return pass_columns(pass_rows(field, spec_rows), spec_columns)


def phase_term(gradient, wavefield):
    return jnp.imag(gradient) * jnp.real(wavefield) - jnp.real(gradient) * jnp.imag(wavefield)


def reference(incident, phases, cotangent, propagator):
    spec_rows = spectrum(propagator, NY)
    spec_columns = spectrum(propagator, NX)
    adj_rows = jnp.conj(spec_rows)
    adj_columns = jnp.conj(spec_columns)
    trans_zero = lax.complex(jnp.cos(phases[0]), jnp.sin(phases[0]))
    trans_one = lax.complex(jnp.cos(phases[1]), jnp.sin(phases[1]))
    wave_zero = lax.complex(incident[0], incident[1]) * trans_zero
    wave_one = propagate(wave_zero, spec_rows, spec_columns) * trans_one
    grad_one = propagate(lax.complex(cotangent[0], cotangent[1]), adj_rows, adj_columns)
    grad_zero = propagate(grad_one * jnp.conj(trans_one), adj_rows, adj_columns)
    phase_grad = jnp.stack([phase_term(grad_zero, wave_zero), phase_term(grad_one, wave_one)])
    probe = grad_zero * jnp.conj(trans_zero)
    probe_grad = jnp.stack([jnp.real(probe), jnp.imag(probe)])
    return phase_grad, probe_grad
```

```python
import jax
import jax.numpy as jnp
from jax import lax
from jax.experimental import pallas as pl
from jax.experimental.pallas import tpu as pltpu
from jax.sharding import PartitionSpec as P

RIM = 16
WIDE = 2 * RIM
LANES = 128
OUT = LANES - WIDE
F32 = jnp.float32
BF16 = jnp.bfloat16


def sincos(angle):
    half = angle * 0.5
    sq = half * half
    s = -1.0 / 39916800.0
    for c in (1.0 / 362880.0, -1.0 / 5040.0, 1.0 / 120.0, -1.0 / 6.0):
        s = s * sq + c
    s = half + half * sq * s
    c = 1.0 / 479001600.0
    for k in (-1.0 / 3628800.0, 1.0 / 40320.0, -1.0 / 720.0, 1.0 / 24.0, -0.5, 1.0):
        c = c * sq + k
    return 2.0 * s * c, 1.0 - 2.0 * s * s


def split(x):
    hi = x.astype(BF16)
    return hi, (x - hi.astype(F32)).astype(BF16)


def lanes_of(rows, width=LANES):
    return lax.broadcasted_iota(jnp.int32, (rows, width), 1)


def toeplitz(line, rows, width, shift):
    wide = jnp.broadcast_to(line[:, :width], (rows, width))
    return pltpu.roll(wide, shift % width, 1, stride=1, stride_axis=0)


PIECES = (("c0", WIDE, 0), ("c1", WIDE, 32), ("p1", RIM, 64), ("i0", RIM, 80), ("i1", RIM, 96), ("p0", RIM, 112))


def make_kernel(H, W):
    tiles = W // LANES
    full = W + LANES
    step = 32

    def kernel(
        inc, ph, cot, prop, pg, pb,
        incv, phv, cotv, packl, packr, hl, hr, crow, irow, prow,
        line, xh, xl, zh, zl, gh, gl, uh, ul, vh, vl,
        c1, s1, c0, s0, wz, gout, fout, rowf, rowa, colf, cola, pgv, pbv,
        load, store, send, recv,
    ):
        ty, tx = lax.axis_index("ty"), lax.axis_index("tx")
        ny, nx = lax.axis_size("ty"), lax.axis_size("tx")
        up, down = lax.rem(ty + ny - 1, ny), lax.rem(ty + 1, ny)
        left, right = lax.rem(tx + nx - 1, nx), lax.rem(tx + 1, nx)

        loads = [
            pltpu.make_async_copy(src, dst, load.at[k])
            for k, (src, dst) in enumerate(((cot, cotv), (ph, phv), (inc, incv)))
        ]
        for c in loads:
            c.start()
        barrier = pltpu.get_barrier_semaphore()
        others = [(up, tx), (down, tx), (ty, left), (ty, right), (up, left), (up, right), (down, left), (down, right)]
        for dev in others:
            pl.semaphore_signal(barrier, inc=1, device_id=dev, device_id_type=pl.DeviceIdType.MESH)
        for c in loads:
            c.wait()

        def plane(name):
            return {"c0": (cotv, 0), "c1": (cotv, 1), "p0": (phv, 0), "p1": (phv, 1), "i0": (incv, 0), "i1": (incv, 1)}[name]

        @pl.loop(0, H // step)
        def _(i):
            r = pl.ds(pl.multiple_of(i * step, step), step)
            lane = lanes_of(step)
            a = jnp.zeros((step, LANES), F32)
            b = jnp.zeros((step, LANES), F32)
            for name, w, dst in PIECES:
                ref, p = plane(name)
                first = ref[p, r, 0:LANES]
                last = ref[p, r, W - LANES : W]
                here = (lane >= dst) & (lane < dst + w)
                a = jnp.where(here, pltpu.roll(first, dst, 1) if dst else first, a)
                b = jnp.where(here, pltpu.roll(last, (dst + w) % LANES, 1), b)
            packl[r, :] = a
            packr[r, :] = b

        pl.semaphore_wait(barrier, 8)
        copies = []

        def push(src, dst, dev):
            k = len(copies)
            c = pltpu.make_async_remote_copy(
                src_ref=src, dst_ref=dst, send_sem=send.at[k], recv_sem=recv.at[k],
                device_id=dev, device_id_type=pl.DeviceIdType.MESH,
            )
            c.start()
            copies.append(c)

        push(packl, hr.at[WIDE : WIDE + H], (ty, left))
        push(packr, hl.at[WIDE : WIDE + H], (ty, right))
        push(cot.at[:, 0:WIDE, :], crow.at[1], (up, tx))
        push(cot.at[:, H - WIDE : H, :], crow.at[0], (down, tx))
        push(inc.at[:, 0:RIM, :], irow.at[1], (up, tx))
        push(inc.at[:, H - RIM : H, :], irow.at[0], (down, tx))
        push(ph.at[:, 0:RIM, :], prow.at[1], (up, tx))
        push(ph.at[:, H - RIM : H, :], prow.at[0], (down, tx))
        push(packl.at[0:WIDE], hr.at[WIDE + H : WIDE + H + WIDE], (up, left))
        push(packl.at[H - WIDE : H], hr.at[0:WIDE], (down, left))
        push(packr.at[0:WIDE], hl.at[WIDE + H : WIDE + H + WIDE], (up, right))
        push(packr.at[H - WIDE : H], hl.at[0:WIDE], (down, right))

        line[...] = jnp.zeros(line.shape, F32)
        line[0:2, 0 : prop.shape[1]] = prop[...]
        kr, ki = line[0:1, :], line[1:2, :]

        def rows_band(dst, mr, mi):
            top = jnp.concatenate([mr, -mi], axis=1)
            low = jnp.concatenate([mi, mr], axis=1)
            hi, lo = split(jnp.concatenate([top, low], axis=0))
            k = 2 * LANES
            dst[:, 0:k] = hi
            dst[:, k : 2 * k] = hi
            dst[:, 2 * k : 3 * k] = lo

        def cols_band(dst, tr, ti):
            top = jnp.concatenate([tr, ti], axis=1)
            low = jnp.concatenate([-ti, tr], axis=1)
            hi, lo = split(jnp.concatenate([top, low], axis=0))
            k = 4 * LANES
            dst[0:k, :] = hi
            dst[k : 2 * k, :] = hi
            dst[2 * k : 3 * k, :] = lo

        rows_band(rowf, toeplitz(kr, LANES, LANES, 0)[:OUT], toeplitz(ki, LANES, LANES, 0)[:OUT])
        rows_band(rowa, toeplitz(kr, LANES, LANES, -WIDE).T[:OUT], -toeplitz(ki, LANES, LANES, -WIDE).T[:OUT])
        cols_band(colf, toeplitz(kr, LANES, 2 * LANES, 0).T, toeplitz(ki, LANES, 2 * LANES, 0).T)
        cols_band(
            cola,
            toeplitz(kr, 2 * LANES, 2 * LANES, -WIDE)[:, :LANES],
            -toeplitz(ki, 2 * LANES, 2 * LANES, -WIDE)[:, :LANES],
        )

        @pl.loop(0, H // 16)
        def _(i):
            r0 = pl.multiple_of(i * 16, 16)
            r = pl.ds(r0, 16)
            for p in range(2):
                hi, lo = split(cotv[p, r, :])
                q = pl.ds(pl.multiple_of(r0 + WIDE, 16), 16)
                xh[p, q, 0:W] = hi
                xl[p, q, 0:W] = lo
            q = pl.ds(pl.multiple_of(r0 + RIM, 16), 16)
            s, c = sincos(phv[1, r, :])
            s1[q, 0:W] = s
            c1[q, 0:W] = c
            s, c = sincos(phv[0, r, :])
            s0[r, :] = s
            c0[r, :] = c
            a, b = incv[0, r, :], incv[1, r, :]
            for p, w in enumerate((a * c - b * s, a * s + b * c)):
                wz[p, r, :] = w
                hi, lo = split(w)
                zh[p, q, 0:W] = hi
                zl[p, q, 0:W] = lo

        for k in (2, 3, 4, 5, 6, 7):
            copies[k].wait_recv()
        for side in range(2):
            q = slice(0, WIDE) if side == 0 else slice(WIDE + H, WIDE + H + WIDE)
            for p in range(2):
                hi, lo = split(crow[side, p])
                xh[p, q, 0:W] = hi
                xl[p, q, 0:W] = lo
            q = slice(0, RIM) if side == 0 else slice(RIM + H, RIM + H + RIM)
            s, c = sincos(prow[side, 1])
            s1[q, 0:W] = s
            c1[q, 0:W] = c
            s, c = sincos(prow[side, 0])
            a, b = irow[side, 0], irow[side, 1]
            for p, w in enumerate((a * c - b * s, a * s + b * c)):
                hi, lo = split(w)
                zh[p, q, 0:W] = hi
                zl[p, q, 0:W] = lo

        def down_pass(src_h, src_l, dst_h, dst_l, band, rows, lo_lane, hi_lane):
            starts = list(range(0, rows - OUT, OUT)) + [rows - OUT]
            cols = slice(lo_lane, hi_lane)
            for q0 in starts:
                win = slice(q0, q0 + LANES)
                hi = [src_h[0, win, cols], src_h[1, win, cols]]
                lo = [src_l[0, win, cols], src_l[1, win, cols]]
                operand = jnp.concatenate(hi + lo + hi, axis=0)
                u = jnp.dot(band[...], operand, preferred_element_type=F32)
                h, l = split(u)
                for p in range(2):
                    dst_h[p, q0 : q0 + OUT, cols] = h[p * OUT : (p + 1) * OUT]
                    dst_l[p, q0 : q0 + OUT, cols] = l[p * OUT : (p + 1) * OUT]

        def across_pass(src_h, src_l, dst, band, rows, which):
            for t in which:
                n = (t + 1) % (tiles + 1)
                a, b = slice(t * LANES, (t + 1) * LANES), slice(n * LANES, (n + 1) * LANES)
                hi = [src_h[0, 0:rows, a], src_h[0, 0:rows, b], src_h[1, 0:rows, a], src_h[1, 0:rows, b]]
                lo = [src_l[0, 0:rows, a], src_l[0, 0:rows, b], src_l[1, 0:rows, a], src_l[1, 0:rows, b]]
                operand = jnp.concatenate(hi + lo + hi, axis=1)
                dst[t, 0:rows, :] = jnp.dot(operand, band[...], preferred_element_type=F32)

        def shifted(src, p, t, r, rows):
            cols = slice(p * LANES, (p + 1) * LANES)
            before = pltpu.roll(src[(t + tiles) % (tiles + 1), r, cols], RIM, 1)
            own = pltpu.roll(src[t, r, cols], RIM, 1)
            return jnp.where(lanes_of(rows) < RIM, before, own)

        down_pass(xh, xl, uh, ul, rowa, H + WIDE, 0, W)
        down_pass(zh, zl, vh, vl, rowf, H, 0, W)
        across_pass(uh, ul, gout, cola, H + WIDE, range(tiles - 1))
        across_pass(vh, vl, fout, colf, H, range(tiles - 1))

        for k in (0, 1, 8, 9, 10, 11):
            copies[k].wait_recv()
        edge = slice(W, full)

        def piece(a, b, index, rows):
            _, w, dst = PIECES[index]
            lane = lanes_of(rows)
            a = pltpu.roll(a, (LANES - w - dst) % LANES, 1)
            b = pltpu.roll(b, (-dst) % LANES, 1) if dst else b
            return jnp.where(lane < w, b, jnp.where(lane >= LANES - w, a, 0.0))

        @pl.loop(0, (H + 2 * WIDE) // 16)
        def _(i):
            r = pl.ds(pl.multiple_of(i * 16, 16), 16)
            a, b = hl[r, :], hr[r, :]
            for p in range(2):
                hi, lo = split(piece(a, b, p, 16))
                xh[p, r, edge] = hi
                xl[p, r, edge] = lo

        @pl.loop(0, (H + WIDE) // 16)
        def _(i):
            r = pl.ds(pl.multiple_of(i * 16, 16), 16)
            q = pl.ds(pl.multiple_of(i * 16 + RIM, 16), 16)
            a, b = hl[q, :], hr[q, :]
            s, c = sincos(piece(a, b, 2, 16))
            s1[r, edge] = s
            c1[r, edge] = c
            s, c = sincos(piece(a, b, 5, 16))
            x, y = piece(a, b, 3, 16), piece(a, b, 4, 16)
            for p, w in enumerate((x * c - y * s, x * s + y * c)):
                hi, lo = split(w)
                zh[p, r, edge] = hi
                zl[p, r, edge] = lo

        down_pass(xh, xl, uh, ul, rowa, H + WIDE, W, full)
        across_pass(uh, ul, gout, cola, H + WIDE, range(tiles - 1, tiles + 1))

        @pl.loop(0, (H + WIDE) // 16)
        def _(i):
            r = pl.ds(pl.multiple_of(i * 16, 16), 16)
            for t in range(tiles + 1):
                cols = slice(t * LANES, (t + 1) * LANES)
                gr, gi = shifted(gout, 0, t, r, 16), shifted(gout, 1, t, r, 16)
                c, s = c1[r, cols], s1[r, cols]
                for p, g in enumerate((gr * c + gi * s, gi * c - gr * s)):
                    hi, lo = split(g)
                    gh[p, r, cols] = hi
                    gl[p, r, cols] = lo

        down_pass(zh, zl, vh, vl, rowf, H, W, full)
        across_pass(vh, vl, fout, colf, H, range(tiles - 1, tiles + 1))

        @pl.loop(0, H // 16)
        def _(i):
            r = pl.ds(pl.multiple_of(i * 16, 16), 16)
            q = pl.ds(pl.multiple_of(i * 16 + RIM, 16), 16)
            for t in range(tiles):
                cols = slice(t * LANES, (t + 1) * LANES)
                gr, gi = shifted(gout, 0, t, q, 16), shifted(gout, 1, t, q, 16)
                fr, fi = shifted(fout, 0, t, r, 16), shifted(fout, 1, t, r, 16)
                c, s = c1[q, cols], s1[q, cols]
                pgv[1, r, cols] = gi * (fr * c - fi * s) - gr * (fr * s + fi * c)

        stores = [pltpu.make_async_copy(pgv.at[1], pg.at[1], store.at[0])]
        stores[0].start()

        down_pass(gh, gl, vh, vl, rowa, H, 0, full)
        across_pass(vh, vl, fout, cola, H, range(tiles + 1))

        @pl.loop(0, H // 16)
        def _(i):
            r = pl.ds(pl.multiple_of(i * 16, 16), 16)
            for t in range(tiles):
                cols = slice(t * LANES, (t + 1) * LANES)
                gr, gi = shifted(fout, 0, t, r, 16), shifted(fout, 1, t, r, 16)
                c, s = c0[r, cols], s0[r, cols]
                pgv[0, r, cols] = gi * wz[0, r, cols] - gr * wz[1, r, cols]
                pbv[0, r, cols] = gr * c + gi * s
                pbv[1, r, cols] = gi * c - gr * s

        stores.append(pltpu.make_async_copy(pgv.at[0], pg.at[0], store.at[1]))
        stores.append(pltpu.make_async_copy(pbv, pb, store.at[2]))
        stores[1].start()
        stores[2].start()
        for c in copies:
            c.wait_send()
        for c in stores:
            c.wait()

    V = pltpu.VMEM
    scratch = [
        V((2, H, W), F32), V((2, H, W), F32), V((2, H, W), F32),
        V((H, LANES), F32), V((H, LANES), F32),
        V((H + 2 * WIDE, LANES), F32), V((H + 2 * WIDE, LANES), F32),
        V((2, 2, WIDE, W), F32), V((2, 2, RIM, W), F32), V((2, 2, RIM, W), F32),
        V((8, 2 * LANES), F32),
        V((2, H + 2 * WIDE, full), BF16), V((2, H + 2 * WIDE, full), BF16),
        V((2, H + WIDE, full), BF16), V((2, H + WIDE, full), BF16),
        V((2, H + WIDE, full), BF16), V((2, H + WIDE, full), BF16),
        V((2, H + WIDE, full), BF16), V((2, H + WIDE, full), BF16),
        V((2, H, full), BF16), V((2, H, full), BF16),
        V((H + WIDE, full), F32), V((H + WIDE, full), F32),
        V((H, W), F32), V((H, W), F32), V((2, H, W), F32),
        V((tiles + 1, H + WIDE, 2 * LANES), F32), V((tiles + 1, H, 2 * LANES), F32),
        V((2 * OUT, 6 * LANES), BF16), V((2 * OUT, 6 * LANES), BF16),
        V((12 * LANES, 2 * LANES), BF16), V((12 * LANES, 2 * LANES), BF16),
        V((2, H, W), F32), V((2, H, W), F32),
        pltpu.SemaphoreType.DMA((3,)), pltpu.SemaphoreType.DMA((3,)),
        pltpu.SemaphoreType.DMA((12,)), pltpu.SemaphoreType.DMA((12,)),
    ]
    anywhere = pl.BlockSpec(memory_space=pl.ANY)
    return pl.pallas_call(
        kernel,
        out_shape=(jax.ShapeDtypeStruct((2, H, W), F32), jax.ShapeDtypeStruct((2, H, W), F32)),
        in_specs=[anywhere, anywhere, anywhere, pl.BlockSpec(memory_space=pltpu.VMEM)],
        out_specs=(anywhere, anywhere),
        scratch_shapes=scratch,
        compiler_params=pltpu.CompilerParams(
            collective_id=0, has_side_effects=True, vmem_limit_bytes=40 * 1024 * 1024
        ),
        cost_estimate=pl.CostEstimate(flops=10**10, bytes_accessed=5 * 10**6, transcendentals=0),
    )


def on_device(incident, phases, cotangent, propagator):
    H, W = incident.shape[1], incident.shape[2]
    return make_kernel(H, W)(incident, phases, cotangent, propagator)


def solution(mesh):
    placed = (P(None, "ty", "tx"), P(None, "ty", "tx"), P(None, "ty", "tx"), P())
    return jax.shard_map(
        on_device,
        mesh=mesh,
        in_specs=placed,
        out_specs=(P(None, "ty", "tx"), P(None, "ty", "tx")),
        check_vma=False,
    )
```

```python
import jax
import jax.numpy as jnp
from jax import lax
from jax.experimental import pallas as pl
from jax.experimental.pallas import tpu as pltpu
from jax.sharding import PartitionSpec as P

RIM = 16
WIDE = 2 * RIM
LANES = 128
OUT = LANES - WIDE
F32 = jnp.float32
BF16 = jnp.bfloat16


def block(rows, most):
    return max(n for n in range(16, most + 1, 16) if rows % n == 0)


def sincos(angle):
    half = angle * 0.5
    sq = half * half
    s = -1.0 / 39916800.0
    for c in (1.0 / 362880.0, -1.0 / 5040.0, 1.0 / 120.0, -1.0 / 6.0):
        s = s * sq + c
    s = half + half * sq * s
    c = 1.0 / 479001600.0
    for k in (-1.0 / 3628800.0, 1.0 / 40320.0, -1.0 / 720.0, 1.0 / 24.0, -0.5, 1.0):
        c = c * sq + k
    return 2.0 * s * c, 1.0 - 2.0 * s * s


def split(x):
    hi = x.astype(BF16)
    return hi, (x - hi.astype(F32)).astype(BF16)


def lanes_of(rows, width=LANES):
    return lax.broadcasted_iota(jnp.int32, (rows, width), 1)


def toeplitz(line, rows, width, shift):
    wide = jnp.broadcast_to(line[:, :width], (rows, width))
    return pltpu.roll(wide, shift % width, 1, stride=1, stride_axis=0)


PIECES = (("c0", WIDE, 0), ("c1", WIDE, 32), ("p1", RIM, 64), ("i0", RIM, 80), ("i1", RIM, 96), ("p0", RIM, 112))


def make_kernel(H, W, tap_shape):
    tiles = W // LANES
    full = W + LANES
    step = block(H, 80)

    def kernel(
        inc, ph, cot, prop, pg, pb,
        incv, phv, cotv, packl, packr, hl, hr, crow, irow, prow,
        taps, line, xh, xl, zh, zl, gh, gl, uh, ul, vh, vl,
        c1, s1, c0, s0, wz, gout, fout, rowf, rowa, colf, cola, colb, pgv, pbv,
        load, store, send, recv,
    ):
        ty, tx = lax.axis_index("ty"), lax.axis_index("tx")
        ny, nx = lax.axis_size("ty"), lax.axis_size("tx")
        up, down = lax.rem(ty + ny - 1, ny), lax.rem(ty + 1, ny)
        left, right = lax.rem(tx + nx - 1, nx), lax.rem(tx + 1, nx)

        loads = [
            pltpu.make_async_copy(src, dst, load.at[k])
            for k, (src, dst) in enumerate(((cot, cotv), (ph, phv), (inc, incv), (prop, taps)))
        ]
        for c in loads:
            c.start()
        barrier = pltpu.get_barrier_semaphore()
        others = [(up, tx), (down, tx), (ty, left), (ty, right), (up, left), (up, right), (down, left), (down, right)]
        for dev in others:
            pl.semaphore_signal(barrier, inc=1, device_id=dev, device_id_type=pl.DeviceIdType.MESH)
        for c in loads:
            c.wait()

        def plane(name):
            return {"c0": (cotv, 0), "c1": (cotv, 1), "p0": (phv, 0), "p1": (phv, 1), "i0": (incv, 0), "i1": (incv, 1)}[name]

        @pl.loop(0, H // step)
        def _(i):
            r = pl.ds(pl.multiple_of(i * step, step), step)
            lane = lanes_of(step)
            a = jnp.zeros((step, LANES), F32)
            b = jnp.zeros((step, LANES), F32)
            for name, w, dst in PIECES:
                ref, p = plane(name)
                first = ref[p, r, 0:LANES]
                last = ref[p, r, W - LANES : W]
                here = (lane >= dst) & (lane < dst + w)
                a = jnp.where(here, pltpu.roll(first, dst, 1) if dst else first, a)
                b = jnp.where(here, pltpu.roll(last, (dst + w) % LANES, 1), b)
            packl[r, :] = a
            packr[r, :] = b

        pl.semaphore_wait(barrier, 8)
        copies = []

        def push(src, dst, dev):
            k = len(copies)
            c = pltpu.make_async_remote_copy(
                src_ref=src, dst_ref=dst, send_sem=send.at[k], recv_sem=recv.at[k],
                device_id=dev, device_id_type=pl.DeviceIdType.MESH,
            )
            c.start()
            copies.append(c)

        push(packl, hr.at[WIDE : WIDE + H], (ty, left))
        push(packr, hl.at[WIDE : WIDE + H], (ty, right))
        push(cot.at[:, 0:WIDE, :], crow.at[1], (up, tx))
        push(cot.at[:, H - WIDE : H, :], crow.at[0], (down, tx))
        push(inc.at[:, 0:RIM, :], irow.at[1], (up, tx))
        push(inc.at[:, H - RIM : H, :], irow.at[0], (down, tx))
        push(ph.at[:, 0:RIM, :], prow.at[1], (up, tx))
        push(ph.at[:, H - RIM : H, :], prow.at[0], (down, tx))
        push(packl.at[0:WIDE], hr.at[WIDE + H : WIDE + H + WIDE], (up, left))
        push(packl.at[H - WIDE : H], hr.at[0:WIDE], (down, left))
        push(packr.at[0:WIDE], hl.at[WIDE + H : WIDE + H + WIDE], (up, right))
        push(packr.at[H - WIDE : H], hl.at[0:WIDE], (down, right))

        line[...] = jnp.zeros(line.shape, F32)
        line[0:2, 0 : prop.shape[1]] = taps[...]
        kr, ki = line[0:1, :], line[1:2, :]

        def rows_band(dst, mr, mi):
            top = jnp.concatenate([mr, -mi], axis=1)
            low = jnp.concatenate([mi, mr], axis=1)
            hi, lo = split(jnp.concatenate([top, low], axis=0))
            k = 2 * LANES
            dst[:, 0:k] = hi
            dst[:, k : 2 * k] = hi
            dst[:, 2 * k : 3 * k] = lo

        def cols_band(dst, tr, ti):
            top = jnp.concatenate([tr, ti], axis=1)
            low = jnp.concatenate([-ti, tr], axis=1)
            hi, lo = split(jnp.concatenate([top, low], axis=0))
            k = 4 * LANES
            dst[0:k, :] = hi
            dst[k : 2 * k, :] = hi
            dst[2 * k : 3 * k, :] = lo

        rows_band(rowf, toeplitz(kr, LANES, LANES, 0)[:OUT], toeplitz(ki, LANES, LANES, 0)[:OUT])
        rows_band(rowa, toeplitz(kr, LANES, LANES, -WIDE).T[:OUT], -toeplitz(ki, LANES, LANES, -WIDE).T[:OUT])
        cols_band(colf, toeplitz(kr, LANES, 2 * LANES, 0).T, toeplitz(ki, LANES, 2 * LANES, 0).T)
        cols_band(
            cola,
            toeplitz(kr, 2 * LANES, 2 * LANES, -WIDE)[:, :LANES],
            -toeplitz(ki, 2 * LANES, 2 * LANES, -WIDE)[:, :LANES],
        )

        cols_band(
            colb,
            toeplitz(kr, 2 * LANES, 2 * LANES, -LANES)[:, :LANES],
            -toeplitz(ki, 2 * LANES, 2 * LANES, -LANES)[:, :LANES],
        )

        def moved(ref, t, r):
            return pltpu.roll(ref[1, r, t * LANES : (t + 1) * LANES], LANES - RIM, 1)

        def phase_one(ref, r, q, rows, which):
            last = lanes_of(rows) >= LANES - RIM
            for t in which:
                s, c = sincos(jnp.where(last, moved(ref, t + 1, r), moved(ref, t, r)))
                s1[q, t * LANES : (t + 1) * LANES] = s
                c1[q, t * LANES : (t + 1) * LANES] = c

        @pl.loop(0, H // 16)
        def _(i):
            r0 = pl.multiple_of(i * 16, 16)
            r = pl.ds(r0, 16)
            for p in range(2):
                hi, lo = split(cotv[p, r, :])
                q = pl.ds(pl.multiple_of(r0 + WIDE, 16), 16)
                xh[p, q, 0:W] = hi
                xl[p, q, 0:W] = lo
            q = pl.ds(pl.multiple_of(r0 + RIM, 16), 16)
            phase_one(phv, r, q, 16, range(tiles - 1))
            s, c = sincos(phv[0, r, :])
            s0[r, :] = s
            c0[r, :] = c
            a, b = incv[0, r, :], incv[1, r, :]
            for p, w in enumerate((a * c - b * s, a * s + b * c)):
                wz[p, r, :] = w
                hi, lo = split(w)
                zh[p, q, 0:W] = hi
                zl[p, q, 0:W] = lo

        for k in (2, 3, 4, 5, 6, 7):
            copies[k].wait_recv()
        for side in range(2):
            q = slice(0, WIDE) if side == 0 else slice(WIDE + H, WIDE + H + WIDE)
            for p in range(2):
                hi, lo = split(crow[side, p])
                xh[p, q, 0:W] = hi
                xl[p, q, 0:W] = lo
            q = slice(0, RIM) if side == 0 else slice(RIM + H, RIM + H + RIM)
            phase_one(prow.at[side], slice(0, RIM), q, RIM, range(tiles - 1))
            s, c = sincos(prow[side, 0])
            a, b = irow[side, 0], irow[side, 1]
            for p, w in enumerate((a * c - b * s, a * s + b * c)):
                hi, lo = split(w)
                zh[p, q, 0:W] = hi
                zl[p, q, 0:W] = lo

        def down_pass(src_h, src_l, dst_h, dst_l, band, rows, lo_lane, hi_lane):
            starts = list(range(0, rows - OUT, OUT)) + [rows - OUT]
            cols = slice(lo_lane, hi_lane)
            for q0 in starts:
                win = slice(q0, q0 + LANES)
                hi = [src_h[0, win, cols], src_h[1, win, cols]]
                lo = [src_l[0, win, cols], src_l[1, win, cols]]
                operand = jnp.concatenate(hi + lo + hi, axis=0)
                u = jnp.dot(band[...], operand, preferred_element_type=F32)
                h, l = split(u)
                for p in range(2):
                    dst_h[p, q0 : q0 + OUT, cols] = h[p * OUT : (p + 1) * OUT]
                    dst_l[p, q0 : q0 + OUT, cols] = l[p * OUT : (p + 1) * OUT]

        def across_pass(src_h, src_l, dst, band, rows, which, first=0):
            for t in which:
                m, n = (t + first) % (tiles + 1), (t + first + 1) % (tiles + 1)
                a, b = slice(m * LANES, (m + 1) * LANES), slice(n * LANES, (n + 1) * LANES)
                hi = [src_h[0, 0:rows, a], src_h[0, 0:rows, b], src_h[1, 0:rows, a], src_h[1, 0:rows, b]]
                lo = [src_l[0, 0:rows, a], src_l[0, 0:rows, b], src_l[1, 0:rows, a], src_l[1, 0:rows, b]]
                operand = jnp.concatenate(hi + lo + hi, axis=1)
                dst[t, 0:rows, :] = jnp.dot(operand, band[...], preferred_element_type=F32)

        down_pass(xh, xl, uh, ul, rowa, H + WIDE, 0, W)
        down_pass(zh, zl, vh, vl, rowf, H, 0, W)
        across_pass(uh, ul, gout, cola, H + WIDE, range(tiles - 1))
        across_pass(vh, vl, fout, colf, H, range(tiles - 1))

        for k in (0, 1, 8, 9, 10, 11):
            copies[k].wait_recv()
        edge = slice(W, full)

        def piece(a, b, index, rows):
            _, w, dst = PIECES[index]
            lane = lanes_of(rows)
            a = pltpu.roll(a, (LANES - w - dst) % LANES, 1)
            b = pltpu.roll(b, (-dst) % LANES, 1) if dst else b
            return jnp.where(lane < w, b, jnp.where(lane >= LANES - w, a, 0.0))

        xstep = block(H + 2 * WIDE, 96)

        @pl.loop(0, (H + 2 * WIDE) // xstep)
        def _(i):
            r = pl.ds(pl.multiple_of(i * xstep, 16), xstep)
            a, b = hl[r, :], hr[r, :]
            for p in range(2):
                hi, lo = split(piece(a, b, p, xstep))
                xh[p, r, edge] = hi
                xl[p, r, edge] = lo

        estep = block(H + WIDE, 64)

        def phase_edge(r, q, own, own_r, rows):
            a, b = hl[q, :], hr[q, :]
            _, _, dst = PIECES[2]
            lane = lanes_of(rows)
            inner = moved(own, tiles - 1, own_r)
            x = jnp.where(lane >= LANES - RIM, pltpu.roll(b, LANES - RIM - dst, 1), inner)
            outer = jnp.where(lane >= LANES - WIDE, pltpu.roll(a, LANES - WIDE - dst, 1), 0.0)
            y = jnp.where(lane >= LANES - RIM, moved(own, 0, own_r), outer)
            for t, v in ((tiles - 1, x), (tiles, y)):
                s, c = sincos(v)
                s1[r, t * LANES : (t + 1) * LANES] = s
                c1[r, t * LANES : (t + 1) * LANES] = c

        hstep = block(H, 64)

        @pl.loop(0, H // hstep)
        def _(i):
            r = pl.ds(pl.multiple_of(i * hstep + RIM, 16), hstep)
            q = pl.ds(pl.multiple_of(i * hstep + WIDE, 16), hstep)
            phase_edge(r, q, phv, pl.ds(pl.multiple_of(i * hstep, 16), hstep), hstep)

        for side in range(2):
            e = side * (H + RIM)
            phase_edge(slice(e, e + RIM), slice(e + RIM, e + WIDE), prow.at[side], slice(0, RIM), RIM)

        @pl.loop(0, (H + WIDE) // estep)
        def _(i):
            r = pl.ds(pl.multiple_of(i * estep, 16), estep)
            q = pl.ds(pl.multiple_of(i * estep + RIM, 16), estep)
            a, b = hl[q, :], hr[q, :]
            s, c = sincos(piece(a, b, 5, estep))
            x, y = piece(a, b, 3, estep), piece(a, b, 4, estep)
            for p, w in enumerate((x * c - y * s, x * s + y * c)):
                hi, lo = split(w)
                zh[p, r, edge] = hi
                zl[p, r, edge] = lo

        down_pass(xh, xl, uh, ul, rowa, H + WIDE, W, full)
        across_pass(uh, ul, gout, cola, H + WIDE, range(tiles - 1, tiles + 1))

        @pl.loop(0, (H + WIDE) // estep)
        def _(i):
            r = pl.ds(pl.multiple_of(i * estep, 16), estep)
            for t in range(tiles + 1):
                cols = slice(t * LANES, (t + 1) * LANES)
                gr, gi = gout[t, r, 0:LANES], gout[t, r, LANES : 2 * LANES]
                c, s = c1[r, cols], s1[r, cols]
                for p, g in enumerate((gr * c + gi * s, gi * c - gr * s)):
                    hi, lo = split(g)
                    gh[p, r, cols] = hi
                    gl[p, r, cols] = lo

        down_pass(zh, zl, vh, vl, rowf, H, W, full)
        across_pass(vh, vl, fout, colf, H, range(tiles - 1, tiles + 1))

        fstep = block(H, 32)

        @pl.loop(0, H // fstep)
        def _(i):
            r = pl.ds(pl.multiple_of(i * fstep, 16), fstep)
            q = pl.ds(pl.multiple_of(i * fstep + RIM, 16), fstep)
            first = lanes_of(fstep) < RIM
            before = None
            for t in [tiles] + list(range(tiles)):
                cols = slice(t * LANES, (t + 1) * LANES)
                gr, gi = gout[t, q, 0:LANES], gout[t, q, LANES : 2 * LANES]
                fr, fi = fout[t, r, 0:LANES], fout[t, r, LANES : 2 * LANES]
                c, s = c1[q, cols], s1[q, cols]
                term = pltpu.roll(gi * (fr * c - fi * s) - gr * (fr * s + fi * c), RIM, 1)
                if before is not None:
                    pgv[1, r, cols] = jnp.where(first, before, term)
                before = term

        stores = [pltpu.make_async_copy(pgv.at[1], pg.at[1], store.at[0])]
        stores[0].start()

        down_pass(gh, gl, vh, vl, rowa, H, 0, full)
        across_pass(vh, vl, fout, colb, H, range(tiles), -1)

        @pl.loop(0, H // fstep)
        def _(i):
            r = pl.ds(pl.multiple_of(i * fstep, 16), fstep)
            for t in range(tiles):
                cols = slice(t * LANES, (t + 1) * LANES)
                gr, gi = fout[t, r, 0:LANES], fout[t, r, LANES : 2 * LANES]
                c, s = c0[r, cols], s0[r, cols]
                pgv[0, r, cols] = gi * wz[0, r, cols] - gr * wz[1, r, cols]
                pbv[0, r, cols] = gr * c + gi * s
                pbv[1, r, cols] = gi * c - gr * s

        stores.append(pltpu.make_async_copy(pgv.at[0], pg.at[0], store.at[1]))
        stores.append(pltpu.make_async_copy(pbv, pb, store.at[2]))
        stores[1].start()
        stores[2].start()
        for c in copies:
            c.wait_send()
        for c in stores:
            c.wait()

    V = pltpu.VMEM
    scratch = [
        V((2, H, W), F32), V((2, H, W), F32), V((2, H, W), F32),
        V((H, LANES), F32), V((H, LANES), F32),
        V((H + 2 * WIDE, LANES), F32), V((H + 2 * WIDE, LANES), F32),
        V((2, 2, WIDE, W), F32), V((2, 2, RIM, W), F32), V((2, 2, RIM, W), F32),
        V(tap_shape, F32), V((8, 2 * LANES), F32),
        V((2, H + 2 * WIDE, full), BF16), V((2, H + 2 * WIDE, full), BF16),
        V((2, H + WIDE, full), BF16), V((2, H + WIDE, full), BF16),
        V((2, H + WIDE, full), BF16), V((2, H + WIDE, full), BF16),
        V((2, H + WIDE, full), BF16), V((2, H + WIDE, full), BF16),
        V((2, H, full), BF16), V((2, H, full), BF16),
        V((H + WIDE, full), F32), V((H + WIDE, full), F32),
        V((H, W), F32), V((H, W), F32), V((2, H, W), F32),
        V((tiles + 1, H + WIDE, 2 * LANES), F32), V((tiles + 1, H, 2 * LANES), F32),
        V((2 * OUT, 6 * LANES), BF16), V((2 * OUT, 6 * LANES), BF16),
        V((12 * LANES, 2 * LANES), BF16), V((12 * LANES, 2 * LANES), BF16),
        V((12 * LANES, 2 * LANES), BF16),
        V((2, H, W), F32), V((2, H, W), F32),
        pltpu.SemaphoreType.DMA((4,)), pltpu.SemaphoreType.DMA((3,)),
        pltpu.SemaphoreType.DMA((12,)), pltpu.SemaphoreType.DMA((12,)),
    ]
    anywhere = pl.BlockSpec(memory_space=pl.ANY)
    return pl.pallas_call(
        kernel,
        out_shape=(jax.ShapeDtypeStruct((2, H, W), F32), jax.ShapeDtypeStruct((2, H, W), F32)),
        in_specs=[pl.BlockSpec(memory_space=pltpu.HBM)] * 4,
        out_specs=(anywhere, anywhere),
        scratch_shapes=scratch,
        compiler_params=pltpu.CompilerParams(
            collective_id=0, has_side_effects=True, vmem_limit_bytes=40 * 1024 * 1024
        ),
        cost_estimate=pl.CostEstimate(flops=10**10, bytes_accessed=5 * 10**6, transcendentals=0),
    )


def on_device(incident, phases, cotangent, propagator):
    H, W = incident.shape[1], incident.shape[2]
    return make_kernel(H, W, propagator.shape)(incident, phases, cotangent, propagator)


def solution(mesh):
    placed = (P(None, "ty", "tx"), P(None, "ty", "tx"), P(None, "ty", "tx"), P())
    return jax.shard_map(
        on_device,
        mesh=mesh,
        in_specs=placed,
        out_specs=(P(None, "ty", "tx"), P(None, "ty", "tx")),
        check_vma=False,
    )
```

```python
import jax
import jax.numpy as jnp
from jax import lax
from jax.experimental import pallas as pl
from jax.experimental.pallas import tpu as pltpu
from jax.sharding import PartitionSpec as P

RIM = 16
WIDE = 2 * RIM
LANES = 128
OUT = LANES - WIDE
F32 = jnp.float32
BF16 = jnp.bfloat16


def block(rows, most):
    return max(n for n in range(16, most + 1, 16) if rows % n == 0)


def sincos(angle):
    half = angle * 0.5
    sq = half * half
    s = -1.0 / 39916800.0
    for c in (1.0 / 362880.0, -1.0 / 5040.0, 1.0 / 120.0, -1.0 / 6.0):
        s = s * sq + c
    s = half + half * sq * s
    c = 1.0 / 479001600.0
    for k in (-1.0 / 3628800.0, 1.0 / 40320.0, -1.0 / 720.0, 1.0 / 24.0, -0.5, 1.0):
        c = c * sq + k
    return 2.0 * s * c, 1.0 - 2.0 * s * s


def split(x):
    hi = x.astype(BF16)
    return hi, (x - hi.astype(F32)).astype(BF16)


def lanes_of(rows, width=LANES):
    return lax.broadcasted_iota(jnp.int32, (rows, width), 1)


def toeplitz(line, rows, width, shift):
    wide = jnp.broadcast_to(line[:, :width], (rows, width))
    return pltpu.roll(wide, shift % width, 1, stride=1, stride_axis=0)


def down_pass(src_h, src_l, dst_h, dst_l, band, rows, lo_lane, hi_lane):
    starts = list(range(0, rows - OUT, OUT)) + [rows - OUT]
    cols = slice(lo_lane, hi_lane)
    for q0 in starts:
        win = slice(q0, q0 + LANES)
        hi = [src_h[0, win, cols], src_h[1, win, cols]]
        lo = [src_l[0, win, cols], src_l[1, win, cols]]
        operand = jnp.concatenate(hi + lo + hi, axis=0)
        u = jnp.dot(band[...], operand, preferred_element_type=F32)
        h, l = split(u)
        for p in range(2):
            dst_h[p, q0 : q0 + OUT, cols] = h[p * OUT : (p + 1) * OUT]
            dst_l[p, q0 : q0 + OUT, cols] = l[p * OUT : (p + 1) * OUT]


def across(src_h, src_l, band, rows, t, tiles):
    a, b = [slice(n * LANES, (n + 1) * LANES) for n in (t % (tiles + 1), (t + 1) % (tiles + 1))]
    hi = [src_h[0, rows, a], src_h[0, rows, b], src_h[1, rows, a], src_h[1, rows, b]]
    lo = [src_l[0, rows, a], src_l[0, rows, b], src_l[1, rows, a], src_l[1, rows, b]]
    return jnp.dot(jnp.concatenate(hi + lo + hi, axis=1), band[...], preferred_element_type=F32)


PIECES = (("c0", WIDE, 0), ("c1", WIDE, 32), ("p1", RIM, 64), ("i0", RIM, 80), ("i1", RIM, 96), ("p0", RIM, 112))


def make_kernel(H, W, tap_shape):
    tiles = W // LANES
    full = W + LANES
    step = block(H, 80)

    def kernel(
        inc, ph, cot, prop, gh, gl, pgv, wz, c0, s0, rowa, colb,
        incv, phv, cotv, packl, packr, hl, hr, crow, irow, prow,
        taps, line, xh, xl, zh, zl, uh, ul, vh, vl,
        c1, s1, gout, fout, rowf, colf, cola,
        load, send, recv,
    ):
        ty, tx = lax.axis_index("ty"), lax.axis_index("tx")
        ny, nx = lax.axis_size("ty"), lax.axis_size("tx")
        up, down = lax.rem(ty + ny - 1, ny), lax.rem(ty + 1, ny)
        left, right = lax.rem(tx + nx - 1, nx), lax.rem(tx + 1, nx)

        loads = [
            pltpu.make_async_copy(src, dst, load.at[k])
            for k, (src, dst) in enumerate(((cot, cotv), (ph, phv), (inc, incv), (prop, taps)))
        ]
        for c in loads:
            c.start()
        barrier = pltpu.get_barrier_semaphore()
        others = [(up, tx), (down, tx), (ty, left), (ty, right), (up, left), (up, right), (down, left), (down, right)]
        for dev in others:
            pl.semaphore_signal(barrier, inc=1, device_id=dev, device_id_type=pl.DeviceIdType.MESH)
        for c in loads:
            c.wait()

        def plane(name):
            return {"c0": (cotv, 0), "c1": (cotv, 1), "p0": (phv, 0), "p1": (phv, 1), "i0": (incv, 0), "i1": (incv, 1)}[name]

        @pl.loop(0, H // step)
        def _(i):
            r = pl.ds(pl.multiple_of(i * step, step), step)
            lane = lanes_of(step)
            a = jnp.zeros((step, LANES), F32)
            b = jnp.zeros((step, LANES), F32)
            for name, w, dst in PIECES:
                ref, p = plane(name)
                first = ref[p, r, 0:LANES]
                last = ref[p, r, W - LANES : W]
                here = (lane >= dst) & (lane < dst + w)
                a = jnp.where(here, pltpu.roll(first, dst, 1) if dst else first, a)
                b = jnp.where(here, pltpu.roll(last, (dst + w) % LANES, 1), b)
            packl[r, :] = a
            packr[r, :] = b

        pl.semaphore_wait(barrier, 8)
        copies = []

        def push(src, dst, dev):
            k = len(copies)
            c = pltpu.make_async_remote_copy(
                src_ref=src, dst_ref=dst, send_sem=send.at[k], recv_sem=recv.at[k],
                device_id=dev, device_id_type=pl.DeviceIdType.MESH,
            )
            c.start()
            copies.append(c)

        push(packl, hr.at[WIDE : WIDE + H], (ty, left))
        push(packr, hl.at[WIDE : WIDE + H], (ty, right))
        push(cot.at[:, 0:WIDE, :], crow.at[1], (up, tx))
        push(cot.at[:, H - WIDE : H, :], crow.at[0], (down, tx))
        push(inc.at[:, 0:RIM, :], irow.at[1], (up, tx))
        push(inc.at[:, H - RIM : H, :], irow.at[0], (down, tx))
        push(ph.at[:, 0:RIM, :], prow.at[1], (up, tx))
        push(ph.at[:, H - RIM : H, :], prow.at[0], (down, tx))
        push(packl.at[0:WIDE], hr.at[WIDE + H : WIDE + H + WIDE], (up, left))
        push(packl.at[H - WIDE : H], hr.at[0:WIDE], (down, left))
        push(packr.at[0:WIDE], hl.at[WIDE + H : WIDE + H + WIDE], (up, right))
        push(packr.at[H - WIDE : H], hl.at[0:WIDE], (down, right))

        line[...] = jnp.zeros(line.shape, F32)
        line[0:2, 0 : prop.shape[1]] = taps[...]
        kr, ki = line[0:1, :], line[1:2, :]

        def rows_band(dst, mr, mi):
            top = jnp.concatenate([mr, -mi], axis=1)
            low = jnp.concatenate([mi, mr], axis=1)
            hi, lo = split(jnp.concatenate([top, low], axis=0))
            k = 2 * LANES
            dst[:, 0:k] = hi
            dst[:, k : 2 * k] = hi
            dst[:, 2 * k : 3 * k] = lo

        def cols_band(dst, tr, ti):
            top = jnp.concatenate([tr, ti], axis=1)
            low = jnp.concatenate([-ti, tr], axis=1)
            hi, lo = split(jnp.concatenate([top, low], axis=0))
            k = 4 * LANES
            dst[0:k, :] = hi
            dst[k : 2 * k, :] = hi
            dst[2 * k : 3 * k, :] = lo

        rows_band(rowf, toeplitz(kr, LANES, LANES, 0)[:OUT], toeplitz(ki, LANES, LANES, 0)[:OUT])
        rows_band(rowa, toeplitz(kr, LANES, LANES, -WIDE).T[:OUT], -toeplitz(ki, LANES, LANES, -WIDE).T[:OUT])
        cols_band(colf, toeplitz(kr, LANES, 2 * LANES, 0).T, toeplitz(ki, LANES, 2 * LANES, 0).T)
        cols_band(
            cola,
            toeplitz(kr, 2 * LANES, 2 * LANES, -WIDE)[:, :LANES],
            -toeplitz(ki, 2 * LANES, 2 * LANES, -WIDE)[:, :LANES],
        )

        cols_band(
            colb,
            toeplitz(kr, 2 * LANES, 2 * LANES, -LANES)[:, :LANES],
            -toeplitz(ki, 2 * LANES, 2 * LANES, -LANES)[:, :LANES],
        )

        def moved(ref, t, r):
            return pltpu.roll(ref[1, r, t * LANES : (t + 1) * LANES], LANES - RIM, 1)

        def phase_one(ref, r, q, rows, which):
            last = lanes_of(rows) >= LANES - RIM
            for t in which:
                s, c = sincos(jnp.where(last, moved(ref, t + 1, r), moved(ref, t, r)))
                s1[q, t * LANES : (t + 1) * LANES] = s
                c1[q, t * LANES : (t + 1) * LANES] = c

        @pl.loop(0, H // 16)
        def _(i):
            r0 = pl.multiple_of(i * 16, 16)
            r = pl.ds(r0, 16)
            for p in range(2):
                hi, lo = split(cotv[p, r, :])
                q = pl.ds(pl.multiple_of(r0 + WIDE, 16), 16)
                xh[p, q, 0:W] = hi
                xl[p, q, 0:W] = lo
            q = pl.ds(pl.multiple_of(r0 + RIM, 16), 16)
            phase_one(phv, r, q, 16, range(tiles - 1))
            s, c = sincos(phv[0, r, :])
            s0[r, :] = s
            c0[r, :] = c
            a, b = incv[0, r, :], incv[1, r, :]
            for p, w in enumerate((a * c - b * s, a * s + b * c)):
                wz[p, r, :] = w
                hi, lo = split(w)
                zh[p, q, 0:W] = hi
                zl[p, q, 0:W] = lo

        for k in (2, 3, 4, 5, 6, 7):
            copies[k].wait_recv()
        for side in range(2):
            q = slice(0, WIDE) if side == 0 else slice(WIDE + H, WIDE + H + WIDE)
            for p in range(2):
                hi, lo = split(crow[side, p])
                xh[p, q, 0:W] = hi
                xl[p, q, 0:W] = lo
            q = slice(0, RIM) if side == 0 else slice(RIM + H, RIM + H + RIM)
            phase_one(prow.at[side], slice(0, RIM), q, RIM, range(tiles - 1))
            s, c = sincos(prow[side, 0])
            a, b = irow[side, 0], irow[side, 1]
            for p, w in enumerate((a * c - b * s, a * s + b * c)):
                hi, lo = split(w)
                zh[p, q, 0:W] = hi
                zl[p, q, 0:W] = lo

        def across_pass(src_h, src_l, dst, band, rows, which):
            for t in which:
                dst[t, 0:rows, :] = across(src_h, src_l, band, slice(0, rows), t, tiles)

        down_pass(xh, xl, uh, ul, rowa, H + WIDE, 0, W)
        down_pass(zh, zl, vh, vl, rowf, H, 0, W)
        across_pass(uh, ul, gout, cola, H + WIDE, range(tiles - 1))
        across_pass(vh, vl, fout, colf, H, range(tiles - 1))

        for k in (0, 1, 8, 9, 10, 11):
            copies[k].wait_recv()
        edge = slice(W, full)

        def piece(a, b, index, rows):
            _, w, dst = PIECES[index]
            lane = lanes_of(rows)
            a = pltpu.roll(a, (LANES - w - dst) % LANES, 1)
            b = pltpu.roll(b, (-dst) % LANES, 1) if dst else b
            return jnp.where(lane < w, b, jnp.where(lane >= LANES - w, a, 0.0))

        xstep = block(H + 2 * WIDE, 96)

        @pl.loop(0, (H + 2 * WIDE) // xstep)
        def _(i):
            r = pl.ds(pl.multiple_of(i * xstep, 16), xstep)
            a, b = hl[r, :], hr[r, :]
            for p in range(2):
                hi, lo = split(piece(a, b, p, xstep))
                xh[p, r, edge] = hi
                xl[p, r, edge] = lo

        estep = block(H + WIDE, 64)

        def phase_edge(r, q, own, own_r, rows):
            a, b = hl[q, :], hr[q, :]
            _, _, dst = PIECES[2]
            lane = lanes_of(rows)
            inner = moved(own, tiles - 1, own_r)
            x = jnp.where(lane >= LANES - RIM, pltpu.roll(b, LANES - RIM - dst, 1), inner)
            outer = jnp.where(lane >= LANES - WIDE, pltpu.roll(a, LANES - WIDE - dst, 1), 0.0)
            y = jnp.where(lane >= LANES - RIM, moved(own, 0, own_r), outer)
            for t, v in ((tiles - 1, x), (tiles, y)):
                s, c = sincos(v)
                s1[r, t * LANES : (t + 1) * LANES] = s
                c1[r, t * LANES : (t + 1) * LANES] = c

        hstep = block(H, 64)

        @pl.loop(0, H // hstep)
        def _(i):
            r = pl.ds(pl.multiple_of(i * hstep + RIM, 16), hstep)
            q = pl.ds(pl.multiple_of(i * hstep + WIDE, 16), hstep)
            phase_edge(r, q, phv, pl.ds(pl.multiple_of(i * hstep, 16), hstep), hstep)

        for side in range(2):
            e = side * (H + RIM)
            phase_edge(slice(e, e + RIM), slice(e + RIM, e + WIDE), prow.at[side], slice(0, RIM), RIM)

        @pl.loop(0, (H + WIDE) // estep)
        def _(i):
            r = pl.ds(pl.multiple_of(i * estep, 16), estep)
            q = pl.ds(pl.multiple_of(i * estep + RIM, 16), estep)
            a, b = hl[q, :], hr[q, :]
            s, c = sincos(piece(a, b, 5, estep))
            x, y = piece(a, b, 3, estep), piece(a, b, 4, estep)
            for p, w in enumerate((x * c - y * s, x * s + y * c)):
                hi, lo = split(w)
                zh[p, r, edge] = hi
                zl[p, r, edge] = lo

        down_pass(xh, xl, uh, ul, rowa, H + WIDE, W, full)
        across_pass(uh, ul, gout, cola, H + WIDE, range(tiles - 1, tiles + 1))

        @pl.loop(0, (H + WIDE) // estep)
        def _(i):
            r = pl.ds(pl.multiple_of(i * estep, 16), estep)
            for t in range(tiles + 1):
                cols = slice(t * LANES, (t + 1) * LANES)
                gr, gi = gout[t, r, 0:LANES], gout[t, r, LANES : 2 * LANES]
                c, s = c1[r, cols], s1[r, cols]
                for p, g in enumerate((gr * c + gi * s, gi * c - gr * s)):
                    hi, lo = split(g)
                    gh[p, r, cols] = hi
                    gl[p, r, cols] = lo

        down_pass(zh, zl, vh, vl, rowf, H, W, full)
        across_pass(vh, vl, fout, colf, H, range(tiles - 1, tiles + 1))

        fstep = block(H, 32)

        @pl.loop(0, H // fstep)
        def _(i):
            r = pl.ds(pl.multiple_of(i * fstep, 16), fstep)
            q = pl.ds(pl.multiple_of(i * fstep + RIM, 16), fstep)
            first = lanes_of(fstep) < RIM
            before = None
            for t in [tiles] + list(range(tiles)):
                cols = slice(t * LANES, (t + 1) * LANES)
                gr, gi = gout[t, q, 0:LANES], gout[t, q, LANES : 2 * LANES]
                fr, fi = fout[t, r, 0:LANES], fout[t, r, LANES : 2 * LANES]
                c, s = c1[q, cols], s1[q, cols]
                term = pltpu.roll(gi * (fr * c - fi * s) - gr * (fr * s + fi * c), RIM, 1)
                if before is not None:
                    pgv[r, cols] = jnp.where(first, before, term)
                before = term

        for c in copies:
            c.wait_send()

    V = pltpu.VMEM
    scratch = [
        V((2, H, W), F32), V((2, H, W), F32), V((2, H, W), F32),
        V((H, LANES), F32), V((H, LANES), F32),
        V((H + 2 * WIDE, LANES), F32), V((H + 2 * WIDE, LANES), F32),
        V((2, 2, WIDE, W), F32), V((2, 2, RIM, W), F32), V((2, 2, RIM, W), F32),
        V(tap_shape, F32), V((8, 2 * LANES), F32),
        V((2, H + 2 * WIDE, full), BF16), V((2, H + 2 * WIDE, full), BF16),
        V((2, H + WIDE, full), BF16), V((2, H + WIDE, full), BF16),
        V((2, H + WIDE, full), BF16), V((2, H + WIDE, full), BF16),
        V((2, H, full), BF16), V((2, H, full), BF16),
        V((H + WIDE, full), F32), V((H + WIDE, full), F32),
        V((tiles + 1, H + WIDE, 2 * LANES), F32), V((tiles + 1, H, 2 * LANES), F32),
        V((2 * OUT, 6 * LANES), BF16),
        V((12 * LANES, 2 * LANES), BF16), V((12 * LANES, 2 * LANES), BF16),
        pltpu.SemaphoreType.DMA((4,)),
        pltpu.SemaphoreType.DMA((12,)), pltpu.SemaphoreType.DMA((12,)),
    ]
    results = (
        V((2, H + WIDE, full), BF16), V((2, H + WIDE, full), BF16),
        V((H, W), F32), V((2, H, W), F32), V((H, W), F32), V((H, W), F32),
        V((2 * OUT, 6 * LANES), BF16), V((12 * LANES, 2 * LANES), BF16),
    )
    return pl.pallas_call(
        kernel,
        out_shape=results,
        in_specs=[pl.BlockSpec(memory_space=pltpu.HBM)] * 4,
        out_specs=tuple(pl.BlockSpec(memory_space=V) for _ in results),
        scratch_shapes=scratch,
        compiler_params=pltpu.CompilerParams(
            collective_id=0, has_side_effects=True, vmem_limit_bytes=40 * 1024 * 1024
        ),
        cost_estimate=pl.CostEstimate(flops=10**10, bytes_accessed=5 * 10**6, transcendentals=0),
    )


def make_last(H, W):
    tiles = W // LANES
    step = block(H, 160)

    def kernel(gh, gl, pgv, wz, c0, s0, rowa, colb, pg, pb, vh, vl, term, probe, store):
        copies = []

        def put(src, dst):
            c = pltpu.make_async_copy(src, dst, store.at[len(copies)])
            c.start()
            copies.append(c)

        put(pgv, pg.at[1])
        down_pass(gh, gl, vh, vl, rowa, H, 0, W + LANES)
        for r0 in range(0, H, step):
            r = slice(r0, r0 + step)
            for t in range(tiles):
                cols = slice(t * LANES, (t + 1) * LANES)
                g = across(vh, vl, colb, r, t - 1, tiles)
                gr, gi = g[:, 0:LANES], g[:, LANES : 2 * LANES]
                c, s = c0[r, cols], s0[r, cols]
                term[r, cols] = gi * wz[0, r, cols] - gr * wz[1, r, cols]
                probe[0, r, cols] = gr * c + gi * s
                probe[1, r, cols] = gi * c - gr * s
            put(term.at[r], pg.at[0, r])
            put(probe.at[:, r], pb.at[:, r])
        for c in copies:
            c.wait()

    V = pltpu.VMEM
    out = jax.ShapeDtypeStruct((2, H, W), F32)
    return pl.pallas_call(
        kernel,
        out_shape=(out, out),
        in_specs=[pl.BlockSpec(memory_space=V)] * 8,
        out_specs=(pl.BlockSpec(memory_space=pltpu.HBM),) * 2,
        scratch_shapes=[
            V((2, H, W + LANES), BF16), V((2, H, W + LANES), BF16), V((H, W), F32), V((2, H, W), F32),
            pltpu.SemaphoreType.DMA((1 + 2 * (H // step),)),
        ],
        compiler_params=pltpu.CompilerParams(vmem_limit_bytes=32 * 1024 * 1024),
        cost_estimate=pl.CostEstimate(flops=10**10, bytes_accessed=5 * 10**6, transcendentals=0),
    )


def on_device(incident, phases, cotangent, propagator):
    H, W = incident.shape[1], incident.shape[2]
    operands = [pltpu.with_memory_space_constraint(x, pltpu.HBM) for x in (incident, phases, cotangent, propagator)]
    return make_last(H, W)(*make_kernel(H, W, propagator.shape)(*operands))


def solution(mesh):
    placed = (P(None, "ty", "tx"), P(None, "ty", "tx"), P(None, "ty", "tx"), P())
    return jax.shard_map(
        on_device,
        mesh=mesh,
        in_specs=placed,
        out_specs=(P(None, "ty", "tx"), P(None, "ty", "tx")),
        check_vma=False,
    )
```

```python
import jax
import jax.numpy as jnp
from jax import lax
from jax.experimental import pallas as pl
from jax.experimental.pallas import tpu as pltpu
from jax.sharding import PartitionSpec as P

RIM = 16
WIDE = 2 * RIM
LANES = 128
OUT = LANES - WIDE
F32 = jnp.float32
BF16 = jnp.bfloat16


def block(rows, most):
    return max(n for n in range(16, most + 1, 16) if rows % n == 0)


def sincos(angle):
    half = angle * 0.5
    sq = half * half
    s = -1.0 / 39916800.0
    for c in (1.0 / 362880.0, -1.0 / 5040.0, 1.0 / 120.0, -1.0 / 6.0):
        s = s * sq + c
    s = half + half * sq * s
    c = 1.0 / 479001600.0
    for k in (-1.0 / 3628800.0, 1.0 / 40320.0, -1.0 / 720.0, 1.0 / 24.0, -0.5, 1.0):
        c = c * sq + k
    return 2.0 * s * c, 1.0 - 2.0 * s * s


def split(x):
    hi = x.astype(BF16)
    return hi, (x - hi.astype(F32)).astype(BF16)


def lanes_of(rows, width=LANES):
    return lax.broadcasted_iota(jnp.int32, (rows, width), 1)


def toeplitz(line, rows, width, shift):
    wide = jnp.broadcast_to(line[:, :width], (rows, width))
    return pltpu.roll(wide, shift % width, 1, stride=1, stride_axis=0)


def down_pass(src_h, src_l, dst_h, dst_l, band, rows, lo_lane, hi_lane):
    starts = list(range(0, rows - OUT, OUT)) + [rows - OUT]
    cols = slice(lo_lane, hi_lane)
    for q0 in starts:
        win = slice(q0, q0 + LANES)
        hi = [src_h[0, win, cols], src_h[1, win, cols]]
        lo = [src_l[0, win, cols], src_l[1, win, cols]]
        operand = jnp.concatenate(hi + lo + hi, axis=0)
        u = jnp.dot(band[...], operand, preferred_element_type=F32)
        h, l = split(u)
        for p in range(2):
            dst_h[p, q0 : q0 + OUT, cols] = h[p * OUT : (p + 1) * OUT]
            dst_l[p, q0 : q0 + OUT, cols] = l[p * OUT : (p + 1) * OUT]


def across(src_h, src_l, band, rows, t, tiles):
    a, b = [slice(n * LANES, (n + 1) * LANES) for n in (t % (tiles + 1), (t + 1) % (tiles + 1))]
    hi = [src_h[0, rows, a], src_h[0, rows, b], src_h[1, rows, a], src_h[1, rows, b]]
    lo = [src_l[0, rows, a], src_l[0, rows, b], src_l[1, rows, a], src_l[1, rows, b]]
    return jnp.dot(jnp.concatenate(hi + lo + hi, axis=1), band[...], preferred_element_type=F32)


def weave(parts, rows):
    lane = lanes_of(rows)
    out = None
    for value, src, dst in parts:
        turn = (dst - src) % LANES
        value = pltpu.roll(value, turn, 1) if turn else value
        out = value if out is None else jnp.where(lane >= dst, value, out)
    return out


def edges(a, b, width, src):
    lane = lanes_of(a.shape[0])
    turn = (LANES - width - src) % LANES
    a = pltpu.roll(a, turn, 1) if turn else a
    b = pltpu.roll(b, -src % LANES, 1) if src else b
    return jnp.where(lane < width, b, jnp.where(lane >= LANES - width, a, 0.0))


def make_kernel(H, W, tap_shape):
    tiles = W // LANES
    full = W + LANES

    def kernel(
        inc, ph, cot, prop, gh, gl, pgv, wz, c0, s0, rowa, colb,
        incv, phv, cotv, packl, packr, wavel, waver, corner, cl, cr, wl, wr, met, crow, irow, prow,
        taps, line, xh, xl, zh, zl, uh, ul, vh, vl,
        c1, s1, gout, fout, rowf, colf, cola,
        load, send, recv,
    ):
        ty, tx = lax.axis_index("ty"), lax.axis_index("tx")
        ny, nx = lax.axis_size("ty"), lax.axis_size("tx")
        up, down = lax.rem(ty + ny - 1, ny), lax.rem(ty + 1, ny)
        left, right = lax.rem(tx + nx - 1, nx), lax.rem(tx + 1, nx)

        pairs = [(a.at[p], b.at[p]) for a, b, p in ((cot, cotv, 0), (cot, cotv, 1), (ph, phv, 1), (ph, phv, 0), (inc, incv, 0), (inc, incv, 1))]
        loads = [pltpu.make_async_copy(src, dst, load.at[k]) for k, (src, dst) in enumerate(pairs + [(prop, taps)])]
        for c in loads:
            c.start()
        barrier = pltpu.get_barrier_semaphore()
        others = [(up, tx), (down, tx), (ty, left), (ty, right), (up, left), (up, right), (down, left), (down, right)]
        for dev in others:
            pl.semaphore_signal(barrier, inc=1, device_id=dev, device_id_type=pl.DeviceIdType.MESH)

        sides = ((slice(0, LANES), 0), (slice(W - LANES, W), 1))
        part2, part4, part8 = H // 2, H // 4, H // 8
        for c in loads[:3]:
            c.wait()
        for (cols, far), dst in zip(sides, (packl, packr)):
            src = far * (LANES - WIDE)
            for r0 in range(0, part2, part4):
                dst[r0 : r0 + part4, :] = weave(
                    [(cotv[p, g * part2 + r0 : g * part2 + r0 + part4, cols], src, 2 * WIDE * g + WIDE * p) for g in range(2) for p in range(2)],
                    part4,
                )
            src = far * (LANES - RIM)
            dst[part2 : part2 + part8, :] = weave(
                [(phv[1, g * part8 : (g + 1) * part8, cols], src, RIM * g) for g in range(8)], part8
            )

        pl.semaphore_wait(barrier, 8)
        copies = []

        def push(src, dst, dev):
            k = len(copies)
            c = pltpu.make_async_remote_copy(
                src_ref=src, dst_ref=dst, send_sem=send.at[k], recv_sem=recv.at[k],
                device_id=dev, device_id_type=pl.DeviceIdType.MESH,
            )
            c.start()
            copies.append(c)

        push(packl, cr, (ty, left))
        push(packr, cl, (ty, right))
        push(cot.at[:, 0:WIDE, :], crow.at[1], (up, tx))
        push(cot.at[:, H - WIDE : H, :], crow.at[0], (down, tx))
        push(inc.at[:, 0:RIM, :], irow.at[1], (up, tx))
        push(inc.at[:, H - RIM : H, :], irow.at[0], (down, tx))
        push(ph.at[:, 0:RIM, :], prow.at[1], (up, tx))
        push(ph.at[:, H - RIM : H, :], prow.at[0], (down, tx))

        for c in loads[3:]:
            c.wait()

        @pl.loop(0, H // 16)
        def _(i):
            r0 = pl.multiple_of(i * 16, 16)
            r = pl.ds(r0, 16)
            q = pl.ds(pl.multiple_of(r0 + RIM, 16), 16)
            s, c = sincos(phv[0, r, :])
            s0[r, :] = s
            c0[r, :] = c
            a, b = incv[0, r, :], incv[1, r, :]
            for p, w in enumerate((a * c - b * s, a * s + b * c)):
                wz[p, r, :] = w
                hi, lo = split(w)
                zh[p, q, 0:W] = hi
                zl[p, q, 0:W] = lo

        for n, (cols, far) in enumerate(sides):
            wide, rim = far * (LANES - WIDE), far * (LANES - RIM)
            for m, r in enumerate((slice(0, WIDE), slice(H - WIDE, H))):
                corner[n, m] = weave(
                    [(cotv[0, r, cols], wide, 0), (cotv[1, r, cols], wide, WIDE), (phv[1, r, cols], rim, 2 * WIDE)]
                    + [(wz[p, r, cols], rim, 2 * WIDE + RIM * (p + 1)) for p in range(2)],
                    WIDE,
                )
        for (cols, far), dst in zip(sides, (wavel, waver)):
            src = far * (LANES - RIM)
            dst[...] = weave(
                [(wz[p, g * part4 : (g + 1) * part4, cols], src, WIDE * g + RIM * p) for g in range(4) for p in range(2)], part4
            )
        push(corner.at[0, 0], met.at[1, 1], (up, left))
        push(corner.at[0, 1], met.at[1, 0], (down, left))
        push(corner.at[1, 0], met.at[0, 1], (up, right))
        push(corner.at[1, 1], met.at[0, 0], (down, right))
        push(wavel, wr, (ty, left))
        push(waver, wl, (ty, right))

        line[...] = jnp.zeros(line.shape, F32)
        line[0:2, 0 : prop.shape[1]] = taps[...]
        kr, ki = line[0:1, :], line[1:2, :]

        def rows_band(dst, mr, mi):
            top = jnp.concatenate([mr, -mi], axis=1)
            low = jnp.concatenate([mi, mr], axis=1)
            hi, lo = split(jnp.concatenate([top, low], axis=0))
            k = 2 * LANES
            dst[:, 0:k] = hi
            dst[:, k : 2 * k] = hi
            dst[:, 2 * k : 3 * k] = lo

        def cols_band(dst, tr, ti):
            top = jnp.concatenate([tr, ti], axis=1)
            low = jnp.concatenate([-ti, tr], axis=1)
            hi, lo = split(jnp.concatenate([top, low], axis=0))
            k = 4 * LANES
            dst[0:k, :] = hi
            dst[k : 2 * k, :] = hi
            dst[2 * k : 3 * k, :] = lo

        rows_band(rowf, toeplitz(kr, LANES, LANES, 0)[:OUT], toeplitz(ki, LANES, LANES, 0)[:OUT])
        rows_band(rowa, toeplitz(kr, LANES, LANES, -WIDE).T[:OUT], -toeplitz(ki, LANES, LANES, -WIDE).T[:OUT])
        cols_band(colf, toeplitz(kr, LANES, 2 * LANES, 0).T, toeplitz(ki, LANES, 2 * LANES, 0).T)
        cols_band(
            cola,
            toeplitz(kr, 2 * LANES, 2 * LANES, -WIDE)[:, :LANES],
            -toeplitz(ki, 2 * LANES, 2 * LANES, -WIDE)[:, :LANES],
        )

        cols_band(
            colb,
            toeplitz(kr, 2 * LANES, 2 * LANES, -LANES)[:, :LANES],
            -toeplitz(ki, 2 * LANES, 2 * LANES, -LANES)[:, :LANES],
        )

        def moved(ref, t, r):
            return pltpu.roll(ref[1, r, t * LANES : (t + 1) * LANES], LANES - RIM, 1)

        def phase_one(ref, r, q, rows, which):
            last = lanes_of(rows) >= LANES - RIM
            for t in which:
                s, c = sincos(jnp.where(last, moved(ref, t + 1, r), moved(ref, t, r)))
                s1[q, t * LANES : (t + 1) * LANES] = s
                c1[q, t * LANES : (t + 1) * LANES] = c

        @pl.loop(0, H // 16)
        def _(i):
            r0 = pl.multiple_of(i * 16, 16)
            r = pl.ds(r0, 16)
            for p in range(2):
                hi, lo = split(cotv[p, r, :])
                q = pl.ds(pl.multiple_of(r0 + WIDE, 16), 16)
                xh[p, q, 0:W] = hi
                xl[p, q, 0:W] = lo
            q = pl.ds(pl.multiple_of(r0 + RIM, 16), 16)
            phase_one(phv, r, q, 16, range(tiles - 1))

        for k in (2, 3, 4, 5, 6, 7):
            copies[k].wait_recv()
        for side in range(2):
            q = slice(0, WIDE) if side == 0 else slice(WIDE + H, WIDE + H + WIDE)
            for p in range(2):
                hi, lo = split(crow[side, p])
                xh[p, q, 0:W] = hi
                xl[p, q, 0:W] = lo
            q = slice(0, RIM) if side == 0 else slice(RIM + H, RIM + H + RIM)
            phase_one(prow.at[side], slice(0, RIM), q, RIM, range(tiles - 1))
            s, c = sincos(prow[side, 0])
            a, b = irow[side, 0], irow[side, 1]
            for p, w in enumerate((a * c - b * s, a * s + b * c)):
                hi, lo = split(w)
                zh[p, q, 0:W] = hi
                zl[p, q, 0:W] = lo

        def across_pass(src_h, src_l, dst, band, rows, which):
            for t in which:
                dst[t, 0:rows, :] = across(src_h, src_l, band, slice(0, rows), t, tiles)

        down_pass(xh, xl, uh, ul, rowa, H + WIDE, 0, W)
        down_pass(zh, zl, vh, vl, rowf, H, 0, W)
        across_pass(uh, ul, gout, cola, H + WIDE, range(tiles - 1))
        across_pass(vh, vl, fout, colf, H, range(tiles - 1))

        for k in (0, 1, 8, 9, 10, 11):
            copies[k].wait_recv()
        edge = slice(W, full)
        for p in range(2):
            for g in range(2):
                for r0 in range(0, part2, part4):
                    r = slice(r0, r0 + part4)
                    q = slice(WIDE + g * part2 + r0, WIDE + g * part2 + r0 + part4)
                    xh[p, q, edge], xl[p, q, edge] = split(edges(cl[r, :], cr[r, :], WIDE, 2 * WIDE * g + WIDE * p))
            for m, q in enumerate((slice(0, WIDE), slice(WIDE + H, 2 * WIDE + H))):
                xh[p, q, edge], xl[p, q, edge] = split(edges(met[0, m], met[1, m], WIDE, WIDE * p))

        down_pass(xh, xl, uh, ul, rowa, H + WIDE, W, full)
        across_pass(uh, ul, gout, cola, H + WIDE, range(tiles - 1, tiles + 1))

        def phase_edge(q, a, b, src, own, own_r, rows):
            lane = lanes_of(rows)
            inner = moved(own, tiles - 1, own_r)
            x = jnp.where(lane >= LANES - RIM, pltpu.roll(b, (LANES - RIM - src) % LANES, 1), inner)
            outer = jnp.where(lane >= LANES - WIDE, pltpu.roll(a, (LANES - WIDE - src) % LANES, 1), 0.0)
            y = jnp.where(lane >= LANES - RIM, moved(own, 0, own_r), outer)
            for t, v in ((tiles - 1, x), (tiles, y)):
                s, c = sincos(v)
                s1[q, t * LANES : (t + 1) * LANES] = s
                c1[q, t * LANES : (t + 1) * LANES] = c

        for g in range(8):
            r = slice(part2, part2 + part8)
            q = slice(RIM + g * part8, RIM + (g + 1) * part8)
            phase_edge(q, cl[r, :], cr[r, :], RIM * g, phv, slice(g * part8, (g + 1) * part8), part8)
        near = (slice(RIM, WIDE), slice(0, RIM))
        rims = (slice(0, RIM), slice(RIM + H, WIDE + H))
        for m in range(2):
            phase_edge(rims[m], met[0, m, near[m]], met[1, m, near[m]], 2 * WIDE, prow.at[m], slice(0, RIM), RIM)

        estep = block(H + WIDE, 64)

        @pl.loop(0, (H + WIDE) // estep)
        def _(i):
            r = pl.ds(pl.multiple_of(i * estep, 16), estep)
            for t in range(tiles + 1):
                cols = slice(t * LANES, (t + 1) * LANES)
                gr, gi = gout[t, r, 0:LANES], gout[t, r, LANES : 2 * LANES]
                c, s = c1[r, cols], s1[r, cols]
                for p, g in enumerate((gr * c + gi * s, gi * c - gr * s)):
                    hi, lo = split(g)
                    gh[p, r, cols] = hi
                    gl[p, r, cols] = lo

        for k in (12, 13):
            copies[k].wait_recv()
        for p in range(2):
            for g in range(4):
                q = slice(RIM + g * part4, RIM + (g + 1) * part4)
                zh[p, q, edge], zl[p, q, edge] = split(edges(wl[...], wr[...], RIM, WIDE * g + RIM * p))
            for m in range(2):
                value = edges(met[0, m, near[m]], met[1, m, near[m]], RIM, 2 * WIDE + RIM * (p + 1))
                zh[p, rims[m], edge], zl[p, rims[m], edge] = split(value)

        down_pass(zh, zl, vh, vl, rowf, H, W, full)
        across_pass(vh, vl, fout, colf, H, range(tiles - 1, tiles + 1))

        fstep = block(H, 32)

        @pl.loop(0, H // fstep)
        def _(i):
            r = pl.ds(pl.multiple_of(i * fstep, 16), fstep)
            q = pl.ds(pl.multiple_of(i * fstep + RIM, 16), fstep)
            first = lanes_of(fstep) < RIM
            before = None
            for t in [tiles] + list(range(tiles)):
                cols = slice(t * LANES, (t + 1) * LANES)
                gr, gi = gout[t, q, 0:LANES], gout[t, q, LANES : 2 * LANES]
                fr, fi = fout[t, r, 0:LANES], fout[t, r, LANES : 2 * LANES]
                c, s = c1[q, cols], s1[q, cols]
                term = pltpu.roll(gi * (fr * c - fi * s) - gr * (fr * s + fi * c), RIM, 1)
                if before is not None:
                    pgv[r, cols] = jnp.where(first, before, term)
                before = term

        for c in copies:
            c.wait_send()

    V = pltpu.VMEM
    scratch = [
        V((2, H, W), F32), V((2, H, W), F32), V((2, H, W), F32),
        V((H // 2 + H // 8, LANES), F32), V((H // 2 + H // 8, LANES), F32),
        V((H // 4, LANES), F32), V((H // 4, LANES), F32), V((2, 2, WIDE, LANES), F32),
        V((H // 2 + H // 8, LANES), F32), V((H // 2 + H // 8, LANES), F32),
        V((H // 4, LANES), F32), V((H // 4, LANES), F32), V((2, 2, WIDE, LANES), F32),
        V((2, 2, WIDE, W), F32), V((2, 2, RIM, W), F32), V((2, 2, RIM, W), F32),
        V(tap_shape, F32), V((8, 2 * LANES), F32),
        V((2, H + 2 * WIDE, full), BF16), V((2, H + 2 * WIDE, full), BF16),
        V((2, H + WIDE, full), BF16), V((2, H + WIDE, full), BF16),
        V((2, H + WIDE, full), BF16), V((2, H + WIDE, full), BF16),
        V((2, H, full), BF16), V((2, H, full), BF16),
        V((H + WIDE, full), F32), V((H + WIDE, full), F32),
        V((tiles + 1, H + WIDE, 2 * LANES), F32), V((tiles + 1, H, 2 * LANES), F32),
        V((2 * OUT, 6 * LANES), BF16),
        V((12 * LANES, 2 * LANES), BF16), V((12 * LANES, 2 * LANES), BF16),
        pltpu.SemaphoreType.DMA((7,)),
        pltpu.SemaphoreType.DMA((14,)), pltpu.SemaphoreType.DMA((14,)),
    ]
    results = (
        V((2, H + WIDE, full), BF16), V((2, H + WIDE, full), BF16),
        V((H, W), F32), V((2, H, W), F32), V((H, W), F32), V((H, W), F32),
        V((2 * OUT, 6 * LANES), BF16), V((12 * LANES, 2 * LANES), BF16),
    )
    return pl.pallas_call(
        kernel,
        out_shape=results,
        in_specs=[pl.BlockSpec(memory_space=pltpu.HBM)] * 4,
        out_specs=tuple(pl.BlockSpec(memory_space=V) for _ in results),
        scratch_shapes=scratch,
        compiler_params=pltpu.CompilerParams(
            collective_id=0, has_side_effects=True, vmem_limit_bytes=40 * 1024 * 1024
        ),
        cost_estimate=pl.CostEstimate(flops=10**10, bytes_accessed=5 * 10**6, transcendentals=0),
    )


def make_last(H, W):
    tiles = W // LANES
    step = block(H, 160)

    def kernel(gh, gl, pgv, wz, c0, s0, rowa, colb, pg, pb, vh, vl, term, probe, store):
        copies = []

        def put(src, dst):
            c = pltpu.make_async_copy(src, dst, store.at[len(copies)])
            c.start()
            copies.append(c)

        put(pgv, pg.at[1])
        down_pass(gh, gl, vh, vl, rowa, H, 0, W + LANES)
        for r0 in range(0, H, step):
            r = slice(r0, r0 + step)
            for t in range(tiles):
                cols = slice(t * LANES, (t + 1) * LANES)
                g = across(vh, vl, colb, r, t - 1, tiles)
                gr, gi = g[:, 0:LANES], g[:, LANES : 2 * LANES]
                c, s = c0[r, cols], s0[r, cols]
                term[r, cols] = gi * wz[0, r, cols] - gr * wz[1, r, cols]
                probe[0, r, cols] = gr * c + gi * s
                probe[1, r, cols] = gi * c - gr * s
            put(term.at[r], pg.at[0, r])
            put(probe.at[:, r], pb.at[:, r])
        for c in copies:
            c.wait()

    V = pltpu.VMEM
    out = jax.ShapeDtypeStruct((2, H, W), F32)
    return pl.pallas_call(
        kernel,
        out_shape=(out, out),
        in_specs=[pl.BlockSpec(memory_space=V)] * 8,
        out_specs=(pl.BlockSpec(memory_space=pltpu.HBM),) * 2,
        scratch_shapes=[
            V((2, H, W + LANES), BF16), V((2, H, W + LANES), BF16), V((H, W), F32), V((2, H, W), F32),
            pltpu.SemaphoreType.DMA((1 + 2 * (H // step),)),
        ],
        compiler_params=pltpu.CompilerParams(vmem_limit_bytes=32 * 1024 * 1024),
        cost_estimate=pl.CostEstimate(flops=10**10, bytes_accessed=5 * 10**6, transcendentals=0),
    )


def on_device(incident, phases, cotangent, propagator):
    H, W = incident.shape[1], incident.shape[2]
    operands = [pltpu.with_memory_space_constraint(x, pltpu.HBM) for x in (incident, phases, cotangent, propagator)]
    return make_last(H, W)(*make_kernel(H, W, propagator.shape)(*operands))


def solution(mesh):
    placed = (P(None, "ty", "tx"), P(None, "ty", "tx"), P(None, "ty", "tx"), P())
    return jax.shard_map(
        on_device,
        mesh=mesh,
        in_specs=placed,
        out_specs=(P(None, "ty", "tx"), P(None, "ty", "tx")),
        check_vma=False,
    )
```

```python
import jax
import jax.numpy as jnp
from jax import lax
from jax.experimental import pallas as pl
from jax.experimental.pallas import tpu as pltpu
from jax.sharding import PartitionSpec as P

RIM = 16
WIDE = 2 * RIM
LANES = 128
OUT = LANES - WIDE
F32 = jnp.float32
BF16 = jnp.bfloat16


def block(rows, most):
    return max(n for n in range(16, most + 1, 16) if rows % n == 0)


def sincos(angle):
    half = angle * 0.5
    sq = half * half
    s = -1.0 / 39916800.0
    for c in (1.0 / 362880.0, -1.0 / 5040.0, 1.0 / 120.0, -1.0 / 6.0):
        s = s * sq + c
    s = half + half * sq * s
    c = 1.0 / 479001600.0
    for k in (-1.0 / 3628800.0, 1.0 / 40320.0, -1.0 / 720.0, 1.0 / 24.0, -0.5, 1.0):
        c = c * sq + k
    return 2.0 * s * c, 1.0 - 2.0 * s * s


def split(x):
    hi = x.astype(BF16)
    return hi, (x - hi.astype(F32)).astype(BF16)


def lanes_of(rows, width=LANES):
    return lax.broadcasted_iota(jnp.int32, (rows, width), 1)


def toeplitz(line, rows, width, shift):
    wide = jnp.broadcast_to(line[:, :width], (rows, width))
    return pltpu.roll(wide, shift % width, 1, stride=1, stride_axis=0)


def row_blocks(rows):
    return list(range(0, rows - OUT, OUT)) + [rows - OUT]


def down_pass(src_h, src_l, dst_h, dst_l, band, starts, lo_lane, hi_lane):
    cols = slice(lo_lane, hi_lane)
    for q0 in starts:
        win = slice(q0, q0 + LANES)
        hi = [src_h[0, win, cols], src_h[1, win, cols]]
        lo = [src_l[0, win, cols], src_l[1, win, cols]]
        operand = jnp.concatenate(hi + lo + hi, axis=0)
        u = jnp.dot(band[...], operand, preferred_element_type=F32)
        h, l = split(u)
        for p in range(2):
            dst_h[p, q0 : q0 + OUT, cols] = h[p * OUT : (p + 1) * OUT]
            dst_l[p, q0 : q0 + OUT, cols] = l[p * OUT : (p + 1) * OUT]


def across(src_h, src_l, band, rows, t, tiles):
    a, b = [slice(n * LANES, (n + 1) * LANES) for n in (t % (tiles + 1), (t + 1) % (tiles + 1))]
    hi = [src_h[0, rows, a], src_h[0, rows, b], src_h[1, rows, a], src_h[1, rows, b]]
    lo = [src_l[0, rows, a], src_l[0, rows, b], src_l[1, rows, a], src_l[1, rows, b]]
    return jnp.dot(jnp.concatenate(hi + lo + hi, axis=1), band[...], preferred_element_type=F32)


def weave(parts, rows):
    lane = lanes_of(rows)
    out = None
    for value, src, dst in parts:
        turn = (dst - src) % LANES
        value = pltpu.roll(value, turn, 1) if turn else value
        out = value if out is None else jnp.where(lane >= dst, value, out)
    return out


def edges(a, b, width, src):
    lane = lanes_of(a.shape[0])
    turn = (LANES - width - src) % LANES
    a = pltpu.roll(a, turn, 1) if turn else a
    b = pltpu.roll(b, -src % LANES, 1) if src else b
    return jnp.where(lane < width, b, jnp.where(lane >= LANES - width, a, 0.0))


def make_kernel(H, W, tap_shape):
    tiles = W // LANES
    full = W + LANES

    def kernel(
        inc, ph, cot, prop, th, tl, pgv, wz, c0, s0, colb,
        tilel, tiler, phasel, phaser, incv, phv, cotv, packl, packr, wavel, waver, corner, cl, cr, wl, wr, met, crow, irow, prow,
        taps, line, xh, xl, zh, zl, gh, gl, uh, ul, vh, vl,
        c1, s1, gout, fout, rowf, rowa, colf, cola,
        load, send, recv,
    ):
        ty, tx = lax.axis_index("ty"), lax.axis_index("tx")
        ny, nx = lax.axis_size("ty"), lax.axis_size("tx")
        up, down = lax.rem(ty + ny - 1, ny), lax.rem(ty + 1, ny)
        left, right = lax.rem(tx + nx - 1, nx), lax.rem(tx + 1, nx)

        near_edge = ((cot, slice(0, 2), tilel), (cot, slice(0, 2), tiler), (ph, 1, phasel), (ph, 1, phaser))
        first = [
            pltpu.make_async_copy(src.at[p, :, slice(0, LANES) if k % 2 == 0 else slice(W - LANES, W)], dst, load.at[7 + k])
            for k, (src, p, dst) in enumerate(near_edge)
        ]
        for c in first:
            c.start()
        pairs = [(a.at[p], b.at[p]) for a, b, p in ((cot, cotv, 0), (cot, cotv, 1), (ph, phv, 1), (ph, phv, 0), (inc, incv, 0), (inc, incv, 1))]
        loads = [pltpu.make_async_copy(src, dst, load.at[k]) for k, (src, dst) in enumerate(pairs + [(prop, taps)])]
        for c in loads:
            c.start()
        barrier = pltpu.get_barrier_semaphore()
        others = [(up, tx), (down, tx), (ty, left), (ty, right), (up, left), (up, right), (down, left), (down, right)]
        for dev in others:
            pl.semaphore_signal(barrier, inc=1, device_id=dev, device_id_type=pl.DeviceIdType.MESH)

        sides = ((slice(0, LANES), 0), (slice(W - LANES, W), 1))
        part2, part4, part8 = H // 2, H // 4, H // 8
        for c in first:
            c.wait()
        for far, cotx, phx, dst in ((0, tilel, phasel, packl), (1, tiler, phaser, packr)):
            src = far * (LANES - WIDE)
            for r0 in range(0, part2, part4):
                dst[r0 : r0 + part4, :] = weave(
                    [(cotx[p, g * part2 + r0 : g * part2 + r0 + part4, :], src, 2 * WIDE * g + WIDE * p) for g in range(2) for p in range(2)],
                    part4,
                )
            src = far * (LANES - RIM)
            dst[part2 : part2 + part8, :] = weave(
                [(phx[g * part8 : (g + 1) * part8, :], src, RIM * g) for g in range(8)], part8
            )

        pl.semaphore_wait(barrier, 8)
        copies = []

        def push(src, dst, dev, start=True):
            k = len(copies)
            c = pltpu.make_async_remote_copy(
                src_ref=src, dst_ref=dst, send_sem=send.at[k], recv_sem=recv.at[k],
                device_id=dev, device_id_type=pl.DeviceIdType.MESH,
            )
            if start:
                c.start()
            copies.append(c)

        odd = lax.rem(tx, 2)

        def push_both(to_left, to_right):
            push(*to_left, (ty, left), start=False)
            push(*to_right, (ty, right), start=False)
            a, b = copies[-2:]

            @pl.when(odd == 0)
            def _():
                a.start()
                b.start()

            @pl.when(odd == 1)
            def _():
                b.start()
                a.start()

        push_both((packl, cr), (packr, cl))
        push(cot.at[:, 0:WIDE, :], crow.at[1], (up, tx))
        push(cot.at[:, H - WIDE : H, :], crow.at[0], (down, tx))
        push(inc.at[:, 0:RIM, :], irow.at[1], (up, tx))
        push(inc.at[:, H - RIM : H, :], irow.at[0], (down, tx))
        push(ph.at[:, 0:RIM, :], prow.at[1], (up, tx))
        push(ph.at[:, H - RIM : H, :], prow.at[0], (down, tx))

        for c in loads:
            c.wait()

        @pl.loop(0, H // 16)
        def _(i):
            r0 = pl.multiple_of(i * 16, 16)
            r = pl.ds(r0, 16)
            q = pl.ds(pl.multiple_of(r0 + RIM, 16), 16)
            s, c = sincos(phv[0, r, :])
            s0[r, :] = s
            c0[r, :] = c
            a, b = incv[0, r, :], incv[1, r, :]
            for p, w in enumerate((a * c - b * s, a * s + b * c)):
                wz[p, r, :] = w
                hi, lo = split(w)
                zh[p, q, 0:W] = hi
                zl[p, q, 0:W] = lo

        for n, (cols, far) in enumerate(sides):
            wide, rim = far * (LANES - WIDE), far * (LANES - RIM)
            for m, r in enumerate((slice(0, WIDE), slice(H - WIDE, H))):
                corner[n, m] = weave(
                    [(cotv[0, r, cols], wide, 0), (cotv[1, r, cols], wide, WIDE), (phv[1, r, cols], rim, 2 * WIDE)]
                    + [(wz[p, r, cols], rim, 2 * WIDE + RIM * (p + 1)) for p in range(2)],
                    WIDE,
                )
        for (cols, far), dst in zip(sides, (wavel, waver)):
            src = far * (LANES - RIM)
            dst[...] = weave(
                [(wz[p, g * part4 : (g + 1) * part4, cols], src, WIDE * g + RIM * p) for g in range(4) for p in range(2)], part4
            )
        push(corner.at[0, 0], met.at[1, 1], (up, left))
        push(corner.at[0, 1], met.at[1, 0], (down, left))
        push(corner.at[1, 0], met.at[0, 1], (up, right))
        push(corner.at[1, 1], met.at[0, 0], (down, right))
        push_both((wavel, wr), (waver, wl))

        line[...] = jnp.zeros(line.shape, F32)
        line[0:2, 0 : prop.shape[1]] = taps[...]
        kr, ki = line[0:1, :], line[1:2, :]

        def rows_band(dst, mr, mi):
            top = jnp.concatenate([mr, -mi], axis=1)
            low = jnp.concatenate([mi, mr], axis=1)
            hi, lo = split(jnp.concatenate([top, low], axis=0))
            k = 2 * LANES
            dst[:, 0:k] = hi
            dst[:, k : 2 * k] = hi
            dst[:, 2 * k : 3 * k] = lo

        def cols_band(dst, tr, ti):
            top = jnp.concatenate([tr, ti], axis=1)
            low = jnp.concatenate([-ti, tr], axis=1)
            hi, lo = split(jnp.concatenate([top, low], axis=0))
            k = 4 * LANES
            dst[0:k, :] = hi
            dst[k : 2 * k, :] = hi
            dst[2 * k : 3 * k, :] = lo

        rows_band(rowf, toeplitz(kr, LANES, LANES, 0)[:OUT], toeplitz(ki, LANES, LANES, 0)[:OUT])
        rows_band(rowa, toeplitz(kr, LANES, LANES, -WIDE).T[:OUT], -toeplitz(ki, LANES, LANES, -WIDE).T[:OUT])
        cols_band(colf, toeplitz(kr, LANES, 2 * LANES, 0).T, toeplitz(ki, LANES, 2 * LANES, 0).T)
        cols_band(
            cola,
            toeplitz(kr, 2 * LANES, 2 * LANES, -WIDE)[:, :LANES],
            -toeplitz(ki, 2 * LANES, 2 * LANES, -WIDE)[:, :LANES],
        )

        cols_band(
            colb,
            toeplitz(kr, 2 * LANES, 2 * LANES, -LANES)[:, :LANES],
            -toeplitz(ki, 2 * LANES, 2 * LANES, -LANES)[:, :LANES],
        )

        def moved(ref, t, r):
            return pltpu.roll(ref[1, r, t * LANES : (t + 1) * LANES], LANES - RIM, 1)

        def phase_one(ref, r, q, rows, which):
            last = lanes_of(rows) >= LANES - RIM
            for t in which:
                s, c = sincos(jnp.where(last, moved(ref, t + 1, r), moved(ref, t, r)))
                s1[q, t * LANES : (t + 1) * LANES] = s
                c1[q, t * LANES : (t + 1) * LANES] = c

        @pl.loop(0, H // 16)
        def _(i):
            r0 = pl.multiple_of(i * 16, 16)
            r = pl.ds(r0, 16)
            for p in range(2):
                hi, lo = split(cotv[p, r, :])
                q = pl.ds(pl.multiple_of(r0 + WIDE, 16), 16)
                xh[p, q, 0:W] = hi
                xl[p, q, 0:W] = lo
            q = pl.ds(pl.multiple_of(r0 + RIM, 16), 16)
            phase_one(phv, r, q, 16, range(tiles - 1))

        xall, zall = row_blocks(H + WIDE), row_blocks(H)
        xin = [q for q in xall if q >= WIDE and q + LANES <= WIDE + H]
        zin = [q for q in zall if q >= RIM and q + LANES <= RIM + H]
        down_pass(xh, xl, uh, ul, rowa, xin, 0, W)
        down_pass(zh, zl, vh, vl, rowf, zin, 0, W)

        for k in (2, 3, 4, 5, 6, 7):
            copies[k].wait_recv()
        for side in range(2):
            q = slice(0, WIDE) if side == 0 else slice(WIDE + H, WIDE + H + WIDE)
            for p in range(2):
                hi, lo = split(crow[side, p])
                xh[p, q, 0:W] = hi
                xl[p, q, 0:W] = lo
            q = slice(0, RIM) if side == 0 else slice(RIM + H, RIM + H + RIM)
            phase_one(prow.at[side], slice(0, RIM), q, RIM, range(tiles - 1))
            s, c = sincos(prow[side, 0])
            a, b = irow[side, 0], irow[side, 1]
            for p, w in enumerate((a * c - b * s, a * s + b * c)):
                hi, lo = split(w)
                zh[p, q, 0:W] = hi
                zl[p, q, 0:W] = lo

        def across_pass(src_h, src_l, dst, band, rows, which):
            for t in which:
                dst[t, 0:rows, :] = across(src_h, src_l, band, slice(0, rows), t, tiles)

        down_pass(xh, xl, uh, ul, rowa, [q for q in xall if q not in xin], 0, W)
        down_pass(zh, zl, vh, vl, rowf, [q for q in zall if q not in zin], 0, W)
        across_pass(uh, ul, gout, cola, H + WIDE, range(tiles - 1))
        across_pass(vh, vl, fout, colf, H, range(tiles - 1))

        estep = block(H + WIDE, 64)

        def turn_back(which):
            @pl.loop(0, (H + WIDE) // estep)
            def _(i):
                r = pl.ds(pl.multiple_of(i * estep, 16), estep)
                for t in which:
                    cols = slice(t * LANES, (t + 1) * LANES)
                    gr, gi = gout[t, r, 0:LANES], gout[t, r, LANES : 2 * LANES]
                    c, s = c1[r, cols], s1[r, cols]
                    for p, g in enumerate((gr * c + gi * s, gi * c - gr * s)):
                        gh[p, r, cols], gl[p, r, cols] = split(g)

        turn_back(range(tiles - 1))
        down_pass(gh, gl, th, tl, rowa, zall, 0, (tiles - 1) * LANES)

        for k in (0, 1, 8, 9, 10, 11):
            copies[k].wait_recv()
        edge = slice(W, full)
        for p in range(2):
            for g in range(2):
                for r0 in range(0, part2, part4):
                    r = slice(r0, r0 + part4)
                    q = slice(WIDE + g * part2 + r0, WIDE + g * part2 + r0 + part4)
                    xh[p, q, edge], xl[p, q, edge] = split(edges(cl[r, :], cr[r, :], WIDE, 2 * WIDE * g + WIDE * p))
            for m, q in enumerate((slice(0, WIDE), slice(WIDE + H, 2 * WIDE + H))):
                xh[p, q, edge], xl[p, q, edge] = split(edges(met[0, m], met[1, m], WIDE, WIDE * p))

        down_pass(xh, xl, uh, ul, rowa, xall, W, full)
        across_pass(uh, ul, gout, cola, H + WIDE, range(tiles - 1, tiles + 1))

        def phase_edge(q, a, b, src, own, own_r, rows):
            lane = lanes_of(rows)
            inner = moved(own, tiles - 1, own_r)
            x = jnp.where(lane >= LANES - RIM, pltpu.roll(b, (LANES - RIM - src) % LANES, 1), inner)
            outer = jnp.where(lane >= LANES - WIDE, pltpu.roll(a, (LANES - WIDE - src) % LANES, 1), 0.0)
            y = jnp.where(lane >= LANES - RIM, moved(own, 0, own_r), outer)
            for t, v in ((tiles - 1, x), (tiles, y)):
                s, c = sincos(v)
                s1[q, t * LANES : (t + 1) * LANES] = s
                c1[q, t * LANES : (t + 1) * LANES] = c

        for g in range(8):
            r = slice(part2, part2 + part8)
            q = slice(RIM + g * part8, RIM + (g + 1) * part8)
            phase_edge(q, cl[r, :], cr[r, :], RIM * g, phv, slice(g * part8, (g + 1) * part8), part8)
        near = (slice(RIM, WIDE), slice(0, RIM))
        rims = (slice(0, RIM), slice(RIM + H, WIDE + H))
        for m in range(2):
            phase_edge(rims[m], met[0, m, near[m]], met[1, m, near[m]], 2 * WIDE, prow.at[m], slice(0, RIM), RIM)

        turn_back(range(tiles - 1, tiles + 1))
        down_pass(gh, gl, th, tl, rowa, zall, (tiles - 1) * LANES, full)

        for k in (12, 13):
            copies[k].wait_recv()
        for p in range(2):
            for g in range(4):
                q = slice(RIM + g * part4, RIM + (g + 1) * part4)
                zh[p, q, edge], zl[p, q, edge] = split(edges(wl[...], wr[...], RIM, WIDE * g + RIM * p))
            for m in range(2):
                value = edges(met[0, m, near[m]], met[1, m, near[m]], RIM, 2 * WIDE + RIM * (p + 1))
                zh[p, rims[m], edge], zl[p, rims[m], edge] = split(value)

        down_pass(zh, zl, vh, vl, rowf, zall, W, full)
        across_pass(vh, vl, fout, colf, H, range(tiles - 1, tiles + 1))

        fstep = block(H, 32)

        @pl.loop(0, H // fstep)
        def _(i):
            r = pl.ds(pl.multiple_of(i * fstep, 16), fstep)
            q = pl.ds(pl.multiple_of(i * fstep + RIM, 16), fstep)
            first = lanes_of(fstep) < RIM
            before = None
            for t in [tiles] + list(range(tiles)):
                cols = slice(t * LANES, (t + 1) * LANES)
                gr, gi = gout[t, q, 0:LANES], gout[t, q, LANES : 2 * LANES]
                fr, fi = fout[t, r, 0:LANES], fout[t, r, LANES : 2 * LANES]
                c, s = c1[q, cols], s1[q, cols]
                term = pltpu.roll(gi * (fr * c - fi * s) - gr * (fr * s + fi * c), RIM, 1)
                if before is not None:
                    pgv[r, cols] = jnp.where(first, before, term)
                before = term

        for c in copies:
            c.wait_send()

    V = pltpu.VMEM
    scratch = [
        V((2, H, LANES), F32), V((2, H, LANES), F32), V((H, LANES), F32), V((H, LANES), F32),
        V((2, H, W), F32), V((2, H, W), F32), V((2, H, W), F32),
        V((H // 2 + H // 8, LANES), F32), V((H // 2 + H // 8, LANES), F32),
        V((H // 4, LANES), F32), V((H // 4, LANES), F32), V((2, 2, WIDE, LANES), F32),
        V((H // 2 + H // 8, LANES), F32), V((H // 2 + H // 8, LANES), F32),
        V((H // 4, LANES), F32), V((H // 4, LANES), F32), V((2, 2, WIDE, LANES), F32),
        V((2, 2, WIDE, W), F32), V((2, 2, RIM, W), F32), V((2, 2, RIM, W), F32),
        V(tap_shape, F32), V((8, 2 * LANES), F32),
        V((2, H + 2 * WIDE, full), BF16), V((2, H + 2 * WIDE, full), BF16),
        V((2, H + WIDE, full), BF16), V((2, H + WIDE, full), BF16),
        V((2, H + WIDE, full), BF16), V((2, H + WIDE, full), BF16),
        V((2, H + WIDE, full), BF16), V((2, H + WIDE, full), BF16),
        V((2, H, full), BF16), V((2, H, full), BF16),
        V((H + WIDE, full), F32), V((H + WIDE, full), F32),
        V((tiles + 1, H + WIDE, 2 * LANES), F32), V((tiles + 1, H, 2 * LANES), F32),
        V((2 * OUT, 6 * LANES), BF16), V((2 * OUT, 6 * LANES), BF16),
        V((12 * LANES, 2 * LANES), BF16), V((12 * LANES, 2 * LANES), BF16),
        pltpu.SemaphoreType.DMA((11,)),
        pltpu.SemaphoreType.DMA((14,)), pltpu.SemaphoreType.DMA((14,)),
    ]
    results = (
        V((2, H, full), BF16), V((2, H, full), BF16),
        V((H, W), F32), V((2, H, W), F32), V((H, W), F32), V((H, W), F32),
        V((12 * LANES, 2 * LANES), BF16),
    )
    return pl.pallas_call(
        kernel,
        out_shape=results,
        in_specs=[pl.BlockSpec(memory_space=pltpu.HBM)] * 4,
        out_specs=tuple(pl.BlockSpec(memory_space=V) for _ in results),
        scratch_shapes=scratch,
        compiler_params=pltpu.CompilerParams(
            collective_id=0, has_side_effects=True, vmem_limit_bytes=40 * 1024 * 1024
        ),
        cost_estimate=pl.CostEstimate(flops=10**10, bytes_accessed=5 * 10**6, transcendentals=0),
    )


def make_last(H, W):
    tiles = W // LANES
    step = block(H, 160)

    def kernel(th, tl, pgv, wz, c0, s0, colb, pg, pb, term, probe, store):
        copies = []

        def put(src, dst):
            c = pltpu.make_async_copy(src, dst, store.at[len(copies)])
            c.start()
            copies.append(c)

        put(pgv, pg.at[1])
        for r0 in range(0, H, step):
            r = slice(r0, r0 + step)
            for t in range(tiles):
                cols = slice(t * LANES, (t + 1) * LANES)
                g = across(th, tl, colb, r, t - 1, tiles)
                gr, gi = g[:, 0:LANES], g[:, LANES : 2 * LANES]
                c, s = c0[r, cols], s0[r, cols]
                term[r, cols] = gi * wz[0, r, cols] - gr * wz[1, r, cols]
                probe[0, r, cols] = gr * c + gi * s
                probe[1, r, cols] = gi * c - gr * s
            put(term.at[r], pg.at[0, r])
            put(probe.at[:, r], pb.at[:, r])
        for c in copies:
            c.wait()

    V = pltpu.VMEM
    out = jax.ShapeDtypeStruct((2, H, W), F32)
    return pl.pallas_call(
        kernel,
        out_shape=(out, out),
        in_specs=[pl.BlockSpec(memory_space=V)] * 7,
        out_specs=(pl.BlockSpec(memory_space=pltpu.HBM),) * 2,
        scratch_shapes=[
            V((H, W), F32), V((2, H, W), F32),
            pltpu.SemaphoreType.DMA((1 + 2 * (H // step),)),
        ],
        compiler_params=pltpu.CompilerParams(vmem_limit_bytes=32 * 1024 * 1024),
        cost_estimate=pl.CostEstimate(flops=10**10, bytes_accessed=5 * 10**6, transcendentals=0),
    )


def on_device(incident, phases, cotangent, propagator):
    H, W = incident.shape[1], incident.shape[2]
    operands = [pltpu.with_memory_space_constraint(x, pltpu.HBM) for x in (incident, phases, cotangent, propagator)]
    return make_last(H, W)(*make_kernel(H, W, propagator.shape)(*operands))


def solution(mesh):
    placed = (P(None, "ty", "tx"), P(None, "ty", "tx"), P(None, "ty", "tx"), P())
    return jax.shard_map(
        on_device,
        mesh=mesh,
        in_specs=placed,
        out_specs=(P(None, "ty", "tx"), P(None, "ty", "tx")),
        check_vma=False,
    )
```

```python
import jax
import jax.numpy as jnp
from jax import lax
from jax.experimental import pallas as pl
from jax.experimental.pallas import tpu as pltpu
from jax.sharding import PartitionSpec as P

RIM = 16
WIDE = 2 * RIM
LANES = 128
OUT = LANES - WIDE
F32 = jnp.float32
BF16 = jnp.bfloat16


def block(rows, most):
    return max(n for n in range(16, most + 1, 16) if rows % n == 0)


def sincos(angle):
    half = angle * 0.5
    sq = half * half
    s = -1.0 / 39916800.0
    for c in (1.0 / 362880.0, -1.0 / 5040.0, 1.0 / 120.0, -1.0 / 6.0):
        s = s * sq + c
    s = half + half * sq * s
    c = 1.0 / 479001600.0
    for k in (-1.0 / 3628800.0, 1.0 / 40320.0, -1.0 / 720.0, 1.0 / 24.0, -0.5, 1.0):
        c = c * sq + k
    return 2.0 * s * c, 1.0 - 2.0 * s * s


def split(x):
    hi = x.astype(BF16)
    return hi, (x - hi.astype(F32)).astype(BF16)


def lanes_of(rows, width=LANES):
    return lax.broadcasted_iota(jnp.int32, (rows, width), 1)


def toeplitz(line, rows, width, shift):
    wide = jnp.broadcast_to(line[:, :width], (rows, width))
    return pltpu.roll(wide, shift % width, 1, stride=1, stride_axis=0)


def row_blocks(rows):
    return list(range(0, rows - OUT, OUT)) + [rows - OUT]


def down_pass(src_h, src_l, dst_h, dst_l, band, starts, lo_lane, hi_lane):
    cols = slice(lo_lane, hi_lane)
    for q0 in starts:
        win = slice(q0, q0 + LANES)
        hi = [src_h[0, win, cols], src_h[1, win, cols]]
        lo = [src_l[0, win, cols], src_l[1, win, cols]]
        operand = jnp.concatenate(hi + lo + hi, axis=0)
        u = jnp.dot(band[...], operand, preferred_element_type=F32)
        h, l = split(u)
        for p in range(2):
            dst_h[p, q0 : q0 + OUT, cols] = h[p * OUT : (p + 1) * OUT]
            dst_l[p, q0 : q0 + OUT, cols] = l[p * OUT : (p + 1) * OUT]


def across(src_h, src_l, band, rows, t, tiles):
    a, b = [slice(n * LANES, (n + 1) * LANES) for n in (t % (tiles + 1), (t + 1) % (tiles + 1))]
    hi = [src_h[0, rows, a], src_h[0, rows, b], src_h[1, rows, a], src_h[1, rows, b]]
    lo = [src_l[0, rows, a], src_l[0, rows, b], src_l[1, rows, a], src_l[1, rows, b]]
    return jnp.dot(jnp.concatenate(hi + lo + hi, axis=1), band[...], preferred_element_type=F32)


def weave(parts, rows):
    lane = lanes_of(rows)
    out = None
    for value, src, dst in parts:
        turn = (dst - src) % LANES
        value = pltpu.roll(value, turn, 1) if turn else value
        out = value if out is None else jnp.where(lane >= dst, value, out)
    return out


def edges(a, b, width, src):
    lane = lanes_of(a.shape[0])
    turn = (LANES - width - src) % LANES
    a = pltpu.roll(a, turn, 1) if turn else a
    b = pltpu.roll(b, -src % LANES, 1) if src else b
    return jnp.where(lane < width, b, jnp.where(lane >= LANES - width, a, 0.0))


def make_kernel(H, W, tap_shape):
    tiles = W // LANES
    full = W + LANES

    def kernel(
        inc, ph, cot, prop, gz, pgv, wz, c0, s0,
        tilel, tiler, phasel, phaser, incv, phv, cotv, packl, packr, wavel, waver, cc, ww, metc, metp, metw, crow, irow, prow,
        taps, line, xh, xl, zh, zl, gh, gl, uh, ul, vh, vl, th, tl,
        c1, s1, gout, fout, rowf, rowa, colf, cola, colb,
        load, send, recv,
    ):
        ty, tx = lax.axis_index("ty"), lax.axis_index("tx")
        ny, nx = lax.axis_size("ty"), lax.axis_size("tx")
        up, down = lax.rem(ty + ny - 1, ny), lax.rem(ty + 1, ny)
        left, right = lax.rem(tx + nx - 1, nx), lax.rem(tx + 1, nx)

        near_edge = ((cot, slice(0, 2), tilel), (cot, slice(0, 2), tiler), (ph, 1, phasel), (ph, 1, phaser))
        first = [
            pltpu.make_async_copy(src.at[p, :, slice(0, LANES) if k % 2 == 0 else slice(W - LANES, W)], dst, load.at[7 + k])
            for k, (src, p, dst) in enumerate(near_edge)
        ]
        for c in first:
            c.start()
        pairs = [(a.at[p], b.at[p]) for a, b, p in ((cot, cotv, 0), (cot, cotv, 1), (ph, phv, 1), (ph, phv, 0), (inc, incv, 0), (inc, incv, 1))]
        loads = [pltpu.make_async_copy(src, dst, load.at[k]) for k, (src, dst) in enumerate(pairs + [(prop, taps)])]
        for c in loads:
            c.start()
        barrier = pltpu.get_barrier_semaphore()
        others = [(up, tx), (down, tx), (ty, left), (ty, right)]
        for dev in others:
            pl.semaphore_signal(barrier, inc=1, device_id=dev, device_id_type=pl.DeviceIdType.MESH)

        sides = ((slice(0, LANES), 0), (slice(W - LANES, W), 1))
        part2, part4, part8 = H // 2, H // 4, H // 8
        for c in first:
            c.wait()
        for far, cotx, phx, dst in ((0, tilel, phasel, packl), (1, tiler, phaser, packr)):
            src = far * (LANES - WIDE)
            for r0 in range(0, part2, part4):
                dst[r0 : r0 + part4, :] = weave(
                    [(cotx[p, g * part2 + r0 : g * part2 + r0 + part4, :], src, 2 * WIDE * g + WIDE * p) for g in range(2) for p in range(2)],
                    part4,
                )
            src = far * (LANES - RIM)
            dst[part2 : part2 + part8, :] = weave(
                [(phx[g * part8 : (g + 1) * part8, :], src, RIM * g) for g in range(8)], part8
            )

        pl.semaphore_wait(barrier, 4)
        copies = []

        def push(src, dst, dev, start=True):
            k = len(copies)
            c = pltpu.make_async_remote_copy(
                src_ref=src, dst_ref=dst, send_sem=send.at[k], recv_sem=recv.at[k],
                device_id=dev, device_id_type=pl.DeviceIdType.MESH,
            )
            if start:
                c.start()
            copies.append(c)

        odd = lax.rem(tx, 2)

        def push_both(to_left, to_right):
            push(*to_left, (ty, left), start=False)
            push(*to_right, (ty, right), start=False)
            a, b = copies[-2:]

            @pl.when(odd == 0)
            def _():
                a.start()
                b.start()

            @pl.when(odd == 1)
            def _():
                b.start()
                a.start()

        push_both((packl, cc.at[1]), (packr, cc.at[0]))
        push(cot.at[:, 0:WIDE, :], crow.at[1], (up, tx))
        push(cot.at[:, H - WIDE : H, :], crow.at[0], (down, tx))
        push(inc.at[:, 0:RIM, :], irow.at[1], (up, tx))
        push(inc.at[:, H - RIM : H, :], irow.at[0], (down, tx))
        push(ph.at[:, 0:RIM, :], prow.at[1], (up, tx))
        push(ph.at[:, H - RIM : H, :], prow.at[0], (down, tx))

        for c in loads:
            c.wait()

        @pl.loop(0, H // 16)
        def _(i):
            r0 = pl.multiple_of(i * 16, 16)
            r = pl.ds(r0, 16)
            q = pl.ds(pl.multiple_of(r0 + RIM, 16), 16)
            s, c = sincos(phv[0, r, :])
            s0[r, :] = s
            c0[r, :] = c
            a, b = incv[0, r, :], incv[1, r, :]
            for p, w in enumerate((a * c - b * s, a * s + b * c)):
                wz[p, r, :] = w
                hi, lo = split(w)
                zh[p, q, 0:W] = hi
                zl[p, q, 0:W] = lo

        for (cols, far), dst in zip(sides, (wavel, waver)):
            src = far * (LANES - RIM)
            dst[...] = weave(
                [(wz[p, g * part4 : (g + 1) * part4, cols], src, WIDE * g + RIM * p) for g in range(4) for p in range(2)], part4
            )
        push_both((wavel, ww.at[1]), (waver, ww.at[0]))

        line[...] = jnp.zeros(line.shape, F32)
        line[0:2, 0 : prop.shape[1]] = taps[...]
        kr, ki = line[0:1, :], line[1:2, :]

        def rows_band(dst, mr, mi):
            top = jnp.concatenate([mr, -mi], axis=1)
            low = jnp.concatenate([mi, mr], axis=1)
            hi, lo = split(jnp.concatenate([top, low], axis=0))
            k = 2 * LANES
            dst[:, 0:k] = hi
            dst[:, k : 2 * k] = hi
            dst[:, 2 * k : 3 * k] = lo

        def cols_band(dst, tr, ti):
            top = jnp.concatenate([tr, ti], axis=1)
            low = jnp.concatenate([-ti, tr], axis=1)
            hi, lo = split(jnp.concatenate([top, low], axis=0))
            k = 4 * LANES
            dst[0:k, :] = hi
            dst[k : 2 * k, :] = hi
            dst[2 * k : 3 * k, :] = lo

        rows_band(rowf, toeplitz(kr, LANES, LANES, 0)[:OUT], toeplitz(ki, LANES, LANES, 0)[:OUT])
        rows_band(rowa, toeplitz(kr, LANES, LANES, -WIDE).T[:OUT], -toeplitz(ki, LANES, LANES, -WIDE).T[:OUT])
        cols_band(colf, toeplitz(kr, LANES, 2 * LANES, 0).T, toeplitz(ki, LANES, 2 * LANES, 0).T)
        cols_band(
            cola,
            toeplitz(kr, 2 * LANES, 2 * LANES, -WIDE)[:, :LANES],
            -toeplitz(ki, 2 * LANES, 2 * LANES, -WIDE)[:, :LANES],
        )

        cols_band(
            colb,
            toeplitz(kr, 2 * LANES, 2 * LANES, -LANES)[:, :LANES],
            -toeplitz(ki, 2 * LANES, 2 * LANES, -LANES)[:, :LANES],
        )

        def moved(ref, t, r):
            return pltpu.roll(ref[1, r, t * LANES : (t + 1) * LANES], LANES - RIM, 1)

        def phase_one(ref, r, q, rows, which):
            last = lanes_of(rows) >= LANES - RIM
            for t in which:
                s, c = sincos(jnp.where(last, moved(ref, t + 1, r), moved(ref, t, r)))
                s1[q, t * LANES : (t + 1) * LANES] = s
                c1[q, t * LANES : (t + 1) * LANES] = c

        @pl.loop(0, H // 16)
        def _(i):
            r0 = pl.multiple_of(i * 16, 16)
            r = pl.ds(r0, 16)
            for p in range(2):
                hi, lo = split(cotv[p, r, :])
                q = pl.ds(pl.multiple_of(r0 + WIDE, 16), 16)
                xh[p, q, 0:W] = hi
                xl[p, q, 0:W] = lo
            q = pl.ds(pl.multiple_of(r0 + RIM, 16), 16)
            phase_one(phv, r, q, 16, range(tiles - 1))

        xall, zall = row_blocks(H + WIDE), row_blocks(H)
        xin = [q for q in xall if q >= WIDE and q + LANES <= WIDE + H]
        zin = [q for q in zall if q >= RIM and q + LANES <= RIM + H]
        down_pass(xh, xl, uh, ul, rowa, xin, 0, W)
        down_pass(zh, zl, vh, vl, rowf, zin, 0, W)

        for c in copies[2:8]:
            c.wait_recv()
        for side in range(2):
            q = slice(0, WIDE) if side == 0 else slice(WIDE + H, WIDE + H + WIDE)
            for p in range(2):
                hi, lo = split(crow[side, p])
                xh[p, q, 0:W] = hi
                xl[p, q, 0:W] = lo
            q = slice(0, RIM) if side == 0 else slice(RIM + H, RIM + H + RIM)
            phase_one(prow.at[side], slice(0, RIM), q, RIM, range(tiles - 1))
            s, c = sincos(prow[side, 0])
            a, b = irow[side, 0], irow[side, 1]
            for p, w in enumerate((a * c - b * s, a * s + b * c)):
                hi, lo = split(w)
                zh[p, q, 0:W] = hi
                zl[p, q, 0:W] = lo

        def across_pass(src_h, src_l, dst, band, rows, which):
            for t in which:
                dst[t, 0:rows, :] = across(src_h, src_l, band, slice(0, rows), t, tiles)

        down_pass(xh, xl, uh, ul, rowa, [q for q in xall if q not in xin], 0, W)
        down_pass(zh, zl, vh, vl, rowf, [q for q in zall if q not in zin], 0, W)
        across_pass(uh, ul, gout, cola, H + WIDE, range(tiles - 1))
        across_pass(vh, vl, fout, colf, H, range(tiles - 1))

        estep = block(H + WIDE, 64)

        def turn_back(which):
            @pl.loop(0, (H + WIDE) // estep)
            def _(i):
                r = pl.ds(pl.multiple_of(i * estep, 16), estep)
                for t in which:
                    cols = slice(t * LANES, (t + 1) * LANES)
                    gr, gi = gout[t, r, 0:LANES], gout[t, r, LANES : 2 * LANES]
                    c, s = c1[r, cols], s1[r, cols]
                    for p, g in enumerate((gr * c + gi * s, gi * c - gr * s)):
                        gh[p, r, cols], gl[p, r, cols] = split(g)

        turn_back(range(tiles - 1))
        down_pass(gh, gl, th, tl, rowa, zall, 0, (tiles - 1) * LANES)

        for c in copies[0:2]:
            c.wait_recv()
        push(cc.at[:, 0:WIDE], metc.at[1], (up, tx))
        push(cc.at[:, part2 - WIDE : part2], metc.at[0], (down, tx))
        push(cc.at[:, part2 : part2 + RIM], metp.at[1], (up, tx))
        push(cc.at[:, part2 + part8 - RIM : part2 + part8], metp.at[0], (down, tx))
        edge = slice(W, full)
        for p in range(2):
            for g in range(2):
                for r0 in range(0, part2, part4):
                    r = slice(r0, r0 + part4)
                    q = slice(WIDE + g * part2 + r0, WIDE + g * part2 + r0 + part4)
                    xh[p, q, edge], xl[p, q, edge] = split(edges(cc[0, r, :], cc[1, r, :], WIDE, 2 * WIDE * g + WIDE * p))
        down_pass(xh, xl, uh, ul, rowa, xin, W, full)

        def phase_edge(q, a, b, src, own, own_r, rows):
            lane = lanes_of(rows)
            inner = moved(own, tiles - 1, own_r)
            x = jnp.where(lane >= LANES - RIM, pltpu.roll(b, (LANES - RIM - src) % LANES, 1), inner)
            outer = jnp.where(lane >= LANES - WIDE, pltpu.roll(a, (LANES - WIDE - src) % LANES, 1), 0.0)
            y = jnp.where(lane >= LANES - RIM, moved(own, 0, own_r), outer)
            for t, v in ((tiles - 1, x), (tiles, y)):
                s, c = sincos(v)
                s1[q, t * LANES : (t + 1) * LANES] = s
                c1[q, t * LANES : (t + 1) * LANES] = c

        for g in range(8):
            r = slice(part2, part2 + part8)
            q = slice(RIM + g * part8, RIM + (g + 1) * part8)
            phase_edge(q, cc[0, r, :], cc[1, r, :], RIM * g, phv, slice(g * part8, (g + 1) * part8), part8)
        for c in copies[10:14]:
            c.wait_recv()
        rims = (slice(0, RIM), slice(RIM + H, WIDE + H))
        for m, q in enumerate((slice(0, WIDE), slice(WIDE + H, 2 * WIDE + H))):
            for p in range(2):
                xh[p, q, edge], xl[p, q, edge] = split(edges(metc[m, 0], metc[m, 1], WIDE, (1 - m) * 2 * WIDE + WIDE * p))
            phase_edge(rims[m], metp[m, 0], metp[m, 1], (1 - m) * 7 * RIM, prow.at[m], slice(0, RIM), RIM)
        down_pass(xh, xl, uh, ul, rowa, [q for q in xall if q not in xin], W, full)
        across_pass(uh, ul, gout, cola, H + WIDE, range(tiles - 1, tiles + 1))

        turn_back(range(tiles - 1, tiles + 1))
        down_pass(gh, gl, th, tl, rowa, zall, (tiles - 1) * LANES, full)

        for c in copies[8:10]:
            c.wait_recv()
        push(ww.at[:, 0:RIM], metw.at[1], (up, tx))
        push(ww.at[:, part4 - RIM : part4], metw.at[0], (down, tx))
        for p in range(2):
            for g in range(4):
                q = slice(RIM + g * part4, RIM + (g + 1) * part4)
                zh[p, q, edge], zl[p, q, edge] = split(edges(ww[0], ww[1], RIM, WIDE * g + RIM * p))
        down_pass(zh, zl, vh, vl, rowf, zin, W, full)
        for t in range(tiles):
            gz[t] = across(th, tl, colb, slice(0, H), t - 1, tiles)
        for c in copies[14:16]:
            c.wait_recv()
        for m in range(2):
            for p in range(2):
                value = edges(metw[m, 0], metw[m, 1], RIM, (1 - m) * 3 * WIDE + RIM * p)
                zh[p, rims[m], edge], zl[p, rims[m], edge] = split(value)
        down_pass(zh, zl, vh, vl, rowf, [q for q in zall if q not in zin], W, full)
        across_pass(vh, vl, fout, colf, H, range(tiles - 1, tiles + 1))

        fstep = block(H, 32)

        @pl.loop(0, H // fstep)
        def _(i):
            r = pl.ds(pl.multiple_of(i * fstep, 16), fstep)
            q = pl.ds(pl.multiple_of(i * fstep + RIM, 16), fstep)
            first = lanes_of(fstep) < RIM
            before = None
            for t in [tiles] + list(range(tiles)):
                cols = slice(t * LANES, (t + 1) * LANES)
                gr, gi = gout[t, q, 0:LANES], gout[t, q, LANES : 2 * LANES]
                fr, fi = fout[t, r, 0:LANES], fout[t, r, LANES : 2 * LANES]
                c, s = c1[q, cols], s1[q, cols]
                term = pltpu.roll(gi * (fr * c - fi * s) - gr * (fr * s + fi * c), RIM, 1)
                if before is not None:
                    pgv[r, cols] = jnp.where(first, before, term)
                before = term

        for c in copies:
            c.wait_send()

    V = pltpu.VMEM
    scratch = [
        V((2, H, LANES), F32), V((2, H, LANES), F32), V((H, LANES), F32), V((H, LANES), F32),
        V((2, H, W), F32), V((2, H, W), F32), V((2, H, W), F32),
        V((H // 2 + H // 8, LANES), F32), V((H // 2 + H // 8, LANES), F32),
        V((H // 4, LANES), F32), V((H // 4, LANES), F32),
        V((2, H // 2 + H // 8, LANES), F32), V((2, H // 4, LANES), F32),
        V((2, 2, WIDE, LANES), F32), V((2, 2, RIM, LANES), F32), V((2, 2, RIM, LANES), F32),
        V((2, 2, WIDE, W), F32), V((2, 2, RIM, W), F32), V((2, 2, RIM, W), F32),
        V(tap_shape, F32), V((8, 2 * LANES), F32),
        V((2, H + 2 * WIDE, full), BF16), V((2, H + 2 * WIDE, full), BF16),
        V((2, H + WIDE, full), BF16), V((2, H + WIDE, full), BF16),
        V((2, H + WIDE, full), BF16), V((2, H + WIDE, full), BF16),
        V((2, H + WIDE, full), BF16), V((2, H + WIDE, full), BF16),
        V((2, H, full), BF16), V((2, H, full), BF16),
        V((2, H, full), BF16), V((2, H, full), BF16),
        V((H + WIDE, full), F32), V((H + WIDE, full), F32),
        V((tiles + 1, H + WIDE, 2 * LANES), F32), V((tiles + 1, H, 2 * LANES), F32),
        V((2 * OUT, 6 * LANES), BF16), V((2 * OUT, 6 * LANES), BF16),
        V((12 * LANES, 2 * LANES), BF16), V((12 * LANES, 2 * LANES), BF16), V((12 * LANES, 2 * LANES), BF16),
        pltpu.SemaphoreType.DMA((11,)),
        pltpu.SemaphoreType.DMA((16,)), pltpu.SemaphoreType.DMA((16,)),
    ]
    results = (
        V((tiles, H, 2 * LANES), F32),
        V((H, W), F32), V((2, H, W), F32), V((H, W), F32), V((H, W), F32),
    )
    return pl.pallas_call(
        kernel,
        out_shape=results,
        in_specs=[pl.BlockSpec(memory_space=pltpu.HBM)] * 4,
        out_specs=tuple(pl.BlockSpec(memory_space=V) for _ in results),
        scratch_shapes=scratch,
        compiler_params=pltpu.CompilerParams(
            collective_id=0, has_side_effects=True, vmem_limit_bytes=40 * 1024 * 1024
        ),
        cost_estimate=pl.CostEstimate(flops=10**10, bytes_accessed=5 * 10**6, transcendentals=0),
    )


def make_last(H, W):
    tiles = W // LANES
    step = block(H, 80)

    def kernel(gz, pgv, wz, c0, s0, pg, pb, term, probe, store):
        copies = []

        def put(src, dst):
            c = pltpu.make_async_copy(src, dst, store.at[len(copies)])
            c.start()
            copies.append(c)

        put(pgv, pg.at[1])
        for r0 in range(0, H, step):
            r = slice(r0, r0 + step)
            for t in range(tiles):
                cols = slice(t * LANES, (t + 1) * LANES)
                gr, gi = gz[t, r, 0:LANES], gz[t, r, LANES : 2 * LANES]
                c, s = c0[r, cols], s0[r, cols]
                term[r, cols] = gi * wz[0, r, cols] - gr * wz[1, r, cols]
                probe[0, r, cols] = gr * c + gi * s
                probe[1, r, cols] = gi * c - gr * s
            put(term.at[r], pg.at[0, r])
            put(probe.at[:, r], pb.at[:, r])
        for c in copies:
            c.wait()

    V = pltpu.VMEM
    out = jax.ShapeDtypeStruct((2, H, W), F32)
    return pl.pallas_call(
        kernel,
        out_shape=(out, out),
        in_specs=[pl.BlockSpec(memory_space=V)] * 5,
        out_specs=(pl.BlockSpec(memory_space=pltpu.HBM),) * 2,
        scratch_shapes=[
            V((H, W), F32), V((2, H, W), F32),
            pltpu.SemaphoreType.DMA((1 + 2 * (H // step),)),
        ],
        compiler_params=pltpu.CompilerParams(vmem_limit_bytes=32 * 1024 * 1024),
        cost_estimate=pl.CostEstimate(flops=10**6, bytes_accessed=5 * 10**6, transcendentals=0),
    )


def on_device(incident, phases, cotangent, propagator):
    H, W = incident.shape[1], incident.shape[2]
    operands = [pltpu.with_memory_space_constraint(x, pltpu.HBM) for x in (incident, phases, cotangent, propagator)]
    return make_last(H, W)(*make_kernel(H, W, propagator.shape)(*operands))


def solution(mesh):
    placed = (P(None, "ty", "tx"), P(None, "ty", "tx"), P(None, "ty", "tx"), P())
    return jax.shard_map(
        on_device,
        mesh=mesh,
        in_specs=placed,
        out_specs=(P(None, "ty", "tx"), P(None, "ty", "tx")),
        check_vma=False,
    )
```

```python
import jax
import jax.numpy as jnp
from jax import lax
from jax.experimental import pallas as pl
from jax.experimental.pallas import tpu as pltpu
from jax.sharding import PartitionSpec as P

RIM = 16
WIDE = 2 * RIM
LANES = 128
OUT = LANES - WIDE
F32 = jnp.float32
BF16 = jnp.bfloat16


def block(rows, most):
    return max(n for n in range(16, most + 1, 16) if rows % n == 0)


def sincos(angle):
    half = angle * 0.5
    sq = half * half
    s = -1.0 / 39916800.0
    for c in (1.0 / 362880.0, -1.0 / 5040.0, 1.0 / 120.0, -1.0 / 6.0):
        s = s * sq + c
    s = half + half * sq * s
    c = 1.0 / 479001600.0
    for k in (-1.0 / 3628800.0, 1.0 / 40320.0, -1.0 / 720.0, 1.0 / 24.0, -0.5, 1.0):
        c = c * sq + k
    return 2.0 * s * c, 1.0 - 2.0 * s * s


def split(x):
    hi = x.astype(BF16)
    return hi, (x - hi.astype(F32)).astype(BF16)


def lanes_of(rows, width=LANES):
    return lax.broadcasted_iota(jnp.int32, (rows, width), 1)


def toeplitz(line, rows, width, shift):
    wide = jnp.broadcast_to(line[:, :width], (rows, width))
    return pltpu.roll(wide, shift % width, 1, stride=1, stride_axis=0)


def row_blocks(rows):
    return list(range(0, rows - OUT, OUT)) + [rows - OUT]


def down_pass(src_h, src_l, dst_h, dst_l, band, starts, lo_lane, hi_lane):
    cols = slice(lo_lane, hi_lane)
    for q0 in starts:
        win = slice(q0, q0 + LANES)
        hi = [src_h[0, win, cols], src_h[1, win, cols]]
        lo = [src_l[0, win, cols], src_l[1, win, cols]]
        operand = jnp.concatenate(hi + lo + hi, axis=0)
        u = jnp.dot(band[...], operand, preferred_element_type=F32)
        h, l = split(u)
        for p in range(2):
            dst_h[p, q0 : q0 + OUT, cols] = h[p * OUT : (p + 1) * OUT]
            dst_l[p, q0 : q0 + OUT, cols] = l[p * OUT : (p + 1) * OUT]


def across(src_h, src_l, band, rows, t, tiles):
    a, b = [slice(n * LANES, (n + 1) * LANES) for n in (t % (tiles + 1), (t + 1) % (tiles + 1))]
    hi = [src_h[0, rows, a], src_h[0, rows, b], src_h[1, rows, a], src_h[1, rows, b]]
    lo = [src_l[0, rows, a], src_l[0, rows, b], src_l[1, rows, a], src_l[1, rows, b]]
    return jnp.dot(jnp.concatenate(hi + lo + hi, axis=1), band[...], preferred_element_type=F32)


def weave(parts, rows):
    lane = lanes_of(rows)
    out = None
    for value, src, dst in parts:
        turn = (dst - src) % LANES
        value = pltpu.roll(value, turn, 1) if turn else value
        out = value if out is None else jnp.where(lane >= dst, value, out)
    return out


def edges(a, b, width, src):
    lane = lanes_of(a.shape[0])
    turn = (LANES - width - src) % LANES
    a = pltpu.roll(a, turn, 1) if turn else a
    b = pltpu.roll(b, -src % LANES, 1) if src else b
    return jnp.where(lane < width, b, jnp.where(lane >= LANES - width, a, 0.0))


def make_kernel(H, W, tap_shape):
    tiles = W // LANES
    full = W + LANES

    def kernel(
        inc, ph, cot, prop, th, tl, pgv, wz, c0, s0, colb,
        tilel, tiler, phasel, phaser, incv, phv, cotv, packl, packr, wavel, waver, corner, cl, cr, wl, wr, met, crow, irow, prow,
        taps, line, xh, xl, zh, zl, gh, gl, uh, ul, vh, vl,
        c1, s1, gout, fout, rowf, rowa, colf, cola,
        load, send, recv,
    ):
        ty, tx = lax.axis_index("ty"), lax.axis_index("tx")
        ny, nx = lax.axis_size("ty"), lax.axis_size("tx")
        up, down = lax.rem(ty + ny - 1, ny), lax.rem(ty + 1, ny)
        left, right = lax.rem(tx + nx - 1, nx), lax.rem(tx + 1, nx)

        near_edge = ((cot, slice(0, 2), tilel), (cot, slice(0, 2), tiler), (ph, 1, phasel), (ph, 1, phaser))
        first = [
            pltpu.make_async_copy(src.at[p, :, slice(0, LANES) if k % 2 == 0 else slice(W - LANES, W)], dst, load.at[7 + k])
            for k, (src, p, dst) in enumerate(near_edge)
        ]
        for c in first:
            c.start()
        pairs = [(a.at[p], b.at[p]) for a, b, p in ((cot, cotv, 0), (cot, cotv, 1), (ph, phv, 1), (ph, phv, 0), (inc, incv, 0), (inc, incv, 1))]
        loads = [pltpu.make_async_copy(src, dst, load.at[k]) for k, (src, dst) in enumerate(pairs + [(prop, taps)])]
        for c in loads:
            c.start()
        barrier = pltpu.get_barrier_semaphore()
        others = [(up, tx), (down, tx), (ty, left), (ty, right), (up, left), (up, right), (down, left), (down, right)]
        for dev in others:
            pl.semaphore_signal(barrier, inc=1, device_id=dev, device_id_type=pl.DeviceIdType.MESH)

        sides = ((slice(0, LANES), 0), (slice(W - LANES, W), 1))
        part2, part4, part8 = H // 2, H // 4, H // 8
        for c in first:
            c.wait()
        for far, cotx, phx, dst in ((0, tilel, phasel, packl), (1, tiler, phaser, packr)):
            src = far * (LANES - WIDE)
            for r0 in range(0, part2, part4):
                dst[r0 : r0 + part4, :] = weave(
                    [(cotx[p, g * part2 + r0 : g * part2 + r0 + part4, :], src, 2 * WIDE * g + WIDE * p) for g in range(2) for p in range(2)],
                    part4,
                )
            src = far * (LANES - RIM)
            dst[part2 : part2 + part8, :] = weave(
                [(phx[g * part8 : (g + 1) * part8, :], src, RIM * g) for g in range(8)], part8
            )

        pl.semaphore_wait(barrier, 8)
        copies = []

        def push(src, dst, dev, start=True):
            k = len(copies)
            c = pltpu.make_async_remote_copy(
                src_ref=src, dst_ref=dst, send_sem=send.at[k], recv_sem=recv.at[k],
                device_id=dev, device_id_type=pl.DeviceIdType.MESH,
            )
            if start:
                c.start()
            copies.append(c)

        odd = lax.rem(tx, 2)

        def push_both(to_left, to_right):
            push(*to_left, (ty, left), start=False)
            push(*to_right, (ty, right), start=False)
            a, b = copies[-2:]

            @pl.when(odd == 0)
            def _():
                a.start()
                b.start()

            @pl.when(odd == 1)
            def _():
                b.start()
                a.start()

        push_both((packl, cr), (packr, cl))
        push(cot.at[:, 0:WIDE, :], crow.at[1], (up, tx))
        push(cot.at[:, H - WIDE : H, :], crow.at[0], (down, tx))
        push(inc.at[:, 0:RIM, :], irow.at[1], (up, tx))
        push(inc.at[:, H - RIM : H, :], irow.at[0], (down, tx))
        push(ph.at[:, 0:RIM, :], prow.at[1], (up, tx))
        push(ph.at[:, H - RIM : H, :], prow.at[0], (down, tx))

        for c in loads:
            c.wait()

        @pl.loop(0, H // 16, unroll=H // 16)
        def _(i):
            r0 = pl.multiple_of(i * 16, 16)
            r = pl.ds(r0, 16)
            q = pl.ds(pl.multiple_of(r0 + RIM, 16), 16)
            s, c = sincos(phv[0, r, :])
            s0[r, :] = s
            c0[r, :] = c
            a, b = incv[0, r, :], incv[1, r, :]
            for p, w in enumerate((a * c - b * s, a * s + b * c)):
                wz[p, r, :] = w
                hi, lo = split(w)
                zh[p, q, 0:W] = hi
                zl[p, q, 0:W] = lo

        for n, (cols, far) in enumerate(sides):
            wide, rim = far * (LANES - WIDE), far * (LANES - RIM)
            for m, r in enumerate((slice(0, WIDE), slice(H - WIDE, H))):
                corner[n, m] = weave(
                    [(cotv[0, r, cols], wide, 0), (cotv[1, r, cols], wide, WIDE), (phv[1, r, cols], rim, 2 * WIDE)]
                    + [(wz[p, r, cols], rim, 2 * WIDE + RIM * (p + 1)) for p in range(2)],
                    WIDE,
                )
        for (cols, far), dst in zip(sides, (wavel, waver)):
            src = far * (LANES - RIM)
            dst[...] = weave(
                [(wz[p, g * part4 : (g + 1) * part4, cols], src, WIDE * g + RIM * p) for g in range(4) for p in range(2)], part4
            )
        push(corner.at[0, 0], met.at[1, 1], (up, left))
        push(corner.at[0, 1], met.at[1, 0], (down, left))
        push(corner.at[1, 0], met.at[0, 1], (up, right))
        push(corner.at[1, 1], met.at[0, 0], (down, right))
        push_both((wavel, wr), (waver, wl))

        line[...] = jnp.zeros(line.shape, F32)
        line[0:2, 0 : prop.shape[1]] = taps[...]
        kr, ki = line[0:1, :], line[1:2, :]

        def rows_band(dst, mr, mi):
            top = jnp.concatenate([mr, -mi], axis=1)
            low = jnp.concatenate([mi, mr], axis=1)
            hi, lo = split(jnp.concatenate([top, low], axis=0))
            k = 2 * LANES
            dst[:, 0:k] = hi
            dst[:, k : 2 * k] = hi
            dst[:, 2 * k : 3 * k] = lo

        def cols_band(dst, tr, ti):
            top = jnp.concatenate([tr, ti], axis=1)
            low = jnp.concatenate([-ti, tr], axis=1)
            hi, lo = split(jnp.concatenate([top, low], axis=0))
            k = 4 * LANES
            dst[0:k, :] = hi
            dst[k : 2 * k, :] = hi
            dst[2 * k : 3 * k, :] = lo

        rows_band(rowf, toeplitz(kr, LANES, LANES, 0)[:OUT], toeplitz(ki, LANES, LANES, 0)[:OUT])
        rows_band(rowa, toeplitz(kr, LANES, LANES, -WIDE).T[:OUT], -toeplitz(ki, LANES, LANES, -WIDE).T[:OUT])
        cols_band(colf, toeplitz(kr, LANES, 2 * LANES, 0).T, toeplitz(ki, LANES, 2 * LANES, 0).T)
        cols_band(
            cola,
            toeplitz(kr, 2 * LANES, 2 * LANES, -WIDE)[:, :LANES],
            -toeplitz(ki, 2 * LANES, 2 * LANES, -WIDE)[:, :LANES],
        )

        cols_band(
            colb,
            toeplitz(kr, 2 * LANES, 2 * LANES, -LANES)[:, :LANES],
            -toeplitz(ki, 2 * LANES, 2 * LANES, -LANES)[:, :LANES],
        )

        def moved(ref, t, r):
            return pltpu.roll(ref[1, r, t * LANES : (t + 1) * LANES], LANES - RIM, 1)

        def phase_one(ref, r, q, rows, which):
            last = lanes_of(rows) >= LANES - RIM
            for t in which:
                s, c = sincos(jnp.where(last, moved(ref, t + 1, r), moved(ref, t, r)))
                s1[q, t * LANES : (t + 1) * LANES] = s
                c1[q, t * LANES : (t + 1) * LANES] = c

        @pl.loop(0, H // 16, unroll=H // 16)
        def _(i):
            r0 = pl.multiple_of(i * 16, 16)
            r = pl.ds(r0, 16)
            for p in range(2):
                hi, lo = split(cotv[p, r, :])
                q = pl.ds(pl.multiple_of(r0 + WIDE, 16), 16)
                xh[p, q, 0:W] = hi
                xl[p, q, 0:W] = lo
            q = pl.ds(pl.multiple_of(r0 + RIM, 16), 16)
            phase_one(phv, r, q, 16, range(tiles - 1))

        xall, zall = row_blocks(H + WIDE), row_blocks(H)
        xin = [q for q in xall if q >= WIDE and q + LANES <= WIDE + H]
        zin = [q for q in zall if q >= RIM and q + LANES <= RIM + H]
        down_pass(xh, xl, uh, ul, rowa, xin, 0, W)
        down_pass(zh, zl, vh, vl, rowf, zin, 0, W)

        for k in (2, 3, 4, 5, 6, 7):
            copies[k].wait_recv()
        for side in range(2):
            q = slice(0, WIDE) if side == 0 else slice(WIDE + H, WIDE + H + WIDE)
            for p in range(2):
                hi, lo = split(crow[side, p])
                xh[p, q, 0:W] = hi
                xl[p, q, 0:W] = lo
            q = slice(0, RIM) if side == 0 else slice(RIM + H, RIM + H + RIM)
            phase_one(prow.at[side], slice(0, RIM), q, RIM, range(tiles - 1))
            s, c = sincos(prow[side, 0])
            a, b = irow[side, 0], irow[side, 1]
            for p, w in enumerate((a * c - b * s, a * s + b * c)):
                hi, lo = split(w)
                zh[p, q, 0:W] = hi
                zl[p, q, 0:W] = lo

        def across_pass(src_h, src_l, dst, band, rows, which):
            for t in which:
                dst[t, 0:rows, :] = across(src_h, src_l, band, slice(0, rows), t, tiles)

        down_pass(xh, xl, uh, ul, rowa, [q for q in xall if q not in xin], 0, W)
        down_pass(zh, zl, vh, vl, rowf, [q for q in zall if q not in zin], 0, W)
        across_pass(uh, ul, gout, cola, H + WIDE, range(tiles - 1))
        across_pass(vh, vl, fout, colf, H, range(tiles - 1))

        estep = block(H + WIDE, 64)

        def turn_back(which):
            @pl.loop(0, (H + WIDE) // estep, unroll=(H + WIDE) // estep)
            def _(i):
                r = pl.ds(pl.multiple_of(i * estep, 16), estep)
                for t in which:
                    cols = slice(t * LANES, (t + 1) * LANES)
                    gr, gi = gout[t, r, 0:LANES], gout[t, r, LANES : 2 * LANES]
                    c, s = c1[r, cols], s1[r, cols]
                    for p, g in enumerate((gr * c + gi * s, gi * c - gr * s)):
                        gh[p, r, cols], gl[p, r, cols] = split(g)

        turn_back(range(tiles - 1))
        down_pass(gh, gl, th, tl, rowa, zall, 0, (tiles - 1) * LANES)

        for k in (0, 1, 8, 9, 10, 11):
            copies[k].wait_recv()
        edge = slice(W, full)
        for p in range(2):
            for g in range(2):
                for r0 in range(0, part2, part4):
                    r = slice(r0, r0 + part4)
                    q = slice(WIDE + g * part2 + r0, WIDE + g * part2 + r0 + part4)
                    xh[p, q, edge], xl[p, q, edge] = split(edges(cl[r, :], cr[r, :], WIDE, 2 * WIDE * g + WIDE * p))
            for m, q in enumerate((slice(0, WIDE), slice(WIDE + H, 2 * WIDE + H))):
                xh[p, q, edge], xl[p, q, edge] = split(edges(met[0, m], met[1, m], WIDE, WIDE * p))

        down_pass(xh, xl, uh, ul, rowa, xall, W, full)
        across_pass(uh, ul, gout, cola, H + WIDE, range(tiles - 1, tiles + 1))

        def phase_edge(q, a, b, src, own, own_r, rows):
            lane = lanes_of(rows)
            inner = moved(own, tiles - 1, own_r)
            x = jnp.where(lane >= LANES - RIM, pltpu.roll(b, (LANES - RIM - src) % LANES, 1), inner)
            outer = jnp.where(lane >= LANES - WIDE, pltpu.roll(a, (LANES - WIDE - src) % LANES, 1), 0.0)
            y = jnp.where(lane >= LANES - RIM, moved(own, 0, own_r), outer)
            for t, v in ((tiles - 1, x), (tiles, y)):
                s, c = sincos(v)
                s1[q, t * LANES : (t + 1) * LANES] = s
                c1[q, t * LANES : (t + 1) * LANES] = c

        for g in range(8):
            r = slice(part2, part2 + part8)
            q = slice(RIM + g * part8, RIM + (g + 1) * part8)
            phase_edge(q, cl[r, :], cr[r, :], RIM * g, phv, slice(g * part8, (g + 1) * part8), part8)
        near = (slice(RIM, WIDE), slice(0, RIM))
        rims = (slice(0, RIM), slice(RIM + H, WIDE + H))
        for m in range(2):
            phase_edge(rims[m], met[0, m, near[m]], met[1, m, near[m]], 2 * WIDE, prow.at[m], slice(0, RIM), RIM)

        turn_back(range(tiles - 1, tiles + 1))
        down_pass(gh, gl, th, tl, rowa, zall, (tiles - 1) * LANES, full)

        for k in (12, 13):
            copies[k].wait_recv()
        for p in range(2):
            for g in range(4):
                q = slice(RIM + g * part4, RIM + (g + 1) * part4)
                zh[p, q, edge], zl[p, q, edge] = split(edges(wl[...], wr[...], RIM, WIDE * g + RIM * p))
            for m in range(2):
                value = edges(met[0, m, near[m]], met[1, m, near[m]], RIM, 2 * WIDE + RIM * (p + 1))
                zh[p, rims[m], edge], zl[p, rims[m], edge] = split(value)

        down_pass(zh, zl, vh, vl, rowf, zall, W, full)
        across_pass(vh, vl, fout, colf, H, range(tiles - 1, tiles + 1))

        fstep = block(H, 32)

        @pl.loop(0, H // fstep, unroll=H // fstep)
        def _(i):
            r = pl.ds(pl.multiple_of(i * fstep, 16), fstep)
            q = pl.ds(pl.multiple_of(i * fstep + RIM, 16), fstep)
            first = lanes_of(fstep) < RIM
            before = None
            for t in [tiles] + list(range(tiles)):
                cols = slice(t * LANES, (t + 1) * LANES)
                gr, gi = gout[t, q, 0:LANES], gout[t, q, LANES : 2 * LANES]
                fr, fi = fout[t, r, 0:LANES], fout[t, r, LANES : 2 * LANES]
                c, s = c1[q, cols], s1[q, cols]
                term = pltpu.roll(gi * (fr * c - fi * s) - gr * (fr * s + fi * c), RIM, 1)
                if before is not None:
                    pgv[r, cols] = jnp.where(first, before, term)
                before = term

        for c in copies:
            c.wait_send()

    V = pltpu.VMEM
    scratch = [
        V((2, H, LANES), F32), V((2, H, LANES), F32), V((H, LANES), F32), V((H, LANES), F32),
        V((2, H, W), F32), V((2, H, W), F32), V((2, H, W), F32),
        V((H // 2 + H // 8, LANES), F32), V((H // 2 + H // 8, LANES), F32),
        V((H // 4, LANES), F32), V((H // 4, LANES), F32), V((2, 2, WIDE, LANES), F32),
        V((H // 2 + H // 8, LANES), F32), V((H // 2 + H // 8, LANES), F32),
        V((H // 4, LANES), F32), V((H // 4, LANES), F32), V((2, 2, WIDE, LANES), F32),
        V((2, 2, WIDE, W), F32), V((2, 2, RIM, W), F32), V((2, 2, RIM, W), F32),
        V(tap_shape, F32), V((8, 2 * LANES), F32),
        V((2, H + 2 * WIDE, full), BF16), V((2, H + 2 * WIDE, full), BF16),
        V((2, H + WIDE, full), BF16), V((2, H + WIDE, full), BF16),
        V((2, H + WIDE, full), BF16), V((2, H + WIDE, full), BF16),
        V((2, H + WIDE, full), BF16), V((2, H + WIDE, full), BF16),
        V((2, H, full), BF16), V((2, H, full), BF16),
        V((H + WIDE, full), F32), V((H + WIDE, full), F32),
        V((tiles + 1, H + WIDE, 2 * LANES), F32), V((tiles + 1, H, 2 * LANES), F32),
        V((2 * OUT, 6 * LANES), BF16), V((2 * OUT, 6 * LANES), BF16),
        V((12 * LANES, 2 * LANES), BF16), V((12 * LANES, 2 * LANES), BF16),
        pltpu.SemaphoreType.DMA((11,)),
        pltpu.SemaphoreType.DMA((14,)), pltpu.SemaphoreType.DMA((14,)),
    ]
    results = (
        V((2, H, full), BF16), V((2, H, full), BF16),
        V((H, W), F32), V((2, H, W), F32), V((H, W), F32), V((H, W), F32),
        V((12 * LANES, 2 * LANES), BF16),
    )
    return pl.pallas_call(
        kernel,
        out_shape=results,
        in_specs=[pl.BlockSpec(memory_space=pltpu.HBM)] * 4,
        out_specs=tuple(pl.BlockSpec(memory_space=V) for _ in results),
        scratch_shapes=scratch,
        compiler_params=pltpu.CompilerParams(
            collective_id=0, has_side_effects=True, vmem_limit_bytes=40 * 1024 * 1024
        ),
        cost_estimate=pl.CostEstimate(flops=10**10, bytes_accessed=5 * 10**6, transcendentals=0),
    )


def make_last(H, W):
    tiles = W // LANES
    step = block(H, 160)

    def kernel(th, tl, pgv, wz, c0, s0, colb, pg, pb, term, probe, store):
        copies = []

        def put(src, dst):
            c = pltpu.make_async_copy(src, dst, store.at[len(copies)])
            c.start()
            copies.append(c)

        put(pgv, pg.at[1])
        for r0 in range(0, H, step):
            r = slice(r0, r0 + step)
            for t in range(tiles):
                cols = slice(t * LANES, (t + 1) * LANES)
                g = across(th, tl, colb, r, t - 1, tiles)
                gr, gi = g[:, 0:LANES], g[:, LANES : 2 * LANES]
                c, s = c0[r, cols], s0[r, cols]
                term[r, cols] = gi * wz[0, r, cols] - gr * wz[1, r, cols]
                probe[0, r, cols] = gr * c + gi * s
                probe[1, r, cols] = gi * c - gr * s
            put(term.at[r], pg.at[0, r])
            put(probe.at[:, r], pb.at[:, r])
        for c in copies:
            c.wait()

    V = pltpu.VMEM
    out = jax.ShapeDtypeStruct((2, H, W), F32)
    return pl.pallas_call(
        kernel,
        out_shape=(out, out),
        in_specs=[pl.BlockSpec(memory_space=V)] * 7,
        out_specs=(pl.BlockSpec(memory_space=pltpu.HBM),) * 2,
        scratch_shapes=[
            V((H, W), F32), V((2, H, W), F32),
            pltpu.SemaphoreType.DMA((1 + 2 * (H // step),)),
        ],
        compiler_params=pltpu.CompilerParams(vmem_limit_bytes=32 * 1024 * 1024),
        cost_estimate=pl.CostEstimate(flops=10**10, bytes_accessed=5 * 10**6, transcendentals=0),
    )


def on_device(incident, phases, cotangent, propagator):
    H, W = incident.shape[1], incident.shape[2]
    operands = [pltpu.with_memory_space_constraint(x, pltpu.HBM) for x in (incident, phases, cotangent, propagator)]
    return make_last(H, W)(*make_kernel(H, W, propagator.shape)(*operands))


def solution(mesh):
    placed = (P(None, "ty", "tx"), P(None, "ty", "tx"), P(None, "ty", "tx"), P())
    return jax.shard_map(
        on_device,
        mesh=mesh,
        in_specs=placed,
        out_specs=(P(None, "ty", "tx"), P(None, "ty", "tx")),
        check_vma=False,
    )
```

```python
import jax
import jax.numpy as jnp
from jax import lax
from jax.experimental import pallas as pl
from jax.experimental.pallas import tpu as pltpu
from jax.sharding import PartitionSpec as P

RIM = 16
WIDE = 2 * RIM
LANES = 128
OUT = LANES - WIDE
F32 = jnp.float32
BF16 = jnp.bfloat16


def block(rows, most):
    return max(n for n in range(16, most + 1, 16) if rows % n == 0)


def sincos(angle):
    half = angle * 0.5
    sq = half * half
    s = -1.0 / 39916800.0
    for c in (1.0 / 362880.0, -1.0 / 5040.0, 1.0 / 120.0, -1.0 / 6.0):
        s = s * sq + c
    s = half + half * sq * s
    c = 1.0 / 479001600.0
    for k in (-1.0 / 3628800.0, 1.0 / 40320.0, -1.0 / 720.0, 1.0 / 24.0, -0.5, 1.0):
        c = c * sq + k
    return 2.0 * s * c, 1.0 - 2.0 * s * s


def split(x):
    hi = x.astype(BF16)
    return hi, (x - hi.astype(F32)).astype(BF16)


def lanes_of(rows, width=LANES):
    return lax.broadcasted_iota(jnp.int32, (rows, width), 1)


def toeplitz(line, rows, width, shift):
    wide = jnp.broadcast_to(line[:, :width], (rows, width))
    return pltpu.roll(wide, shift % width, 1, stride=1, stride_axis=0)


def row_blocks(rows):
    return list(range(0, rows - OUT, OUT)) + [rows - OUT]


def down_pass(src_h, src_l, dst_h, dst_l, band, starts, lo_lane, hi_lane):
    cols = slice(lo_lane, hi_lane)
    for q0 in starts:
        win = slice(q0, q0 + LANES)
        hi = [src_h[0, win, cols], src_h[1, win, cols]]
        lo = [src_l[0, win, cols], src_l[1, win, cols]]
        operand = jnp.concatenate(hi + lo + hi, axis=0)
        u = jnp.dot(band[...], operand, preferred_element_type=F32)
        h, l = split(u)
        for p in range(2):
            dst_h[p, q0 : q0 + OUT, cols] = h[p * OUT : (p + 1) * OUT]
            dst_l[p, q0 : q0 + OUT, cols] = l[p * OUT : (p + 1) * OUT]


def across(src_h, src_l, band, rows, t, tiles):
    a, b = [slice(n * LANES, (n + 1) * LANES) for n in (t % (tiles + 1), (t + 1) % (tiles + 1))]
    hi = [src_h[0, rows, a], src_h[0, rows, b], src_h[1, rows, a], src_h[1, rows, b]]
    lo = [src_l[0, rows, a], src_l[0, rows, b], src_l[1, rows, a], src_l[1, rows, b]]
    return jnp.dot(jnp.concatenate(hi + lo + hi, axis=1), band[...], preferred_element_type=F32)


def weave(parts, rows):
    lane = lanes_of(rows)
    out = None
    for value, src, dst in parts:
        turn = (dst - src) % LANES
        value = pltpu.roll(value, turn, 1) if turn else value
        out = value if out is None else jnp.where(lane >= dst, value, out)
    return out


def edges(a, b, width, src):
    lane = lanes_of(a.shape[0])
    turn = (LANES - width - src) % LANES
    a = pltpu.roll(a, turn, 1) if turn else a
    b = pltpu.roll(b, -src % LANES, 1) if src else b
    return jnp.where(lane < width, b, jnp.where(lane >= LANES - width, a, 0.0))


def make_kernel(H, W, tap_shape):
    tiles = W // LANES
    full = W + LANES

    def kernel(
        inc, ph, cot, prop, gz, pgv, wz, c0, s0,
        tilel, tiler, phasel, phaser, incv, phv, cotv, packl, packr, wavel, waver, cornc, corns, cl, cr, wl, wr, metc, mets, crow, irow, prow,
        taps, line, xh, xl, zh, zl, gh, gl, uh, ul, vh, vl, th, tl,
        c1, s1, gout, fout, rowf, rowa, colf, cola, colb,
        load, send, recv,
    ):
        ty, tx = lax.axis_index("ty"), lax.axis_index("tx")
        ny, nx = lax.axis_size("ty"), lax.axis_size("tx")
        up, down = lax.rem(ty + ny - 1, ny), lax.rem(ty + 1, ny)
        left, right = lax.rem(tx + nx - 1, nx), lax.rem(tx + 1, nx)

        near_edge = ((cot, slice(0, 2), tilel), (cot, slice(0, 2), tiler), (ph, 1, phasel), (ph, 1, phaser))
        first = [
            pltpu.make_async_copy(src.at[p, :, slice(0, LANES) if k % 2 == 0 else slice(W - LANES, W)], dst, load.at[7 + k])
            for k, (src, p, dst) in enumerate(near_edge)
        ]
        for c in first:
            c.start()
        pairs = [(a.at[p], b.at[p]) for a, b, p in ((cot, cotv, 0), (cot, cotv, 1), (ph, phv, 1), (ph, phv, 0), (inc, incv, 0), (inc, incv, 1))]
        loads = [pltpu.make_async_copy(src, dst, load.at[k]) for k, (src, dst) in enumerate(pairs + [(prop, taps)])]
        for c in loads:
            c.start()
        barrier = pltpu.get_barrier_semaphore()
        others = [(up, tx), (down, tx), (ty, left), (ty, right), (up, left), (up, right), (down, left), (down, right)]
        for dev in others:
            pl.semaphore_signal(barrier, inc=1, device_id=dev, device_id_type=pl.DeviceIdType.MESH)

        sides = ((slice(0, LANES), 0), (slice(W - LANES, W), 1))
        part2, part4, part8 = H // 2, H // 4, H // 8
        for c in first:
            c.wait()
        for far, cotx, phx, dst in ((0, tilel, phasel, packl), (1, tiler, phaser, packr)):
            src = far * (LANES - WIDE)
            for r0 in range(0, part2, part4):
                dst[r0 : r0 + part4, :] = weave(
                    [(cotx[p, g * part2 + r0 : g * part2 + r0 + part4, :], src, 2 * WIDE * g + WIDE * p) for g in range(2) for p in range(2)],
                    part4,
                )
            src = far * (LANES - RIM)
            dst[part2 : part2 + part8, :] = weave(
                [(phx[g * part8 : (g + 1) * part8, :], src, RIM * g) for g in range(8)], part8
            )

            for m, r0 in enumerate((0, H - WIDE)):
                cornc[far, m] = weave(
                    [(cotx[p, r0 + RIM * g : r0 + RIM * (g + 1), :], far * (LANES - WIDE), 2 * WIDE * g + WIDE * p) for g in range(2) for p in range(2)],
                    RIM,
                )

        pl.semaphore_wait(barrier, 8)
        copies = []

        def push(src, dst, dev, start=True):
            k = len(copies)
            c = pltpu.make_async_remote_copy(
                src_ref=src, dst_ref=dst, send_sem=send.at[k], recv_sem=recv.at[k],
                device_id=dev, device_id_type=pl.DeviceIdType.MESH,
            )
            if start:
                c.start()
            copies.append(c)

        odd = lax.rem(tx, 2)

        def push_both(to_left, to_right):
            push(*to_left, (ty, left), start=False)
            push(*to_right, (ty, right), start=False)
            a, b = copies[-2:]

            @pl.when(odd == 0)
            def _():
                a.start()
                b.start()

            @pl.when(odd == 1)
            def _():
                b.start()
                a.start()

        def push_corners(src, dst):
            push(src.at[0, 0], dst.at[1, 1], (up, left))
            push(src.at[0, 1], dst.at[1, 0], (down, left))
            push(src.at[1, 0], dst.at[0, 1], (up, right))
            push(src.at[1, 1], dst.at[0, 0], (down, right))

        push_both((packl, cr), (packr, cl))
        push(cot.at[:, 0:WIDE, :], crow.at[1], (up, tx))
        push(cot.at[:, H - WIDE : H, :], crow.at[0], (down, tx))
        push(inc.at[:, 0:RIM, :], irow.at[1], (up, tx))
        push(inc.at[:, H - RIM : H, :], irow.at[0], (down, tx))
        push(ph.at[:, 0:RIM, :], prow.at[1], (up, tx))
        push(ph.at[:, H - RIM : H, :], prow.at[0], (down, tx))
        push_corners(cornc, metc)

        for c in loads:
            c.wait()

        @pl.loop(0, H // 16, unroll=H // 16)
        def _(i):
            r0 = pl.multiple_of(i * 16, 16)
            r = pl.ds(r0, 16)
            q = pl.ds(pl.multiple_of(r0 + RIM, 16), 16)
            s, c = sincos(phv[0, r, :])
            s0[r, :] = s
            c0[r, :] = c
            a, b = incv[0, r, :], incv[1, r, :]
            for p, w in enumerate((a * c - b * s, a * s + b * c)):
                wz[p, r, :] = w
                hi, lo = split(w)
                zh[p, q, 0:W] = hi
                zl[p, q, 0:W] = lo

        for cols, far in sides:
            rim = far * (LANES - RIM)
            for m, r0 in enumerate((0, H - RIM)):
                halves = [slice(r0 + 8 * g, r0 + 8 * (g + 1)) for g in range(2)]
                corns[far, m] = weave(
                    [(phv[1, r, cols], rim, RIM * g) for g, r in enumerate(halves)]
                    + [(wz[p, r, cols], rim, WIDE + WIDE * g + RIM * p) for g, r in enumerate(halves) for p in range(2)],
                    8,
                )
        for (cols, far), dst in zip(sides, (wavel, waver)):
            src = far * (LANES - RIM)
            dst[...] = weave(
                [(wz[p, g * part4 : (g + 1) * part4, cols], src, WIDE * g + RIM * p) for g in range(4) for p in range(2)], part4
            )
        push_corners(corns, mets)
        push_both((wavel, wr), (waver, wl))

        line[...] = jnp.zeros(line.shape, F32)
        line[0:2, 0 : prop.shape[1]] = taps[...]
        kr, ki = line[0:1, :], line[1:2, :]

        def rows_band(dst, mr, mi):
            top = jnp.concatenate([mr, -mi], axis=1)
            low = jnp.concatenate([mi, mr], axis=1)
            hi, lo = split(jnp.concatenate([top, low], axis=0))
            k = 2 * LANES
            dst[:, 0:k] = hi
            dst[:, k : 2 * k] = hi
            dst[:, 2 * k : 3 * k] = lo

        def cols_band(dst, tr, ti):
            top = jnp.concatenate([tr, ti], axis=1)
            low = jnp.concatenate([-ti, tr], axis=1)
            hi, lo = split(jnp.concatenate([top, low], axis=0))
            k = 4 * LANES
            dst[0:k, :] = hi
            dst[k : 2 * k, :] = hi
            dst[2 * k : 3 * k, :] = lo

        rows_band(rowf, toeplitz(kr, LANES, LANES, 0)[:OUT], toeplitz(ki, LANES, LANES, 0)[:OUT])
        rows_band(rowa, toeplitz(kr, LANES, LANES, -WIDE).T[:OUT], -toeplitz(ki, LANES, LANES, -WIDE).T[:OUT])
        cols_band(colf, toeplitz(kr, LANES, 2 * LANES, 0).T, toeplitz(ki, LANES, 2 * LANES, 0).T)
        cols_band(
            cola,
            toeplitz(kr, 2 * LANES, 2 * LANES, -WIDE)[:, :LANES],
            -toeplitz(ki, 2 * LANES, 2 * LANES, -WIDE)[:, :LANES],
        )

        cols_band(
            colb,
            toeplitz(kr, 2 * LANES, 2 * LANES, -LANES)[:, :LANES],
            -toeplitz(ki, 2 * LANES, 2 * LANES, -LANES)[:, :LANES],
        )

        def moved(ref, t, r):
            return pltpu.roll(ref[1, r, t * LANES : (t + 1) * LANES], LANES - RIM, 1)

        def phase_one(ref, r, q, rows, which):
            last = lanes_of(rows) >= LANES - RIM
            for t in which:
                s, c = sincos(jnp.where(last, moved(ref, t + 1, r), moved(ref, t, r)))
                s1[q, t * LANES : (t + 1) * LANES] = s
                c1[q, t * LANES : (t + 1) * LANES] = c

        @pl.loop(0, H // 16, unroll=H // 16)
        def _(i):
            r0 = pl.multiple_of(i * 16, 16)
            r = pl.ds(r0, 16)
            for p in range(2):
                hi, lo = split(cotv[p, r, :])
                q = pl.ds(pl.multiple_of(r0 + WIDE, 16), 16)
                xh[p, q, 0:W] = hi
                xl[p, q, 0:W] = lo
            q = pl.ds(pl.multiple_of(r0 + RIM, 16), 16)
            phase_one(phv, r, q, 16, range(tiles - 1))

        xall, zall = row_blocks(H + WIDE), row_blocks(H)
        xin = [q for q in xall if q >= WIDE and q + LANES <= WIDE + H]
        zin = [q for q in zall if q >= RIM and q + LANES <= RIM + H]
        down_pass(xh, xl, uh, ul, rowa, xin, 0, W)
        down_pass(zh, zl, vh, vl, rowf, zin, 0, W)

        for k in (2, 3, 4, 5, 6, 7):
            copies[k].wait_recv()
        for side in range(2):
            q = slice(0, WIDE) if side == 0 else slice(WIDE + H, WIDE + H + WIDE)
            for p in range(2):
                hi, lo = split(crow[side, p])
                xh[p, q, 0:W] = hi
                xl[p, q, 0:W] = lo
            q = slice(0, RIM) if side == 0 else slice(RIM + H, RIM + H + RIM)
            phase_one(prow.at[side], slice(0, RIM), q, RIM, range(tiles - 1))
            s, c = sincos(prow[side, 0])
            a, b = irow[side, 0], irow[side, 1]
            for p, w in enumerate((a * c - b * s, a * s + b * c)):
                hi, lo = split(w)
                zh[p, q, 0:W] = hi
                zl[p, q, 0:W] = lo

        def across_pass(src_h, src_l, dst, band, rows, which):
            for t in which:
                dst[t, 0:rows, :] = across(src_h, src_l, band, slice(0, rows), t, tiles)

        down_pass(xh, xl, uh, ul, rowa, [q for q in xall if q not in xin], 0, W)
        down_pass(zh, zl, vh, vl, rowf, [q for q in zall if q not in zin], 0, W)
        across_pass(uh, ul, gout, cola, H + WIDE, range(tiles - 1))
        across_pass(vh, vl, fout, colf, H, range(tiles - 1))

        estep = block(H + WIDE, 64)

        def turn_back(which):
            @pl.loop(0, (H + WIDE) // estep, unroll=(H + WIDE) // estep)
            def _(i):
                r = pl.ds(pl.multiple_of(i * estep, 16), estep)
                for t in which:
                    cols = slice(t * LANES, (t + 1) * LANES)
                    gr, gi = gout[t, r, 0:LANES], gout[t, r, LANES : 2 * LANES]
                    c, s = c1[r, cols], s1[r, cols]
                    for p, g in enumerate((gr * c + gi * s, gi * c - gr * s)):
                        gh[p, r, cols], gl[p, r, cols] = split(g)

        turn_back(range(tiles - 1))
        down_pass(gh, gl, th, tl, rowa, zall, 0, (tiles - 1) * LANES)

        for k in (0, 1, 8, 9, 10, 11):
            copies[k].wait_recv()
        edge = slice(W, full)
        for p in range(2):
            for g in range(2):
                for r0 in range(0, part2, part4):
                    r = slice(r0, r0 + part4)
                    q = slice(WIDE + g * part2 + r0, WIDE + g * part2 + r0 + part4)
                    xh[p, q, edge], xl[p, q, edge] = split(edges(cl[r, :], cr[r, :], WIDE, 2 * WIDE * g + WIDE * p))
            for m, e in enumerate((0, WIDE + H)):
                for g in range(2):
                    q = slice(e + RIM * g, e + RIM * (g + 1))
                    xh[p, q, edge], xl[p, q, edge] = split(edges(metc[0, m], metc[1, m], WIDE, 2 * WIDE * g + WIDE * p))

        down_pass(xh, xl, uh, ul, rowa, xall, W, full)
        across_pass(uh, ul, gout, cola, H + WIDE, range(tiles - 1, tiles + 1))

        def phase_edge(q, a, b, src, own, own_r, rows):
            lane = lanes_of(rows)
            inner = moved(own, tiles - 1, own_r)
            x = jnp.where(lane >= LANES - RIM, pltpu.roll(b, (LANES - RIM - src) % LANES, 1), inner)
            outer = jnp.where(lane >= LANES - WIDE, pltpu.roll(a, (LANES - WIDE - src) % LANES, 1), 0.0)
            y = jnp.where(lane >= LANES - RIM, moved(own, 0, own_r), outer)
            for t, v in ((tiles - 1, x), (tiles, y)):
                s, c = sincos(v)
                s1[q, t * LANES : (t + 1) * LANES] = s
                c1[q, t * LANES : (t + 1) * LANES] = c

        for g in range(8):
            r = slice(part2, part2 + part8)
            q = slice(RIM + g * part8, RIM + (g + 1) * part8)
            phase_edge(q, cl[r, :], cr[r, :], RIM * g, phv, slice(g * part8, (g + 1) * part8), part8)
        for c in copies[12:16]:
            c.wait_recv()
        rims = (slice(0, RIM), slice(RIM + H, WIDE + H))
        for m in range(2):
            for g in range(2):
                q = slice(rims[m].start + 8 * g, rims[m].start + 8 * (g + 1))
                phase_edge(q, mets[0, m], mets[1, m], RIM * g, prow.at[m], slice(8 * g, 8 * (g + 1)), 8)
        turn_back(range(tiles - 1, tiles + 1))
        down_pass(gh, gl, th, tl, rowa, zall, (tiles - 1) * LANES, full)

        for t in range(tiles):
            gz[t] = across(th, tl, colb, slice(0, H), t - 1, tiles)

        for c in copies[16:18]:
            c.wait_recv()
        for p in range(2):
            for g in range(4):
                q = slice(RIM + g * part4, RIM + (g + 1) * part4)
                zh[p, q, edge], zl[p, q, edge] = split(edges(wl[...], wr[...], RIM, WIDE * g + RIM * p))
            for m in range(2):
                value = [edges(mets[0, m], mets[1, m], RIM, WIDE + WIDE * g + RIM * p) for g in range(2)]
                zh[p, rims[m], edge], zl[p, rims[m], edge] = split(jnp.concatenate(value, axis=0))

        down_pass(zh, zl, vh, vl, rowf, zall, W, full)
        across_pass(vh, vl, fout, colf, H, range(tiles - 1, tiles + 1))

        fstep = block(H, 32)

        @pl.loop(0, H // fstep, unroll=H // fstep)
        def _(i):
            r = pl.ds(pl.multiple_of(i * fstep, 16), fstep)
            q = pl.ds(pl.multiple_of(i * fstep + RIM, 16), fstep)
            first = lanes_of(fstep) < RIM
            before = None
            for t in [tiles] + list(range(tiles)):
                cols = slice(t * LANES, (t + 1) * LANES)
                gr, gi = gout[t, q, 0:LANES], gout[t, q, LANES : 2 * LANES]
                fr, fi = fout[t, r, 0:LANES], fout[t, r, LANES : 2 * LANES]
                c, s = c1[q, cols], s1[q, cols]
                term = pltpu.roll(gi * (fr * c - fi * s) - gr * (fr * s + fi * c), RIM, 1)
                if before is not None:
                    pgv[r, cols] = jnp.where(first, before, term)
                before = term

        for c in copies:
            c.wait_send()

    V = pltpu.VMEM
    scratch = [
        V((2, H, LANES), F32), V((2, H, LANES), F32), V((H, LANES), F32), V((H, LANES), F32),
        V((2, H, W), F32), V((2, H, W), F32), V((2, H, W), F32),
        V((H // 2 + H // 8, LANES), F32), V((H // 2 + H // 8, LANES), F32),
        V((H // 4, LANES), F32), V((H // 4, LANES), F32), V((2, 2, RIM, LANES), F32), V((2, 2, 8, LANES), F32),
        V((H // 2 + H // 8, LANES), F32), V((H // 2 + H // 8, LANES), F32),
        V((H // 4, LANES), F32), V((H // 4, LANES), F32), V((2, 2, RIM, LANES), F32), V((2, 2, 8, LANES), F32),
        V((2, 2, WIDE, W), F32), V((2, 2, RIM, W), F32), V((2, 2, RIM, W), F32),
        V(tap_shape, F32), V((8, 2 * LANES), F32),
        V((2, H + 2 * WIDE, full), BF16), V((2, H + 2 * WIDE, full), BF16),
        V((2, H + WIDE, full), BF16), V((2, H + WIDE, full), BF16),
        V((2, H + WIDE, full), BF16), V((2, H + WIDE, full), BF16),
        V((2, H + WIDE, full), BF16), V((2, H + WIDE, full), BF16),
        V((2, H, full), BF16), V((2, H, full), BF16),
        V((2, H, full), BF16), V((2, H, full), BF16),
        V((H + WIDE, full), F32), V((H + WIDE, full), F32),
        V((tiles + 1, H + WIDE, 2 * LANES), F32), V((tiles + 1, H, 2 * LANES), F32),
        V((2 * OUT, 6 * LANES), BF16), V((2 * OUT, 6 * LANES), BF16),
        V((12 * LANES, 2 * LANES), BF16), V((12 * LANES, 2 * LANES), BF16), V((12 * LANES, 2 * LANES), BF16),
        pltpu.SemaphoreType.DMA((11,)),
        pltpu.SemaphoreType.DMA((18,)), pltpu.SemaphoreType.DMA((18,)),
    ]
    results = (
        V((tiles, H, 2 * LANES), F32),
        V((H, W), F32), V((2, H, W), F32), V((H, W), F32), V((H, W), F32),
    )
    return pl.pallas_call(
        kernel,
        out_shape=results,
        in_specs=[pl.BlockSpec(memory_space=pltpu.HBM)] * 4,
        out_specs=tuple(pl.BlockSpec(memory_space=V) for _ in results),
        scratch_shapes=scratch,
        compiler_params=pltpu.CompilerParams(
            collective_id=0, has_side_effects=True, vmem_limit_bytes=40 * 1024 * 1024
        ),
        cost_estimate=pl.CostEstimate(flops=10**10, bytes_accessed=5 * 10**6, transcendentals=0),
    )


def make_last(H, W):
    tiles = W // LANES
    step = block(H, 80)

    def kernel(gz, pgv, wz, c0, s0, pg, pb, term, probe, store):
        copies = []

        def put(src, dst):
            c = pltpu.make_async_copy(src, dst, store.at[len(copies)])
            c.start()
            copies.append(c)

        put(pgv, pg.at[1])
        for r0 in range(0, H, step):
            r = slice(r0, r0 + step)
            for t in range(tiles):
                cols = slice(t * LANES, (t + 1) * LANES)
                gr, gi = gz[t, r, 0:LANES], gz[t, r, LANES : 2 * LANES]
                c, s = c0[r, cols], s0[r, cols]
                term[r, cols] = gi * wz[0, r, cols] - gr * wz[1, r, cols]
                probe[0, r, cols] = gr * c + gi * s
                probe[1, r, cols] = gi * c - gr * s
            put(term.at[r], pg.at[0, r])
            put(probe.at[:, r], pb.at[:, r])
        for c in copies:
            c.wait()

    V = pltpu.VMEM
    out = jax.ShapeDtypeStruct((2, H, W), F32)
    return pl.pallas_call(
        kernel,
        out_shape=(out, out),
        in_specs=[pl.BlockSpec(memory_space=V)] * 5,
        out_specs=(pl.BlockSpec(memory_space=pltpu.HBM),) * 2,
        scratch_shapes=[
            V((H, W), F32), V((2, H, W), F32),
            pltpu.SemaphoreType.DMA((1 + 2 * (H // step),)),
        ],
        compiler_params=pltpu.CompilerParams(vmem_limit_bytes=32 * 1024 * 1024),
        cost_estimate=pl.CostEstimate(flops=10**10, bytes_accessed=5 * 10**6, transcendentals=0),
    )


def on_device(incident, phases, cotangent, propagator):
    H, W = incident.shape[1], incident.shape[2]
    operands = [pltpu.with_memory_space_constraint(x, pltpu.HBM) for x in (incident, phases, cotangent, propagator)]
    return make_last(H, W)(*make_kernel(H, W, propagator.shape)(*operands))


def solution(mesh):
    placed = (P(None, "ty", "tx"), P(None, "ty", "tx"), P(None, "ty", "tx"), P())
    return jax.shard_map(
        on_device,
        mesh=mesh,
        in_specs=placed,
        out_specs=(P(None, "ty", "tx"), P(None, "ty", "tx")),
        check_vma=False,
    )
```

```python
import jax
import jax.numpy as jnp
from jax import lax
from jax.experimental import pallas as pl
from jax.experimental.pallas import tpu as pltpu
from jax.sharding import PartitionSpec as P

RIM = 16
WIDE = 2 * RIM
LANES = 128
OUT = LANES - WIDE
F32 = jnp.float32
BF16 = jnp.bfloat16


def block(rows, most):
    return max(n for n in range(16, most + 1, 16) if rows % n == 0)


def sincos(angle):
    half = angle * 0.5
    sq = half * half
    s = -1.0 / 39916800.0
    for c in (1.0 / 362880.0, -1.0 / 5040.0, 1.0 / 120.0, -1.0 / 6.0):
        s = s * sq + c
    s = half + half * sq * s
    c = 1.0 / 479001600.0
    for k in (-1.0 / 3628800.0, 1.0 / 40320.0, -1.0 / 720.0, 1.0 / 24.0, -0.5, 1.0):
        c = c * sq + k
    return 2.0 * s * c, 1.0 - 2.0 * s * s


def split(x):
    hi = x.astype(BF16)
    return hi, (x - hi.astype(F32)).astype(BF16)


def lanes_of(rows, width=LANES):
    return lax.broadcasted_iota(jnp.int32, (rows, width), 1)


def toeplitz(line, rows, width, shift):
    wide = jnp.broadcast_to(line[:, :width], (rows, width))
    return pltpu.roll(wide, shift % width, 1, stride=1, stride_axis=0)


def row_blocks(rows):
    return list(range(0, rows - OUT, OUT)) + [rows - OUT]


def down_pass(src_h, src_l, dst_h, dst_l, band, starts, lo_lane, hi_lane):
    cols = slice(lo_lane, hi_lane)
    for q0 in starts:
        win = slice(q0, q0 + LANES)
        hi = [src_h[0, win, cols], src_h[1, win, cols]]
        lo = [src_l[0, win, cols], src_l[1, win, cols]]
        operand = jnp.concatenate(hi + lo + hi, axis=0)
        u = jnp.dot(band[...], operand, preferred_element_type=F32)
        h, l = split(u)
        for p in range(2):
            dst_h[p, q0 : q0 + OUT, cols] = h[p * OUT : (p + 1) * OUT]
            dst_l[p, q0 : q0 + OUT, cols] = l[p * OUT : (p + 1) * OUT]


def across(src_h, src_l, band, rows, t, tiles):
    a, b = [slice(n * LANES, (n + 1) * LANES) for n in (t % (tiles + 1), (t + 1) % (tiles + 1))]
    hi = [src_h[0, rows, a], src_h[0, rows, b], src_h[1, rows, a], src_h[1, rows, b]]
    lo = [src_l[0, rows, a], src_l[0, rows, b], src_l[1, rows, a], src_l[1, rows, b]]
    return jnp.dot(jnp.concatenate(hi + lo + hi, axis=1), band[...], preferred_element_type=F32)


def weave(parts, rows):
    lane = lanes_of(rows)
    out = None
    for value, src, dst in parts:
        turn = (dst - src) % LANES
        value = pltpu.roll(value, turn, 1) if turn else value
        out = value if out is None else jnp.where(lane >= dst, value, out)
    return out


def edges(a, b, width, src):
    lane = lanes_of(a.shape[0])
    turn = (LANES - width - src) % LANES
    a = pltpu.roll(a, turn, 1) if turn else a
    b = pltpu.roll(b, -src % LANES, 1) if src else b
    return jnp.where(lane < width, b, jnp.where(lane >= LANES - width, a, 0.0))


def make_kernel(H, W, tap_shape):
    tiles = W // LANES
    full = W + LANES

    def kernel(
        inc, ph, cot, prop, th, tl, pgv, wz, c0, s0, colb,
        tilel, tiler, phasel, phaser, incv, phv, cotv, packl, packr, wavel, waver, corner, cl, cr, wl, wr, met, crow, irow, prow,
        taps, line, xh, xl, zh, zl, gh, gl, uh, ul, vh, vl,
        c1, s1, gout, fout, rowf, rowa, colf, cola,
        load, send, recv,
    ):
        ty, tx = lax.axis_index("ty"), lax.axis_index("tx")
        ny, nx = lax.axis_size("ty"), lax.axis_size("tx")
        up, down = lax.rem(ty + ny - 1, ny), lax.rem(ty + 1, ny)
        left, right = lax.rem(tx + nx - 1, nx), lax.rem(tx + 1, nx)

        near_edge = ((cot, slice(0, 2), tilel), (cot, slice(0, 2), tiler), (ph, 1, phasel), (ph, 1, phaser))
        first = [
            pltpu.make_async_copy(src.at[p, :, slice(0, LANES) if k % 2 == 0 else slice(W - LANES, W)], dst, load.at[7 + k])
            for k, (src, p, dst) in enumerate(near_edge)
        ]
        for c in first:
            c.start()
        pairs = [(a.at[p], b.at[p]) for a, b, p in ((cot, cotv, 0), (cot, cotv, 1), (ph, phv, 1), (ph, phv, 0), (inc, incv, 0), (inc, incv, 1))]
        loads = [pltpu.make_async_copy(src, dst, load.at[k]) for k, (src, dst) in enumerate(pairs + [(prop, taps)])]
        for c in loads:
            c.start()
        barrier = pltpu.get_barrier_semaphore()
        others = [(up, tx), (down, tx), (ty, left), (ty, right), (up, left), (up, right), (down, left), (down, right)]
        for dev in others:
            pl.semaphore_signal(barrier, inc=1, device_id=dev, device_id_type=pl.DeviceIdType.MESH)

        pl.semaphore_wait(barrier, 8)
        copies = []

        def push(src, dst, dev, start=True):
            k = len(copies)
            c = pltpu.make_async_remote_copy(
                src_ref=src, dst_ref=dst, send_sem=send.at[k], recv_sem=recv.at[k],
                device_id=dev, device_id_type=pl.DeviceIdType.MESH,
            )
            if start:
                c.start()
            copies.append(c)

        odd = lax.rem(tx, 2)

        def push_both(to_left, to_right):
            push(*to_left, (ty, left), start=False)
            push(*to_right, (ty, right), start=False)
            a, b = copies[-2:]

            @pl.when(odd == 0)
            def _():
                a.start()
                b.start()

            @pl.when(odd == 1)
            def _():
                b.start()
                a.start()

        push(cot.at[:, 0:WIDE, :], crow.at[1], (up, tx))
        push(cot.at[:, H - WIDE : H, :], crow.at[0], (down, tx))
        push(inc.at[:, 0:RIM, :], irow.at[1], (up, tx))
        push(inc.at[:, H - RIM : H, :], irow.at[0], (down, tx))
        push(ph.at[:, 0:RIM, :], prow.at[1], (up, tx))
        push(ph.at[:, H - RIM : H, :], prow.at[0], (down, tx))

        sides = ((slice(0, LANES), 0), (slice(W - LANES, W), 1))
        part2, part4, part8 = H // 2, H // 4, H // 8
        for c in first:
            c.wait()
        for far, cotx, phx, dst in ((0, tilel, phasel, packl), (1, tiler, phaser, packr)):
            src = far * (LANES - WIDE)
            for r0 in range(0, part2, part4):
                dst[r0 : r0 + part4, :] = weave(
                    [(cotx[p, g * part2 + r0 : g * part2 + r0 + part4, :], src, 2 * WIDE * g + WIDE * p) for g in range(2) for p in range(2)],
                    part4,
                )
            src = far * (LANES - RIM)
            dst[part2 : part2 + part8, :] = weave(
                [(phx[g * part8 : (g + 1) * part8, :], src, RIM * g) for g in range(8)], part8
            )
        push_both((packl, cr), (packr, cl))

        for c in loads:
            c.wait()

        @pl.loop(0, H // 16, unroll=H // 16)
        def _(i):
            r0 = pl.multiple_of(i * 16, 16)
            r = pl.ds(r0, 16)
            q = pl.ds(pl.multiple_of(r0 + RIM, 16), 16)
            s, c = sincos(phv[0, r, :])
            s0[r, :] = s
            c0[r, :] = c
            a, b = incv[0, r, :], incv[1, r, :]
            for p, w in enumerate((a * c - b * s, a * s + b * c)):
                wz[p, r, :] = w
                hi, lo = split(w)
                zh[p, q, 0:W] = hi
                zl[p, q, 0:W] = lo

        for n, (cols, far) in enumerate(sides):
            wide, rim = far * (LANES - WIDE), far * (LANES - RIM)
            for m, r in enumerate((slice(0, WIDE), slice(H - WIDE, H))):
                corner[n, m] = weave(
                    [(cotv[0, r, cols], wide, 0), (cotv[1, r, cols], wide, WIDE), (phv[1, r, cols], rim, 2 * WIDE)]
                    + [(wz[p, r, cols], rim, 2 * WIDE + RIM * (p + 1)) for p in range(2)],
                    WIDE,
                )
        for (cols, far), dst in zip(sides, (wavel, waver)):
            src = far * (LANES - RIM)
            dst[...] = weave(
                [(wz[p, g * part4 : (g + 1) * part4, cols], src, WIDE * g + RIM * p) for g in range(4) for p in range(2)], part4
            )
        push(corner.at[0, 0], met.at[1, 1], (up, left))
        push(corner.at[0, 1], met.at[1, 0], (down, left))
        push(corner.at[1, 0], met.at[0, 1], (up, right))
        push(corner.at[1, 1], met.at[0, 0], (down, right))
        push_both((wavel, wr), (waver, wl))

        line[...] = jnp.zeros(line.shape, F32)
        line[0:2, 0 : prop.shape[1]] = taps[...]
        kr, ki = line[0:1, :], line[1:2, :]

        def rows_band(dst, mr, mi):
            top = jnp.concatenate([mr, -mi], axis=1)
            low = jnp.concatenate([mi, mr], axis=1)
            hi, lo = split(jnp.concatenate([top, low], axis=0))
            k = 2 * LANES
            dst[:, 0:k] = hi
            dst[:, k : 2 * k] = hi
            dst[:, 2 * k : 3 * k] = lo

        def cols_band(dst, tr, ti):
            top = jnp.concatenate([tr, ti], axis=1)
            low = jnp.concatenate([-ti, tr], axis=1)
            hi, lo = split(jnp.concatenate([top, low], axis=0))
            k = 4 * LANES
            dst[0:k, :] = hi
            dst[k : 2 * k, :] = hi
            dst[2 * k : 3 * k, :] = lo

        rows_band(rowf, toeplitz(kr, LANES, LANES, 0)[:OUT], toeplitz(ki, LANES, LANES, 0)[:OUT])
        rows_band(rowa, toeplitz(kr, LANES, LANES, -WIDE).T[:OUT], -toeplitz(ki, LANES, LANES, -WIDE).T[:OUT])
        cols_band(colf, toeplitz(kr, LANES, 2 * LANES, 0).T, toeplitz(ki, LANES, 2 * LANES, 0).T)
        cols_band(
            cola,
            toeplitz(kr, 2 * LANES, 2 * LANES, -WIDE)[:, :LANES],
            -toeplitz(ki, 2 * LANES, 2 * LANES, -WIDE)[:, :LANES],
        )

        cols_band(
            colb,
            toeplitz(kr, 2 * LANES, 2 * LANES, -LANES)[:, :LANES],
            -toeplitz(ki, 2 * LANES, 2 * LANES, -LANES)[:, :LANES],
        )

        def moved(ref, t, r):
            return pltpu.roll(ref[1, r, t * LANES : (t + 1) * LANES], LANES - RIM, 1)

        def phase_one(ref, r, q, rows, which):
            last = lanes_of(rows) >= LANES - RIM
            for t in which:
                s, c = sincos(jnp.where(last, moved(ref, t + 1, r), moved(ref, t, r)))
                s1[q, t * LANES : (t + 1) * LANES] = s
                c1[q, t * LANES : (t + 1) * LANES] = c

        @pl.loop(0, H // 16, unroll=H // 16)
        def _(i):
            r0 = pl.multiple_of(i * 16, 16)
            r = pl.ds(r0, 16)
            for p in range(2):
                hi, lo = split(cotv[p, r, :])
                q = pl.ds(pl.multiple_of(r0 + WIDE, 16), 16)
                xh[p, q, 0:W] = hi
                xl[p, q, 0:W] = lo
            q = pl.ds(pl.multiple_of(r0 + RIM, 16), 16)
            phase_one(phv, r, q, 16, range(tiles - 1))

        xall, zall = row_blocks(H + WIDE), row_blocks(H)
        xin = [q for q in xall if q >= WIDE and q + LANES <= WIDE + H]
        zin = [q for q in zall if q >= RIM and q + LANES <= RIM + H]
        down_pass(xh, xl, uh, ul, rowa, xin, 0, W)
        down_pass(zh, zl, vh, vl, rowf, zin, 0, W)

        for k in (0, 1, 2, 3, 4, 5):
            copies[k].wait_recv()
        for side in range(2):
            q = slice(0, WIDE) if side == 0 else slice(WIDE + H, WIDE + H + WIDE)
            for p in range(2):
                hi, lo = split(crow[side, p])
                xh[p, q, 0:W] = hi
                xl[p, q, 0:W] = lo
            q = slice(0, RIM) if side == 0 else slice(RIM + H, RIM + H + RIM)
            phase_one(prow.at[side], slice(0, RIM), q, RIM, range(tiles - 1))
            s, c = sincos(prow[side, 0])
            a, b = irow[side, 0], irow[side, 1]
            for p, w in enumerate((a * c - b * s, a * s + b * c)):
                hi, lo = split(w)
                zh[p, q, 0:W] = hi
                zl[p, q, 0:W] = lo

        def across_pass(src_h, src_l, dst, band, rows, which):
            for t in which:
                dst[t, 0:rows, :] = across(src_h, src_l, band, slice(0, rows), t, tiles)

        down_pass(xh, xl, uh, ul, rowa, [q for q in xall if q not in xin], 0, W)
        down_pass(zh, zl, vh, vl, rowf, [q for q in zall if q not in zin], 0, W)
        across_pass(uh, ul, gout, cola, H + WIDE, range(tiles - 1))
        across_pass(vh, vl, fout, colf, H, range(tiles - 1))

        estep = block(H + WIDE, 64)

        def turn_back(which):
            @pl.loop(0, (H + WIDE) // estep, unroll=(H + WIDE) // estep)
            def _(i):
                r = pl.ds(pl.multiple_of(i * estep, 16), estep)
                for t in which:
                    cols = slice(t * LANES, (t + 1) * LANES)
                    gr, gi = gout[t, r, 0:LANES], gout[t, r, LANES : 2 * LANES]
                    c, s = c1[r, cols], s1[r, cols]
                    for p, g in enumerate((gr * c + gi * s, gi * c - gr * s)):
                        gh[p, r, cols], gl[p, r, cols] = split(g)

        turn_back(range(tiles - 1))
        down_pass(gh, gl, th, tl, rowa, zall, 0, (tiles - 1) * LANES)

        for k in (6, 7, 8, 9, 10, 11):
            copies[k].wait_recv()
        edge = slice(W, full)
        for p in range(2):
            for g in range(2):
                for r0 in range(0, part2, part4):
                    r = slice(r0, r0 + part4)
                    q = slice(WIDE + g * part2 + r0, WIDE + g * part2 + r0 + part4)
                    xh[p, q, edge], xl[p, q, edge] = split(edges(cl[r, :], cr[r, :], WIDE, 2 * WIDE * g + WIDE * p))
            for m, q in enumerate((slice(0, WIDE), slice(WIDE + H, 2 * WIDE + H))):
                xh[p, q, edge], xl[p, q, edge] = split(edges(met[0, m], met[1, m], WIDE, WIDE * p))

        down_pass(xh, xl, uh, ul, rowa, xall, W, full)
        across_pass(uh, ul, gout, cola, H + WIDE, range(tiles - 1, tiles + 1))

        def phase_edge(q, a, b, src, own, own_r, rows):
            lane = lanes_of(rows)
            inner = moved(own, tiles - 1, own_r)
            x = jnp.where(lane >= LANES - RIM, pltpu.roll(b, (LANES - RIM - src) % LANES, 1), inner)
            outer = jnp.where(lane >= LANES - WIDE, pltpu.roll(a, (LANES - WIDE - src) % LANES, 1), 0.0)
            y = jnp.where(lane >= LANES - RIM, moved(own, 0, own_r), outer)
            for t, v in ((tiles - 1, x), (tiles, y)):
                s, c = sincos(v)
                s1[q, t * LANES : (t + 1) * LANES] = s
                c1[q, t * LANES : (t + 1) * LANES] = c

        for g in range(8):
            r = slice(part2, part2 + part8)
            q = slice(RIM + g * part8, RIM + (g + 1) * part8)
            phase_edge(q, cl[r, :], cr[r, :], RIM * g, phv, slice(g * part8, (g + 1) * part8), part8)
        near = (slice(RIM, WIDE), slice(0, RIM))
        rims = (slice(0, RIM), slice(RIM + H, WIDE + H))
        for m in range(2):
            phase_edge(rims[m], met[0, m, near[m]], met[1, m, near[m]], 2 * WIDE, prow.at[m], slice(0, RIM), RIM)

        turn_back(range(tiles - 1, tiles + 1))
        down_pass(gh, gl, th, tl, rowa, zall, (tiles - 1) * LANES, full)

        for k in (12, 13):
            copies[k].wait_recv()
        for p in range(2):
            for g in range(4):
                q = slice(RIM + g * part4, RIM + (g + 1) * part4)
                zh[p, q, edge], zl[p, q, edge] = split(edges(wl[...], wr[...], RIM, WIDE * g + RIM * p))
            for m in range(2):
                value = edges(met[0, m, near[m]], met[1, m, near[m]], RIM, 2 * WIDE + RIM * (p + 1))
                zh[p, rims[m], edge], zl[p, rims[m], edge] = split(value)

        down_pass(zh, zl, vh, vl, rowf, zall, W, full)
        across_pass(vh, vl, fout, colf, H, range(tiles - 1, tiles + 1))

        fstep = block(H, 32)

        @pl.loop(0, H // fstep, unroll=H // fstep)
        def _(i):
            r = pl.ds(pl.multiple_of(i * fstep, 16), fstep)
            q = pl.ds(pl.multiple_of(i * fstep + RIM, 16), fstep)
            first = lanes_of(fstep) < RIM
            before = None
            for t in [tiles] + list(range(tiles)):
                cols = slice(t * LANES, (t + 1) * LANES)
                gr, gi = gout[t, q, 0:LANES], gout[t, q, LANES : 2 * LANES]
                fr, fi = fout[t, r, 0:LANES], fout[t, r, LANES : 2 * LANES]
                c, s = c1[q, cols], s1[q, cols]
                term = pltpu.roll(gi * (fr * c - fi * s) - gr * (fr * s + fi * c), RIM, 1)
                if before is not None:
                    pgv[r, cols] = jnp.where(first, before, term)
                before = term

        for c in copies:
            c.wait_send()

    V = pltpu.VMEM
    scratch = [
        V((2, H, LANES), F32), V((2, H, LANES), F32), V((H, LANES), F32), V((H, LANES), F32),
        V((2, H, W), F32), V((2, H, W), F32), V((2, H, W), F32),
        V((H // 2 + H // 8, LANES), F32), V((H // 2 + H // 8, LANES), F32),
        V((H // 4, LANES), F32), V((H // 4, LANES), F32), V((2, 2, WIDE, LANES), F32),
        V((H // 2 + H // 8, LANES), F32), V((H // 2 + H // 8, LANES), F32),
        V((H // 4, LANES), F32), V((H // 4, LANES), F32), V((2, 2, WIDE, LANES), F32),
        V((2, 2, WIDE, W), F32), V((2, 2, RIM, W), F32), V((2, 2, RIM, W), F32),
        V(tap_shape, F32), V((8, 2 * LANES), F32),
        V((2, H + 2 * WIDE, full), BF16), V((2, H + 2 * WIDE, full), BF16),
        V((2, H + WIDE, full), BF16), V((2, H + WIDE, full), BF16),
        V((2, H + WIDE, full), BF16), V((2, H + WIDE, full), BF16),
        V((2, H + WIDE, full), BF16), V((2, H + WIDE, full), BF16),
        V((2, H, full), BF16), V((2, H, full), BF16),
        V((H + WIDE, full), F32), V((H + WIDE, full), F32),
        V((tiles + 1, H + WIDE, 2 * LANES), F32), V((tiles + 1, H, 2 * LANES), F32),
        V((2 * OUT, 6 * LANES), BF16), V((2 * OUT, 6 * LANES), BF16),
        V((12 * LANES, 2 * LANES), BF16), V((12 * LANES, 2 * LANES), BF16),
        pltpu.SemaphoreType.DMA((11,)),
        pltpu.SemaphoreType.DMA((14,)), pltpu.SemaphoreType.DMA((14,)),
    ]
    results = (
        V((2, H, full), BF16), V((2, H, full), BF16),
        V((H, W), F32), V((2, H, W), F32), V((H, W), F32), V((H, W), F32),
        V((12 * LANES, 2 * LANES), BF16),
    )
    return pl.pallas_call(
        kernel,
        out_shape=results,
        in_specs=[pl.BlockSpec(memory_space=pltpu.HBM)] * 4,
        out_specs=tuple(pl.BlockSpec(memory_space=V) for _ in results),
        scratch_shapes=scratch,
        compiler_params=pltpu.CompilerParams(
            collective_id=0, has_side_effects=True, vmem_limit_bytes=40 * 1024 * 1024
        ),
        cost_estimate=pl.CostEstimate(flops=10**10, bytes_accessed=5 * 10**6, transcendentals=0),
    )


def make_last(H, W):
    tiles = W // LANES
    step = block(H, 160)

    def kernel(th, tl, pgv, wz, c0, s0, colb, pg, pb, term, probe, store):
        copies = []

        def put(src, dst):
            c = pltpu.make_async_copy(src, dst, store.at[len(copies)])
            c.start()
            copies.append(c)

        put(pgv, pg.at[1])
        for r0 in range(0, H, step):
            r = slice(r0, r0 + step)
            for t in range(tiles):
                cols = slice(t * LANES, (t + 1) * LANES)
                g = across(th, tl, colb, r, t - 1, tiles)
                gr, gi = g[:, 0:LANES], g[:, LANES : 2 * LANES]
                c, s = c0[r, cols], s0[r, cols]
                term[r, cols] = gi * wz[0, r, cols] - gr * wz[1, r, cols]
                probe[0, r, cols] = gr * c + gi * s
                probe[1, r, cols] = gi * c - gr * s
            put(term.at[r], pg.at[0, r])
            put(probe.at[:, r], pb.at[:, r])
        for c in copies:
            c.wait()

    V = pltpu.VMEM
    out = jax.ShapeDtypeStruct((2, H, W), F32)
    return pl.pallas_call(
        kernel,
        out_shape=(out, out),
        in_specs=[pl.BlockSpec(memory_space=V)] * 7,
        out_specs=(pl.BlockSpec(memory_space=pltpu.HBM),) * 2,
        scratch_shapes=[
            V((H, W), F32), V((2, H, W), F32),
            pltpu.SemaphoreType.DMA((1 + 2 * (H // step),)),
        ],
        compiler_params=pltpu.CompilerParams(vmem_limit_bytes=32 * 1024 * 1024),
        cost_estimate=pl.CostEstimate(flops=10**10, bytes_accessed=5 * 10**6, transcendentals=0),
    )


def on_device(incident, phases, cotangent, propagator):
    H, W = incident.shape[1], incident.shape[2]
    operands = [pltpu.with_memory_space_constraint(x, pltpu.HBM) for x in (incident, phases, cotangent, propagator)]
    return make_last(H, W)(*make_kernel(H, W, propagator.shape)(*operands))


def solution(mesh):
    placed = (P(None, "ty", "tx"), P(None, "ty", "tx"), P(None, "ty", "tx"), P())
    return jax.shard_map(
        on_device,
        mesh=mesh,
        in_specs=placed,
        out_specs=(P(None, "ty", "tx"), P(None, "ty", "tx")),
        check_vma=False,
    )
```
